32 devices in a mesh: batch: 8 (over z, y), pass: 4 (over x, core).
Axes of the slice: x: 2, y: 2, z: 4, core: 2. Of those that a mesh axis runs over, the one named last changes fastest.
Arguments:
- features: bfloat16 [8192, 4, 4, 256], P(('batch', 'pass')), may hold values from -6 to 6
- labels: int32 [8192, 40], P(('batch', 'pass')), may hold values 0 or 1
- image_counts: int32 [8, 4], P('batch', 'pass'), may hold values from 1 to 256, as said below
- block_one_master: float32 [7168, 512], P(('batch', 'pass')), may hold values from -0.125 to 0.125
- block_one_momentum: float32 [7168, 512], P(('batch', 'pass')), may hold values from -0.00036621094 to 0.00036621094
- block_one_average: float32 [7168, 512], P(('batch', 'pass')), may hold values from -0.125 to 0.125
- block_two_master: float32 [9216, 512], P(('batch', 'pass')), may hold values from -0.09375 to 0.09375
- block_two_momentum: float32 [9216, 512], P(('batch', 'pass')), may hold values from -0.00036621094 to 0.00036621094
- block_two_average: float32 [9216, 512], P(('batch', 'pass')), may hold values from -0.09375 to 0.09375
- norm_params: float32 [2, 5, 512], replicated, may hold values from -0.6 to 1.5, as said below
- norm_momentum: float32 [2, 5, 512], replicated, may hold values from -0.00030517578 to 0.00030517578
- norm_average: float32 [2, 5, 512], replicated, may hold values from -0.6 to 1.5, as said below
- head_params: float32 [513, 40], replicated, may hold values from -0.25 to 0.25
- head_momentum: float32 [513, 40], replicated, may hold values from -0.0625 to 0.0625
- head_average: float32 [513, 40], replicated, may hold values from -0.25 to 0.25
Outputs:
- pooled: float32 [8192, 512], P(('batch', 'pass'))
- input_grad: float32 [8192, 4, 4, 256], P(('batch', 'pass'))
- task_losses: float32 [40], replicated
- task_weights: float32 [40], replicated
- block_one_moment: float32 [7168, 512], P(('batch', 'pass'))
- block_one_weight: float32 [7168, 512], P(('batch', 'pass'))
- block_one_mean: float32 [7168, 512], P(('batch', 'pass'))
- block_one_copy: bfloat16 [7168, 512], P(('batch', 'pass'))
- block_two_moment: float32 [9216, 512], P(('batch', 'pass'))
- block_two_weight: float32 [9216, 512], P(('batch', 'pass'))
- block_two_mean: float32 [9216, 512], P(('batch', 'pass'))
- block_two_copy: bfloat16 [9216, 512], P(('batch', 'pass'))
- norm_moment: float32 [2, 5, 512], replicated
- norm_weight: float32 [2, 5, 512], replicated
- norm_mean: float32 [2, 5, 512], replicated
- head_moment: float32 [513, 40], replicated
- head_weight: float32 [513, 40], replicated
- head_mean: float32 [513, 40], replicated
The draws below stay inside these ranges and needn't reach their ends.
Inputs may be any that keep to these rules, and one draw needn't show every extreme that they name: image_counts[b, p] is the number of valid images among the 256 slots of device (b, p); they are its first slots, the rest are padding. Some device has all 256 slots valid. norm_params[0] holds gains, norm_params[1] shifts. norm_average[0] holds gains, norm_average[1] shifts.
All inputs are finite; a program needn't handle non-finite values. No bound on the sum of `labels` on one device may be relied on, other than what follows from the above.
Results may differ from the reference program's by a relative error of at most 0.012.
Values may be sent and summed in bfloat16 or wider, within the bound.
No kernel may reach another device: no remote copies, remote signals or barrier semaphores. Data moves between devices by JAX's collectives and lax.ppermute only.
A program may use at most 320 MiB of HBM per device.

```python
import math
import jax
import jax.numpy as jnp
from jax import lax

CIN = 256
COUT = 512
TASKS = 40
FW_STEPS = 20
CAP = 256
IMAGES = 8192
ROWS_ONE = 7168
ROWS_TWO = 9216
N_BATCH = 8
N_PASS = 4


def draw_image_counts(key, part):
    key = jax.random.fold_in(key, 11)
    batch_index = jnp.arange(N_BATCH, dtype=jnp.int32)[:, None]
    pass_index = jnp.arange(N_PASS, dtype=jnp.int32)[None, :]
    span = 2 * (N_BATCH - 1) * (N_PASS - 1)
    rising = batch_index * (N_PASS - 1) + pass_index * (N_BATCH - 1)
    base_count = 1 + (CAP - 1) * (span + 2 * rising) // (3 * span)
    jitter = jax.random.randint(key, (N_BATCH, N_PASS), 0, CAP // 4 + 1, dtype=jnp.int32)
    counts = jnp.maximum(base_count - jitter, 1)
    last_one = (batch_index == N_BATCH - 1) & (pass_index == N_PASS - 1)
    return jnp.where(last_one, CAP, counts).astype(jnp.int32)


def draw_norm_params(key, part):
    key = jax.random.fold_in(key, 5)
    gain_key, shift_key = jax.random.split(key)
    scale_factors = jnp.clip(1.0 + 0.15 * jax.random.normal(gain_key, (1, 5, COUT), jnp.float32), 0.5, 1.5)
    shifts = jnp.clip(0.2 * jax.random.normal(shift_key, (1, 5, COUT), jnp.float32), -0.6, 0.6)
    return jnp.concatenate([scale_factors, shifts], axis=0)


def draw_norm_average(key, part):
    key = jax.random.fold_in(key, 6)
    gain_key, shift_key = jax.random.split(key)
    scale_factors = jnp.clip(1.0 + 0.15 * jax.random.normal(gain_key, (1, 5, COUT), jnp.float32), 0.5, 1.5)
    shifts = jnp.clip(0.2 * jax.random.normal(shift_key, (1, 5, COUT), jnp.float32), -0.6, 0.6)
    return jnp.concatenate([scale_factors, shifts], axis=0)


def touch_ends(entries, key, low, high):
    extent = entries.shape
    place = [jax.random.randint(jax.random.fold_in(key, axis), (), 0, extent[axis]) for axis in range(len(extent))]
    entries = entries.at[tuple(place)].set(low)
    longest = extent.index(max(extent))
    place[longest] = (place[longest] + 1) % extent[longest]
    return entries.at[tuple(place)].set(high)


def block_scale(stream_key, shape, cuts, least, high):
    gain, own = 1.0, jax.random.fold_in(stream_key, 6)
    for position, parts in cuts:
        draws = jnp.exp(jax.random.uniform(jax.random.fold_in(own, position), (parts,), jnp.float32, least / len(cuts), high / len(cuts)))
        gain = gain * jnp.repeat(draws, shape[position] // parts).reshape([-1 if axis == position else 1 for axis in range(len(shape))])
    return gain


def centred(key, extent, scale, limit, cuts=(), kind=jnp.bfloat16):
    gain = block_scale(key, extent, cuts, -0.22, 0.18) if cuts else 1.0
    array = jax.random.normal(key, extent, jnp.float32) * scale * gain
    return jnp.minimum(jnp.maximum(array, -limit), limit).astype(kind)


def setup_inputs(seed: int = 0) -> dict:
    key_of = jax.random.split(jax.random.key(seed), 16)
    features = centred(key_of[0], (IMAGES, 4, 4, CIN), 1.0, 6.0, ((0, 32),))
    labels = touch_ends((jax.random.randint(key_of[1], (IMAGES, TASKS), 0, 5) < 2).astype(jnp.int32), jax.random.fold_in(key_of[1], 1), 0, 1)
    image_counts = draw_image_counts(jax.random.fold_in(key_of[15], 71), 0)
    block_one_master = centred(key_of[3], (ROWS_ONE, COUT), (9 * CIN) ** -0.5, 0.125, ((0, 32),), jnp.float32)
    block_one_momentum = centred(key_of[4], (ROWS_ONE, COUT), (0.0024 * (CAP * N_BATCH * N_PASS) ** -0.5), 0.00036621094, ((0, 32),), jnp.float32)
    block_one_average = centred(key_of[5], (ROWS_ONE, COUT), (9 * CIN) ** -0.5, 0.125, ((0, 32),), jnp.float32)
    block_two_master = centred(key_of[6], (ROWS_TWO, COUT), (9 * COUT) ** -0.5, 0.09375, ((0, 32),), jnp.float32)
    block_two_momentum = centred(key_of[7], (ROWS_TWO, COUT), (0.0024 * (CAP * N_BATCH * N_PASS) ** -0.5), 0.00036621094, ((0, 32),), jnp.float32)
    block_two_average = centred(key_of[8], (ROWS_TWO, COUT), (9 * COUT) ** -0.5, 0.09375, ((0, 32),), jnp.float32)
    norm_params = draw_norm_params(jax.random.fold_in(key_of[15], 71), 0)
    norm_momentum = centred(key_of[10], (2, 5, COUT), (0.0018 * (CAP * N_BATCH * N_PASS) ** -0.5), 0.00030517578, (), jnp.float32)
    norm_average = draw_norm_average(jax.random.fold_in(key_of[15], 71), 0)
    head_params = centred(key_of[12], (COUT + 1, TASKS), COUT ** -0.5, 0.25, (), jnp.float32)
    head_momentum = centred(key_of[13], (COUT + 1, TASKS), (0.37 * (CAP * N_BATCH * N_PASS) ** -0.5), 0.0625, (), jnp.float32)
    head_average = centred(key_of[14], (COUT + 1, TASKS), COUT ** -0.5, 0.25, (), jnp.float32)
    return {"features": features, "labels": labels, "image_counts": image_counts, "block_one_master": block_one_master, "block_one_momentum": block_one_momentum, "block_one_average": block_one_average, "block_two_master": block_two_master, "block_two_momentum": block_two_momentum, "block_two_average": block_two_average, "norm_params": norm_params, "norm_momentum": norm_momentum, "norm_average": norm_average, "head_params": head_params, "head_momentum": head_momentum, "head_average": head_average}


epsilon = 1e-05
softness = 0.01
momentum_decay = 0.9
average_decay = 0.9
rate_conv = 3.0
rate_norm = 50.0
rate_head = 0.05
highest = lax.Precision.HIGHEST

@jax.custom_vjp
def low(v):
    return lax.optimization_barrier(v.astype(jnp.bfloat16)).astype(jnp.float32)

@jax.custom_vjp
def low_back(v):
    return v

def low_keep(v):
    return (low(v), None)

def low_pass(kept, grad):
    return (grad,)

def back_keep(v):
    return (v, None)

def back_low(kept, grad):
    return (low(grad),)
low.defvjp(low_keep, low_pass)
low_back.defvjp(back_keep, back_low)

def silu_value(v):
    return v * jax.nn.sigmoid(v)

def patches(image, stride):
    amount, height, width_in, channels = image.shape
    side = height // stride
    padded = jnp.pad(image, ((0, 0), (1, 1), (1, 1), (0, 0)))
    reach = stride * (side - 1) + 1
    pieces = [padded[:, row_off:row_off + reach:stride, col_off:col_off + reach:stride, :] for row_off in range(3) for col_off in range(3)]
    return jnp.concatenate(pieces, axis=3).reshape(amount * side * side, 9 * channels)

def conv_blocks(image, weight, stride):
    amount = image.shape[0]
    blocks = image.reshape((amount // CAP, CAP) + image.shape[1:])

    def one_block(block):
        return jnp.dot(patches(block, stride), weight, precision=highest)
    result = lax.map(jax.checkpoint(one_block), blocks)
    return result.reshape(amount * 4, weight.shape[1])

def batch_norm(values, mask_rows, slot_positions, scale, offset):
    centre = lax.optimization_barrier(jnp.sum(values * mask_rows, axis=0)) / slot_positions
    centered = values - centre
    spread = lax.optimization_barrier(jnp.sum(mask_rows * centered * centered, axis=0)) / slot_positions
    return scale * centered * lax.rsqrt(spread + epsilon) + offset

def encoder(image, block_one, block_two, norms, mask_rows, slot_positions):
    amount = image.shape[0]
    row_total = amount * 4
    x_low = low(image)
    one_low = low(block_one)
    two_low = low(block_two)
    w_first = one_low[:9 * CIN]
    w_short = one_low[9 * CIN:10 * CIN]
    w_second = one_low[10 * CIN:]
    w_third = two_low[:9 * COUT]
    w_fourth = two_low[9 * COUT:]
    scale_factors = norms[0]
    start_offsets = norms[1]
    conv_output_first = low_back(conv_blocks(x_low, w_first, 2))
    short_in = x_low[:, ::2, ::2, :].reshape(row_total, CIN)
    conv_output_shortcut = low_back(jnp.dot(short_in, w_short, precision=highest))
    a_first = low(silu_value(batch_norm(conv_output_first, mask_rows, slot_positions, scale_factors[0], start_offsets[0])))
    conv_output_second = low_back(conv_blocks(a_first.reshape(amount, 2, 2, COUT), w_second, 1))
    hidden_first = silu_value(batch_norm(conv_output_second, mask_rows, slot_positions, scale_factors[1], start_offsets[1]) + batch_norm(conv_output_shortcut, mask_rows, slot_positions, scale_factors[2], start_offsets[2]))
    h_low = low(hidden_first)
    conv_output_third = low_back(conv_blocks(h_low.reshape(amount, 2, 2, COUT), w_third, 1))
    a_third = low(silu_value(batch_norm(conv_output_third, mask_rows, slot_positions, scale_factors[3], start_offsets[3])))
    conv_output_fourth = low_back(conv_blocks(a_third.reshape(amount, 2, 2, COUT), w_fourth, 1))
    h_two = silu_value(batch_norm(conv_output_fourth, mask_rows, slot_positions, scale_factors[4], start_offsets[4]) + hidden_first)
    return lax.optimization_barrier(jnp.mean(h_two.reshape(amount, 4, COUT), axis=1))

def task_heads(pooled, head):
    return jnp.dot(pooled, head[:COUT], precision=highest) + head[COUT]

def frank_wolfe(gram):
    scaled = gram / (jnp.mean(jnp.diagonal(gram)) + 1e-06)
    weights = jnp.full((TASKS,), 1.0 / TASKS, jnp.float32)
    for turn in range(FW_STEPS):
        activation_slope = jnp.dot(scaled, weights, precision=highest)
        target_labels = jax.nn.softmax(-activation_slope / softness)
        gamma = 2.0 / (turn + 3.0)
        weights = (1.0 - gamma) * weights + gamma * target_labels
    return weights

def nesterov(grad, master, momentum, average, rate):
    moment = momentum_decay * momentum + grad
    fresh = master - rate * (grad + momentum_decay * moment)
    return (moment, fresh, average_decay * average + (1.0 - average_decay) * fresh)

def reference(features, labels, image_counts, block_one_master, block_one_momentum, block_one_average, block_two_master, block_two_momentum, block_two_average, norm_params, norm_momentum, norm_average, head_params, head_momentum, head_average):
    counts_flat = image_counts.reshape(-1)
    valid = (jnp.arange(CAP)[None, :] < counts_flat[:, None]).astype(jnp.float32).reshape(IMAGES)
    total = jnp.sum(counts_flat).astype(jnp.float32)
    mask_rows = jnp.repeat(valid, 4)[:, None]
    slot_positions = 4.0 * total
    image = features.astype(jnp.float32)

    def forward(image_in, block_one, block_two, norms):
        return encoder(image_in, block_one, block_two, norms, mask_rows, slot_positions)
    pooled, encoder_back = jax.vjp(forward, image, block_one_master, block_two_master, norm_params)
    logits, head_back = jax.vjp(task_heads, pooled, head_params)
    target_labels = labels.astype(jnp.float32)
    resid = (jax.nn.sigmoid(logits) - target_labels) * valid[:, None]
    task_losses = lax.optimization_barrier(jnp.sum(valid[:, None] * (jax.nn.softplus(logits) - target_labels * logits), axis=0)) / total
    weight_rows = head_params[:COUT]
    gram = jnp.dot(resid.T, resid, precision=highest) * jnp.dot(weight_rows.T, weight_rows, precision=highest) / total
    task_weights = frank_wolfe(gram)
    head_grad = head_back(resid / total)[1]
    pooled_grad = head_back(resid * task_weights / total)[0]
    input_grad, block_one_grad, block_two_grad, norm_grad = encoder_back(pooled_grad)
    scale_rate = math.sqrt(IMAGES)
    one_m, one_w, one_a = nesterov(block_one_grad, block_one_master, block_one_momentum, block_one_average, rate_conv * scale_rate)
    two_m, two_w, two_a = nesterov(block_two_grad, block_two_master, block_two_momentum, block_two_average, rate_conv * scale_rate)
    norm_m, norm_w, norm_a = nesterov(norm_grad, norm_params, norm_momentum, norm_average, rate_norm * scale_rate)
    head_m, head_w, head_a = nesterov(head_grad, head_params, head_momentum, head_average, rate_head * scale_rate)
    return (pooled, input_grad, task_losses, task_weights, one_m, one_w, one_a, one_w.astype(jnp.bfloat16), two_m, two_w, two_a, two_w.astype(jnp.bfloat16), norm_m, norm_w, norm_a, head_m, head_w, head_a)
```

```python
import math

import jax
import jax.numpy as jnp
from jax import lax
from jax.experimental import pallas as pl
from jax.experimental.pallas import tpu as pltpu
from jax.sharding import PartitionSpec as P

CIN = 256
COUT = 512
TASKS = 40
FW_STEPS = 20
CAP = 256
WIDE = 4 * COUT
LANES = 128
AXES = ("batch", "pass")

epsilon = 1e-05
softness = 0.01
momentum_decay = 0.9
average_decay = 0.9
rate_conv = 3.0
rate_norm = 50.0
rate_head = 0.05
highest = lax.Precision.HIGHEST

HBM = pl.BlockSpec(memory_space=pltpu.HBM)
VMEM = pl.BlockSpec(memory_space=pltpu.VMEM)
SMEM = pl.BlockSpec(memory_space=pltpu.SMEM)
f32 = jnp.float32
bf16 = jnp.bfloat16


def shape(extent, kind):
    return jax.ShapeDtypeStruct(extent, kind)


def run(body, args, in_specs, outs, out_specs, scratch, flops=0, moved=0, aliases=None, name=None):
    return pl.pallas_call(
        body,
        out_shape=outs,
        in_specs=in_specs,
        out_specs=out_specs,
        scratch_shapes=scratch,
        input_output_aliases=aliases or {},
        compiler_params=pltpu.CompilerParams(vmem_limit_bytes=60 * 1024 * 1024),
        cost_estimate=pl.CostEstimate(flops=flops, bytes_accessed=moved, transcendentals=0),
        name=name,
    )(*args)


class Mover:
    def __init__(self, sems):
        self.sems = sems
        self.used = 0
        self.out = []

    def load(self, src, dst):
        copy = pltpu.make_async_copy(src, dst, self.sems.at[self.used])
        self.used += 1
        copy.start()
        return copy

    def store(self, src, dst):
        self.out.append(self.load(src, dst))

    def finish(self):
        for copy in self.out:
            copy.wait()


def columns(o):
    return pl.ds(o * COUT, COUT)


def split_turn(at, tb, value, place, channels):
    half = channels // 2
    tb[pl.ds(0, channels), :] = value.T
    for group in range(half // 16):
        for parity in range(2):
            at[parity, pl.ds(place * half + 16 * group, 16), :] = tb[
                pl.ds(32 * group + 16 * parity, 16), :
            ]


def hand_out(move, at, side_ref, mine_ref, theirs_ref):
    side = side_ref[0, 0]
    move.store(at.at[side], mine_ref)
    move.store(at.at[1 - side], theirs_ref)


def dot(left, right, precision=None):
    return jnp.dot(left, right, preferred_element_type=f32, precision=precision)


def dot_nt(left, right):
    return lax.dot_general(left, right, (((1,), (1,)), ((), ())), preferred_element_type=f32)


def dot_tn(left, right, precision=None):
    return lax.dot_general(
        left, right, (((0,), (0,)), ((), ())), preferred_element_type=f32, precision=precision
    )


def sigmoid(v):
    return 0.5 * jnp.tanh(0.5 * v) + 0.5


def channel_row(packed, k):
    return jnp.concatenate([packed[4 * k + b : 4 * k + b + 1, :] for b in range(4)], axis=1)


def pack(rows):
    pieces = [row[:, b * LANES : (b + 1) * LANES] for row in rows for b in range(4)]
    while len(pieces) % 8:
        pieces.append(jnp.zeros((1, LANES), f32))
    return jnp.concatenate(pieces, axis=0)


def spread(out_ref, packed):
    out_ref[...] = jnp.broadcast_to(packed[None], out_ref.shape)


def mask_of(count_ref):
    rows = lax.broadcasted_iota(jnp.int32, (CAP, COUT), 0)
    return (rows < count_ref[0, 0]).astype(f32)


def column_sum(v):
    return jnp.sum(v, axis=0, keepdims=True)


def moments(total_sum, total_square, positions):
    centre = total_sum / positions
    spread_value = total_square / positions - centre * centre
    return centre, lax.rsqrt(spread_value + epsilon)


def forward_taps(act_ref, w_ref, o):
    row_out, col_out = divmod(o, 2)
    total = None
    for row_in in range(2):
        tap = (row_in - row_out + 1) * 3 + (1 - col_out)
        part = dot(
            act_ref[:, pl.ds(row_in * 2 * COUT, 2 * COUT)], w_ref[pl.ds(tap * COUT, 2 * COUT), :]
        )
        total = part if total is None else total + part
    return total


def tap_of(i, o):
    return (i // 2 - o // 2 + 1) * 3 + (i % 2 - o % 2 + 1)


def backward_taps(dy_ref, w_ref, i):
    total = None
    for o in range(4):
        part = dot_nt(dy_ref[:, columns(o)], w_ref[pl.ds(tap_of(i, o) * COUT, COUT), :])
        total = part if total is None else total + part
    return total


def first_pairs(o):
    row_out, col_out = divmod(o, 2)
    runs = []
    for row_tap in range(3):
        row_in = 2 * row_out + row_tap - 1
        if 0 <= row_in < 4:
            col_tap = 1 if col_out == 0 else 0
            runs.append((row_in * 4 + 2 * col_out + col_tap - 1, row_tap * 3 + col_tap, 3 - col_tap))
    return runs


def k_first(x_ref, one_ref, count_ref, y1_ref, ys_ref, st_ref, local_ref, xb, wb, yb, sems):
    move = Mover(sems)
    lx = move.load(x_ref, xb)
    lw = move.load(one_ref.at[pl.ds(0, 10 * CIN)], wb)
    mask = mask_of(count_ref)
    lx.wait()
    lw.wait()
    sums = [0.0, 0.0, 0.0, 0.0]
    for o in range(4):
        total = None
        for cell, tap, cells in first_pairs(o):
            part = dot(xb[:, pl.ds(cell * CIN, cells * CIN)], wb[pl.ds(tap * CIN, cells * CIN), :])
            total = part if total is None else total + part
        yb[0, :, columns(o)] = total
        move.store(yb.at[0, :, columns(o)], y1_ref.at[:, columns(o)])
        valid = total * mask
        sums[0] += column_sum(valid)
        sums[1] += column_sum(valid * total)
        cell = (o // 2) * 8 + (o % 2) * 2
        total = dot(xb[:, pl.ds(cell * CIN, CIN)], wb[pl.ds(9 * CIN, CIN), :])
        yb[1, :, columns(o)] = total
        move.store(yb.at[1, :, columns(o)], ys_ref.at[:, columns(o)])
        valid = total * mask
        sums[2] += column_sum(valid)
        sums[3] += column_sum(valid * total)
    counted = jnp.full((8, LANES), count_ref[0, 0].astype(f32), f32)
    spread(st_ref, jnp.concatenate([pack(sums[:2]), counted], axis=0))
    local_ref[...] = pack(sums[2:])
    move.finish()


def k_second(
    y1_ref, recv_ref, norm_ref, local_ref, one_ref, count_ref, side_ref,
    mine_ref, theirs_ref, y2_ref, st_ref, keep_ref,
    yin, ab, at, tb, wb, yb, sems,
):
    move = Mover(sems)
    ly = [move.load(y1_ref.at[:, columns(o)], yin.at[:, columns(o)]) for o in range(4)]
    lw = move.load(one_ref.at[pl.ds(10 * CIN, 9 * COUT)], wb)
    got = jnp.sum(recv_ref[...], axis=0)
    total = got[8:9, 0:1]
    positions = 4.0 * total
    centre, inverse = moments(channel_row(got, 0), channel_row(got, 1), positions)
    keep_ref[...] = jnp.concatenate(
        [centre, inverse, jnp.broadcast_to(positions, (1, COUT)), jnp.zeros((5, COUT), f32)], axis=0
    )
    scale = norm_ref[0, 0:1, :] * inverse
    offset = norm_ref[1, 0:1, :] - centre * scale
    mask = mask_of(count_ref)
    for o in range(4):
        ly[o].wait()
        v = yin[:, columns(o)] * scale + offset
        ab[:, columns(o)] = (v * sigmoid(v)).astype(bf16)
        split_turn(at, tb, ab[:, columns(o)], o, COUT)
    hand_out(move, at, side_ref, mine_ref, theirs_ref)
    lw.wait()
    sums = [0.0, 0.0]
    for o in range(4):
        y = forward_taps(ab, wb, o)
        yb[:, columns(o)] = y
        move.store(yb.at[:, columns(o)], y2_ref.at[:, columns(o)])
        valid = y * mask
        sums[0] += column_sum(valid)
        sums[1] += column_sum(valid * y)
    spread(st_ref, jnp.concatenate([pack(sums), local_ref[...]], axis=0))
    move.finish()


def k_third(
    y2_ref, ys_ref, recv_ref, norm_ref, base_ref, two_ref, count_ref, side_ref,
    h1_ref, mine_ref, theirs_ref, y3_ref, st_ref, keep_ref,
    yin, sin, hout, ab, at, tb, wb, yb, sems,
):
    move = Mover(sems)
    ly, ls = [], []
    for o in range(4):
        ly.append(move.load(y2_ref.at[:, columns(o)], yin.at[:, columns(o)]))
        ls.append(move.load(ys_ref.at[:, columns(o)], sin.at[:, columns(o)]))
    lw = move.load(two_ref.at[pl.ds(0, 9 * COUT)], wb)
    got = jnp.sum(recv_ref[...], axis=0)
    positions = base_ref[2:3, :]
    c1, i1 = moments(channel_row(got, 0), channel_row(got, 1), positions)
    c2, i2 = moments(channel_row(got, 2), channel_row(got, 3), positions)
    keep_ref[...] = jnp.concatenate([c1, i1, c2, i2, jnp.zeros((4, COUT), f32)], axis=0)
    s1 = norm_ref[0, 1:2, :] * i1
    s2 = norm_ref[0, 2:3, :] * i2
    offset = norm_ref[1, 1:2, :] - c1 * s1 + (norm_ref[1, 2:3, :] - c2 * s2)
    mask = mask_of(count_ref)
    for o in range(4):
        ly[o].wait()
        ls[o].wait()
        v = yin[:, columns(o)] * s1 + sin[:, columns(o)] * s2 + offset
        h = v * sigmoid(v)
        hout[:, columns(o)] = h
        ab[:, columns(o)] = h.astype(bf16)
        move.store(hout.at[:, columns(o)], h1_ref.at[:, columns(o)])
        split_turn(at, tb, ab[:, columns(o)], o, COUT)
    hand_out(move, at, side_ref, mine_ref, theirs_ref)
    lw.wait()
    sums = [0.0, 0.0]
    for o in range(4):
        y = forward_taps(ab, wb, o)
        yb[:, columns(o)] = y
        move.store(yb.at[:, columns(o)], y3_ref.at[:, columns(o)])
        valid = y * mask
        sums[0] += column_sum(valid)
        sums[1] += column_sum(valid * y)
    spread(st_ref, pack(sums))
    move.finish()


def k_fourth(
    y3_ref, recv_ref, norm_ref, base_ref, two_ref, count_ref, side_ref,
    mine_ref, theirs_ref, y4_ref, st_ref, keep_ref,
    yin, ab, at, tb, wb, yb, sems,
):
    move = Mover(sems)
    ly = [move.load(y3_ref.at[:, columns(o)], yin.at[:, columns(o)]) for o in range(4)]
    lw = move.load(two_ref.at[pl.ds(9 * COUT, 9 * COUT)], wb)
    got = jnp.sum(recv_ref[...], axis=0)
    centre, inverse = moments(channel_row(got, 0), channel_row(got, 1), base_ref[2:3, :])
    keep_ref[...] = jnp.concatenate([centre, inverse, jnp.zeros((6, COUT), f32)], axis=0)
    scale = norm_ref[0, 3:4, :] * inverse
    offset = norm_ref[1, 3:4, :] - centre * scale
    mask = mask_of(count_ref)
    for o in range(4):
        ly[o].wait()
        v = yin[:, columns(o)] * scale + offset
        ab[:, columns(o)] = (v * sigmoid(v)).astype(bf16)
        split_turn(at, tb, ab[:, columns(o)], o, COUT)
    hand_out(move, at, side_ref, mine_ref, theirs_ref)
    lw.wait()
    sums = [0.0, 0.0]
    for o in range(4):
        y = forward_taps(ab, wb, o)
        yb[:, columns(o)] = y
        move.store(yb.at[:, columns(o)], y4_ref.at[:, columns(o)])
        valid = y * mask
        sums[0] += column_sum(valid)
        sums[1] += column_sum(valid * y)
    spread(st_ref, pack(sums))
    move.finish()


def k_heads(
    y4_ref, h1_ref, recv_ref, norm_ref, base_ref, head_ref, bias_ref, labels_ref, count_ref,
    pooled_ref, resid_ref, slope_ref, gram_ref, part_ref, keep_ref,
    yin, hin, sb, sems,
):
    move = Mover(sems)
    ly, lh = [], []
    for o in range(4):
        ly.append(move.load(y4_ref.at[:, columns(o)], yin.at[:, columns(o)]))
        lh.append(move.load(h1_ref.at[:, columns(o)], hin.at[:, columns(o)]))
    got = jnp.sum(recv_ref[...], axis=0)
    centre, inverse = moments(channel_row(got, 0), channel_row(got, 1), base_ref[2:3, :])
    keep_ref[...] = jnp.concatenate([centre, inverse, jnp.zeros((6, COUT), f32)], axis=0)
    scale = norm_ref[0, 4:5, :] * inverse
    offset = norm_ref[1, 4:5, :] - centre * scale
    total = None
    for o in range(4):
        ly[o].wait()
        lh[o].wait()
        v = yin[:, columns(o)] * scale + offset + hin[:, columns(o)]
        s = sigmoid(v)
        h = v * s
        sb[:, columns(o)] = s * (1.0 + v - h)
        move.store(sb.at[:, columns(o)], slope_ref.at[:, columns(o)])
        total = h if total is None else total + h
    pooled = total * 0.25
    pooled_ref[...] = pooled
    logits = dot(pooled, head_ref[...], highest) + bias_ref[...]
    labels = labels_ref[...]
    valid = (lax.broadcasted_iota(jnp.int32, (CAP, LANES), 0) < count_ref[0, 0]).astype(f32)
    resid = (sigmoid(logits) - labels) * valid
    resid_ref[...] = resid
    softplus = jnp.maximum(logits, 0.0) + jnp.log1p(jnp.exp(-jnp.abs(logits)))
    losses = valid * (softplus - labels * logits)
    gram = dot_tn(resid, resid, highest)
    lane = lax.broadcasted_iota(jnp.int32, (16, LANES), 1)
    packed = jnp.where(lane < TASKS, gram[0:16], jnp.where(lane < 2 * TASKS, gram[16:32], gram[32:48]))
    spread(gram_ref, packed)
    part_ref[...] = jnp.zeros(part_ref.shape, f32)
    for b in range(4):
        part_ref[pl.ds(b * TASKS, TASKS), :] = dot_tn(
            resid, pooled[:, b * LANES : (b + 1) * LANES], highest
        )[0:TASKS]
    ones = jnp.ones((CAP, LANES), f32)
    lane = lax.broadcasted_iota(jnp.int32, (TASKS, LANES), 1)
    part_ref[pl.ds(4 * TASKS, TASKS), :] = jnp.where(
        lane == 0, dot_tn(resid, ones, highest)[0:TASKS], dot_tn(losses, ones, highest)[0:TASKS]
    )
    move.finish()


def k_weights(
    recv_ref, square_ref, resid_ref, turned_ref, base_ref, keep_ref, part_ref, y4_ref, slope_ref, count_ref,
    weights_ref, u2_ref, st_ref,
    yin, sin, ub, sems,
):
    move = Mover(sems)
    ly, ls = [], []
    for o in range(4):
        ly.append(move.load(y4_ref.at[:, columns(o)], yin.at[:, columns(o)]))
        ls.append(move.load(slope_ref.at[:, columns(o)], sin.at[:, columns(o)]))
    total = base_ref[2:3, 0:1] * 0.25
    got = jnp.sum(recv_ref[...], axis=0)
    gram = jnp.concatenate(
        [
            got,
            pltpu.roll(got, LANES - TASKS, 1),
            pltpu.roll(got, LANES - 2 * TASKS, 1)[0:8],
        ],
        axis=0,
    )
    row_at = lax.broadcasted_iota(jnp.int32, (TASKS, LANES), 0)
    lane_at = lax.broadcasted_iota(jnp.int32, (TASKS, LANES), 1)
    gram = jnp.where(lane_at < TASKS, gram * square_ref[...], 0.0) / total
    trace = jnp.sum(
        jnp.sum(jnp.where(row_at == lane_at, gram, 0.0), axis=0, keepdims=True), axis=1, keepdims=True
    )
    scaled = gram / (trace / TASKS + 1e-06)
    live = lax.broadcasted_iota(jnp.int32, (1, LANES), 1) < TASKS
    weights = jnp.where(live, 1.0 / TASKS, 0.0)
    row = jnp.sum(scaled, axis=0, keepdims=True) / TASKS
    col = jnp.sum(scaled, axis=1, keepdims=True) / TASKS
    for turn in range(FW_STEPS):
        gamma = 2.0 / (turn + 3.0)
        low = jnp.min(col, axis=0, keepdims=True)
        grown_col = jnp.exp((low - col) / softness)
        grown_row = jnp.where(live, jnp.exp(jnp.where(live, (low - row) / softness, 0.0)), 0.0)
        share = gamma / jnp.sum(grown_col, axis=0, keepdims=True)
        weights = (1.0 - gamma) * weights + share * grown_row
        if turn + 1 < FW_STEPS:
            next_row = jnp.sum(scaled * grown_col, axis=0, keepdims=True)
            next_col = jnp.sum(scaled * grown_row, axis=1, keepdims=True)
            row = (1.0 - gamma) * row + share * next_row
            col = (1.0 - gamma) * col + share * next_col
    weights_ref[...] = jnp.broadcast_to(weights, (8, LANES))
    pooled_grad = dot(resid_ref[...] * (weights / total), turned_ref[...], highest) * 0.25
    centre, inverse = keep_ref[0:1, :], keep_ref[1:2, :]
    mask = mask_of(count_ref)
    sums = [0.0, 0.0]
    for o in range(4):
        ly[o].wait()
        ls[o].wait()
        u = pooled_grad * sin[:, columns(o)]
        ub[:, columns(o)] = u
        move.store(ub.at[:, columns(o)], u2_ref.at[:, columns(o)])
        valid = u * mask
        sums[0] += column_sum(valid * ((yin[:, columns(o)] - centre) * inverse))
        sums[1] += column_sum(valid)
    st_ref[:, 0:8, :] = jnp.broadcast_to(pack(sums)[None], part_ref.shape)
    st_ref[:, 8:16, :] = part_ref[...]
    move.finish()


def reverse_norm(g, y, mask, centre, inverse, gain, scale_total, shift_total, positions):
    xhat = (y - centre) * inverse
    return (gain * inverse) * (g - mask * ((shift_total + xhat * scale_total) / positions))


def k_back_fourth(
    u2_ref, y4_ref, recv_ref, norm_ref, base_ref, keep4_ref, two_ref, y3_ref, keep3_ref, count_ref,
    dy_ref, u3_ref, st_ref, tot_ref,
    uin, yin, zin, db, wb, ub, sems,
):
    move = Mover(sems)
    lu, ly = [], []
    for o in range(4):
        lu.append(move.load(u2_ref.at[:, columns(o)], uin.at[:, columns(o)]))
        ly.append(move.load(y4_ref.at[:, columns(o)], yin.at[:, columns(o)]))
    lw = move.load(two_ref.at[pl.ds(9 * COUT, 9 * COUT)], wb)
    lz = move.load(y3_ref, zin)
    got = jnp.sum(recv_ref[...], axis=0)
    tot_ref[...] = got[0:8]
    positions = base_ref[2:3, :]
    mask = mask_of(count_ref)
    scale_total, shift_total = channel_row(got, 0), channel_row(got, 1)
    for o in range(4):
        lu[o].wait()
        ly[o].wait()
        dy = reverse_norm(
            uin[:, columns(o)], yin[:, columns(o)], mask, keep4_ref[0:1, :], keep4_ref[1:2, :],
            norm_ref[0, 4:5, :], scale_total, shift_total, positions,
        )
        db[:, columns(o)] = dy.astype(bf16)
        move.store(db.at[:, columns(o)], dy_ref.at[:, columns(o)])
    lw.wait()
    lz.wait()
    centre, inverse = keep3_ref[0:1, :], keep3_ref[1:2, :]
    gain, shift = norm_ref[0, 3:4, :], norm_ref[1, 3:4, :]
    sums = [0.0, 0.0]
    for i in range(4):
        grad = backward_taps(db, wb, i)
        xhat = (zin[:, columns(i)] - centre) * inverse
        v = xhat * gain + shift
        s = sigmoid(v)
        u = grad * (s * (1.0 + v * (1.0 - s)))
        ub[:, columns(i)] = u
        move.store(ub.at[:, columns(i)], u3_ref.at[:, columns(i)])
        valid = u * mask
        sums[0] += column_sum(valid * xhat)
        sums[1] += column_sum(valid)
    spread(st_ref, jnp.concatenate([pack(sums), got[8:16]], axis=0))
    move.finish()


def k_back_third(
    u3_ref, y3_ref, recv_ref, norm_ref, base_ref, keep3_ref, two_ref, u2_ref, y2_ref, ys_ref, keep12_ref, count_ref,
    dy_ref, u1_ref, st_ref, tot_ref, head_ref,
    uin, yin, u2in, y2in, ysin, db, wb, ub, sems,
):
    move = Mover(sems)
    lu, ly = [], []
    for o in range(4):
        lu.append(move.load(u3_ref.at[:, columns(o)], uin.at[:, columns(o)]))
        ly.append(move.load(y3_ref.at[:, columns(o)], yin.at[:, columns(o)]))
    lw = move.load(two_ref.at[pl.ds(0, 9 * COUT)], wb)
    later = [move.load(u2_ref, u2in), move.load(y2_ref, y2in), move.load(ys_ref, ysin)]
    got = jnp.sum(recv_ref[:, 0:8, :], axis=0)
    tot_ref[...] = got
    head_ref[...] = recv_ref[:, 8:16, :]
    positions = base_ref[2:3, :]
    mask = mask_of(count_ref)
    scale_total, shift_total = channel_row(got, 0), channel_row(got, 1)
    for o in range(4):
        lu[o].wait()
        ly[o].wait()
        dy = reverse_norm(
            uin[:, columns(o)], yin[:, columns(o)], mask, keep3_ref[0:1, :], keep3_ref[1:2, :],
            norm_ref[0, 3:4, :], scale_total, shift_total, positions,
        )
        db[:, columns(o)] = dy.astype(bf16)
        move.store(db.at[:, columns(o)], dy_ref.at[:, columns(o)])
    lw.wait()
    for copy in later:
        copy.wait()
    c1, i1, c2, i2 = (keep12_ref[k : k + 1, :] for k in range(4))
    g1, g2 = norm_ref[0, 1:2, :], norm_ref[0, 2:3, :]
    shift = norm_ref[1, 1:2, :] + norm_ref[1, 2:3, :]
    sums = [0.0, 0.0, 0.0]
    for i in range(4):
        grad = backward_taps(db, wb, i) + u2in[:, columns(i)]
        x1 = (y2in[:, columns(i)] - c1) * i1
        x2 = (ysin[:, columns(i)] - c2) * i2
        v = x1 * g1 + x2 * g2 + shift
        s = sigmoid(v)
        u = grad * (s * (1.0 + v * (1.0 - s)))
        ub[:, columns(i)] = u
        move.store(ub.at[:, columns(i)], u1_ref.at[:, columns(i)])
        valid = u * mask
        sums[0] += column_sum(valid * x1)
        sums[1] += column_sum(valid * x2)
        sums[2] += column_sum(valid)
    spread(st_ref, pack(sums))
    move.finish()


def k_back_second(
    u1_ref, y2_ref, ys_ref, recv_ref, norm_ref, base_ref, keep12_ref, one_ref, y1_ref, count_ref,
    dy2_ref, dys_ref, u0_ref, st_ref, tot_ref,
    uin, y2in, ysin, y1in, db, dsb, wb, ub, sems,
):
    move = Mover(sems)
    first = []
    for o in range(4):
        first.append(
            [
                move.load(ref.at[:, columns(o)], buf.at[:, columns(o)])
                for ref, buf in ((u1_ref, uin), (y2_ref, y2in), (ys_ref, ysin))
            ]
        )
    lw = move.load(one_ref.at[pl.ds(10 * CIN, 9 * COUT)], wb)
    ly1 = move.load(y1_ref, y1in)
    got = jnp.sum(recv_ref[...], axis=0)
    tot_ref[...] = got
    positions = base_ref[2:3, :]
    mask = mask_of(count_ref)
    scale1, scale2, shift_total = (channel_row(got, k) for k in range(3))
    c1, i1, c2, i2 = (keep12_ref[k : k + 1, :] for k in range(4))
    for o in range(4):
        for copy in first[o]:
            copy.wait()
        u = uin[:, columns(o)]
        dy2 = reverse_norm(
            u, y2in[:, columns(o)], mask, c1, i1, norm_ref[0, 1:2, :], scale1, shift_total, positions
        )
        db[:, columns(o)] = dy2.astype(bf16)
        move.store(db.at[:, columns(o)], dy2_ref.at[:, columns(o)])
        dys = reverse_norm(
            u, ysin[:, columns(o)], mask, c2, i2, norm_ref[0, 2:3, :], scale2, shift_total, positions
        )
        dsb[:, columns(o)] = dys.astype(bf16)
        move.store(dsb.at[:, columns(o)], dys_ref.at[:, columns(o)])
    lw.wait()
    ly1.wait()
    centre, inverse = base_ref[0:1, :], base_ref[1:2, :]
    gain, shift = norm_ref[0, 0:1, :], norm_ref[1, 0:1, :]
    sums = [0.0, 0.0]
    for i in range(4):
        grad = backward_taps(db, wb, i)
        xhat = (y1in[:, columns(i)] - centre) * inverse
        v = xhat * gain + shift
        s = sigmoid(v)
        u = grad * (s * (1.0 + v * (1.0 - s)))
        ub[:, columns(i)] = u
        move.store(ub.at[:, columns(i)], u0_ref.at[:, columns(i)])
        valid = u * mask
        sums[0] += column_sum(valid * xhat)
        sums[1] += column_sum(valid)
    spread(st_ref, pack(sums))
    move.finish()


def k_back_first(
    u0_ref, y1_ref, recv_ref, norm_ref, base_ref, count_ref, dy_ref, tot_ref, uin, yin, db, sems
):
    move = Mover(sems)
    lu, ly = [], []
    for o in range(4):
        lu.append(move.load(u0_ref.at[:, columns(o)], uin.at[:, columns(o)]))
        ly.append(move.load(y1_ref.at[:, columns(o)], yin.at[:, columns(o)]))
    got = jnp.sum(recv_ref[...], axis=0)
    tot_ref[...] = got
    positions = base_ref[2:3, :]
    mask = mask_of(count_ref)
    scale_total, shift_total = channel_row(got, 0), channel_row(got, 1)
    for o in range(4):
        lu[o].wait()
        ly[o].wait()
        dy = reverse_norm(
            uin[:, columns(o)], yin[:, columns(o)], mask, base_ref[0:1, :], base_ref[1:2, :],
            norm_ref[0, 0:1, :], scale_total, shift_total, positions,
        )
        db[:, columns(o)] = dy.astype(bf16)
        move.store(db.at[:, columns(o)], dy_ref.at[:, columns(o)])
    move.finish()


def k_turn(x_ref, side_ref, mine_ref, theirs_ref, xb, at, tb, sems):
    move = Mover(sems)
    loads = [
        move.load(x_ref.at[:, columns(o)], xb.at[:, columns(o)]) for o in range(16 * CIN // COUT)
    ]
    for cell in range(16):
        if cell % 2 == 0:
            loads[cell // 2].wait()
        split_turn(at, tb, xb[:, pl.ds(cell * CIN, CIN)], cell, CIN)
    hand_out(move, at, side_ref, mine_ref, theirs_ref)
    move.finish()


def pair_taps(move, lefts, rights, gb, grads_ref, base, half, side_in, stride):
    for tap in range(9):
        total = None
        for o in range(4):
            row_in = stride * (o // 2) + tap // 3 - 1
            col_in = stride * (o % 2) + tap % 3 - 1
            if not (0 <= row_in < side_in and 0 <= col_in < side_in):
                continue
            cell = row_in * side_in + col_in
            for left, right in zip(lefts, rights):
                part = dot(left[pl.ds(cell * half, half), :], right[:, columns(o)])
                total = part if total is None else total + part
        gb[pl.ds(tap * half, half), :] = total.astype(bf16)
        move.store(gb.at[pl.ds(tap * half, half)], grads_ref.at[pl.ds(base + tap * half, half)])


def k_pair_grad(
    mine_ref, got_ref, dy_ref, dyg_ref, grads_ref, mb, ob, db, dgb, gb, sems
):
    move = Mover(sems)
    loads = [
        move.load(src, dst)
        for src, dst in ((mine_ref, mb), (dy_ref, db), (got_ref, ob), (dyg_ref, dgb))
    ]
    for copy in loads:
        copy.wait()
    pair_taps(move, (mb, ob), (db, dgb), gb, grads_ref, 0, COUT // 2, 2, 1)
    move.finish()


def k_pair_second(
    mine_ref, got_ref, dy_ref, dyg_ref, xm_ref, xg_ref, dys_ref, dysg_ref, grads_ref,
    mb, ob, db, dgb, gb, xmb, xgb, dsb, dsgb, gsb, sems,
):
    move = Mover(sems)
    half = CIN // 2
    loads = [
        move.load(src, dst)
        for src, dst in ((mine_ref, mb), (dy_ref, db), (got_ref, ob), (dyg_ref, dgb))
    ]
    later = [move.load(dys_ref, dsb), move.load(dysg_ref, dsgb)]
    for o in range(4):
        cell = (o // 2) * 8 + (o % 2) * 2
        for src, dst in ((xm_ref, xmb), (xg_ref, xgb)):
            later.append(move.load(src.at[pl.ds(cell * half, half)], dst.at[pl.ds(o * half, half)]))
    for copy in loads:
        copy.wait()
    pair_taps(move, (mb, ob), (db, dgb), gb, grads_ref, 10 * half, COUT // 2, 2, 1)
    for copy in later:
        copy.wait()
    total = None
    for o in range(4):
        for left, right in ((xmb, dsb), (xgb, dsgb)):
            part = dot(left[pl.ds(o * half, half), :], right[:, columns(o)])
            total = part if total is None else total + part
    gsb[...] = total.astype(bf16)
    move.store(gsb, grads_ref.at[pl.ds(9 * half, half)])
    move.finish()


def k_pair_first(
    xm_ref, xg_ref, dy_ref, dyg_ref, gone_ref, grads_ref, mb, ob, db, dgb, gb, sems
):
    del gone_ref
    move = Mover(sems)
    loads = [
        move.load(src, dst)
        for src, dst in ((xm_ref, mb), (dy_ref, db), (xg_ref, ob), (dyg_ref, dgb))
    ]
    for copy in loads:
        copy.wait()
    pair_taps(move, (mb, ob), (db, dgb), gb, grads_ref, 0, CIN // 2, 4, 2)
    move.finish()


def k_input_grad(dy_ref, dys_ref, one_ref, dx_ref, db, dsb, wb, xb, sems):
    move = Mover(sems)
    loads = [
        move.load(one_ref.at[pl.ds(0, 10 * CIN)], wb),
        move.load(dy_ref, db),
        move.load(dys_ref, dsb),
    ]
    for copy in loads:
        copy.wait()
    for cell in range(16):
        row_in, col_in = divmod(cell, 4)
        total = None
        for o in range(4):
            row_tap, col_tap = row_in - 2 * (o // 2) + 1, col_in - 2 * (o % 2) + 1
            if not (0 <= row_tap < 3 and 0 <= col_tap < 3):
                continue
            part = dot_nt(db[:, columns(o)], wb[pl.ds((row_tap * 3 + col_tap) * CIN, CIN), :])
            total = part if total is None else total + part
        if row_in % 2 == 0 and col_in % 2 == 0:
            o = (row_in // 2) * 2 + col_in // 2
            total = total + dot_nt(dsb[:, columns(o)], wb[pl.ds(9 * CIN, CIN), :])
        xb[:, pl.ds(cell * CIN, CIN)] = total
        move.store(xb.at[:, pl.ds(cell * CIN, CIN)], dx_ref.at[:, pl.ds(cell * CIN, CIN)])
    move.finish()


def nesterov(grad, master, momentum, average, rate):
    moment = momentum_decay * momentum + grad
    fresh = master - rate * (grad + momentum_decay * moment)
    return (moment, fresh, average_decay * average + (1.0 - average_decay) * fresh)


def exchange(packed):
    return lax.all_to_all(packed, AXES, 0, 0, tiled=True)


def swap(value, devices, bits):
    return lax.ppermute(value, AXES, [(i, i ^ bits) for i in range(devices)])


def part_of(value, index, axis):
    return lax.dynamic_index_in_dim(value, index, axis, keepdims=False)


def add(left, right):
    return (left.astype(f32) + right.astype(f32)).astype(bf16)


class Grid:
    def __init__(self, devices):
        self.devices = devices
        number = lax.axis_index("batch") * lax.axis_size("pass") + lax.axis_index("pass")
        self.side, self.x, self.y, self.z = (
            number % 2,
            (number // 2) % 2,
            (number // 4) % 2,
            number // 8,
        )

    def swap(self, value, bits):
        return swap(value, self.devices, bits)


def scatter_plane(grid, grads):
    half = COUT // 2
    left, right = grads[..., :half], grads[..., half:]
    got_left = grid.swap(part_of(left, 1 - grid.x, 2), 2)
    got_right = grid.swap(part_of(right, 1 - grid.y, 1), 4)
    left = add(part_of(left, grid.x, 2), got_left)
    right = add(part_of(right, grid.y, 1), got_right)
    got_left = grid.swap(part_of(left, 1 - grid.y, 1), 4)
    got_right = grid.swap(part_of(right, 1 - grid.x, 1), 2)
    return jnp.concatenate(
        [
            add(part_of(left, grid.y, 1), got_left),
            add(part_of(right, grid.x, 1), got_right),
        ],
        axis=-1,
    )


def scatter_line(grid, value):
    total = part_of(value, grid.z, 0).astype(f32)
    for other in (1, 2, 3):
        total = total + grid.swap(part_of(value, grid.z ^ other, 0), other * 8).astype(f32)
    got = grid.swap(part_of(total, 1 - grid.side, 0).astype(bf16), 1).astype(f32)
    own = part_of(total, grid.side, 0)
    rows = own.shape[0]
    own, got = (v.reshape(rows // 16, 16, COUT) for v in (own, got))
    first = jnp.where(grid.side == 0, own, got)
    second = jnp.where(grid.side == 0, got, own)
    return jnp.stack([first, second], axis=1).reshape(2 * rows, COUT)


def reduce_halves(devices, side, half_grad):
    groups = half_grad.reshape(-1, 16, COUT)
    empty = jnp.zeros_like(groups)
    full = jnp.stack(
        [jnp.where(side == 0, groups, empty), jnp.where(side == 0, empty, groups)], axis=1
    ).reshape(-1, COUT)
    return lax.psum_scatter(full, AXES, scatter_dimension=0, tiled=True).astype(f32)


def make_shards(devices, fast):
    def shards(
        features,
        labels,
        image_counts,
        block_one_master,
        block_one_momentum,
        block_one_average,
        block_two_master,
        block_two_momentum,
        block_two_average,
        norm_params,
        norm_momentum,
        norm_average,
        head_params,
        head_momentum,
        head_average,
    ):
        images_all = CAP * devices
        count = image_counts
        side = (lax.axis_index("pass") % 2).astype(jnp.int32).reshape(1, 1)
        one = lax.all_gather(block_one_master.astype(bf16), AXES, axis=0, tiled=True)
        two = lax.all_gather(block_two_master.astype(bf16), AXES, axis=0, tiled=True)
        x = features.reshape(CAP, 16 * CIN)

        rows_one, rows_two = one.shape[0], two.shape[0]
        wide_f, wide_b = shape((CAP, WIDE), f32), shape((CAP, WIDE), bf16)
        wf, wb16 = pltpu.VMEM((CAP, WIDE), f32), pltpu.VMEM((CAP, WIDE), bf16)
        weight = pltpu.VMEM((9 * COUT, COUT), bf16)
        small = shape((8, COUT), f32)
        packed8, packed16 = shape((8, LANES), f32), shape((16, LANES), f32)
        send8, send16 = shape((devices, 8, LANES), f32), shape((devices, 16, LANES), f32)

        def sems(n):
            return pltpu.SemaphoreType.DMA((n,))

        conv_flops = 2 * 16 * CAP * COUT * COUT
        first_flops = 2 * 29 * CAP * CIN * COUT
        head_rows = head_params[:COUT]
        pad = LANES - 3 * TASKS

        def thrice(v):
            return jnp.concatenate([v, v, v, jnp.zeros((v.shape[0], pad), v.dtype)], axis=1)

        head_wide = thrice(head_rows)
        bias_wide = thrice(head_params[COUT:])
        labels_wide = thrice(labels.astype(f32))
        turned = jnp.pad(head_rows.T, ((0, LANES - TASKS), (0, 0)))
        square = jnp.pad(
            jnp.dot(head_rows.T, head_rows, precision=highest), ((0, 0), (0, LANES - TASKS))
        )

        turned_half = shape((WIDE // 2, CAP), bf16)
        turn_scratch = [pltpu.VMEM((2, WIDE // 2, CAP), bf16), pltpu.VMEM((COUT, CAP), bf16)]

        def sibling(value):
            return swap(value, devices, 1)

        x_mine, x_theirs = run(
            k_turn,
            (x, side),
            [HBM, SMEM],
            [shape((8 * CIN, CAP), bf16)] * 2,
            [HBM, HBM],
            [
                pltpu.VMEM((CAP, 16 * CIN), bf16),
                pltpu.VMEM((2, 8 * CIN, CAP), bf16),
                pltpu.VMEM((COUT, CAP), bf16),
                sems(10),
            ],
            0,
            4_000_000,
            name="turn_features",
        )
        x_got = sibling(x_theirs)
        y1, ys, st, local = run(
            k_first,
            (x, one, count),
            [HBM, HBM, SMEM],
            [wide_f, wide_f, send16, packed8],
            [HBM, HBM, VMEM, VMEM],
            [
                pltpu.VMEM((CAP, 16 * CIN), bf16),
                pltpu.VMEM((10 * CIN, COUT), bf16),
                pltpu.VMEM((2, CAP, WIDE), f32),
                sems(10),
            ],
            first_flops,
            9_000_000,
            name="first_conv",
        )
        got = exchange(st)
        a1_mine, a1_theirs, y2, st, keep0 = run(
            k_second,
            (y1, got, norm_params, local, one, count, side),
            [HBM, VMEM, VMEM, VMEM, HBM, SMEM, SMEM],
            [turned_half, turned_half, wide_f, send16, small],
            [HBM, HBM, HBM, VMEM, VMEM],
            [wf, wb16, *turn_scratch, weight, wf, sems(11)],
            conv_flops,
            10_000_000,
            name="second_conv",
        )
        got = exchange(st)
        a1_got = sibling(a1_theirs)
        h1, hb_mine, hb_theirs, y3, st, keep12 = run(
            k_third,
            (y2, ys, got, norm_params, keep0, two, count, side),
            [HBM, HBM, VMEM, VMEM, VMEM, HBM, SMEM, SMEM],
            [wide_f, turned_half, turned_half, wide_f, send8, small],
            [HBM, HBM, HBM, HBM, VMEM, VMEM],
            [wf, wf, wf, wb16, *turn_scratch, weight, wf, sems(19)],
            conv_flops,
            14_000_000,
            name="third_conv",
        )
        got = exchange(st)
        hb_got = sibling(hb_theirs)
        a3_mine, a3_theirs, y4, st, keep3 = run(
            k_fourth,
            (y3, got, norm_params, keep0, two, count, side),
            [HBM, VMEM, VMEM, VMEM, HBM, SMEM, SMEM],
            [turned_half, turned_half, wide_f, send8, small],
            [HBM, HBM, HBM, VMEM, VMEM],
            [wf, wb16, *turn_scratch, weight, wf, sems(11)],
            conv_flops,
            10_000_000,
            name="fourth_conv",
        )
        got = exchange(st)
        a3_got = sibling(a3_theirs)
        wide_lanes = shape((CAP, LANES), f32)
        pooled, resid, slope, st, part, keep4 = run(
            k_heads,
            (y4, h1, got, norm_params, keep0, head_wide, bias_wide, labels_wide, count),
            [HBM, HBM, VMEM, VMEM, VMEM, VMEM, VMEM, VMEM, SMEM],
            [
                shape((CAP, COUT), f32),
                wide_lanes,
                wide_f,
                send16,
                shape((8 * devices, LANES), f32),
                small,
            ],
            [VMEM, VMEM, HBM, VMEM, VMEM, VMEM],
            [wf, wf, wf, sems(12)],
            1_000_000_000,
            7_000_000,
            name="heads",
        )
        got = exchange(st)
        weights, u2, st = run(
            k_weights,
            (
                got, square, resid, turned, keep0, keep4, part.reshape(devices, 8, LANES), y4, slope, count,
            ),
            [VMEM, VMEM, VMEM, VMEM, VMEM, VMEM, VMEM, HBM, HBM, SMEM],
            [packed8, wide_f, send16],
            [VMEM, HBM, VMEM],
            [wf, wf, wf, sems(12)],
            1_000_000_000,
            7_000_000,
            name="task_weights",
        )

        got = exchange(st)
        dy4, u3, st, tot4 = run(
            k_back_fourth,
            (u2, y4, got, norm_params, keep0, keep4, two, y3, keep3, count),
            [HBM, HBM, VMEM, VMEM, VMEM, VMEM, HBM, HBM, VMEM, SMEM],
            [wide_b, wide_f, send16, packed8],
            [HBM, HBM, VMEM, VMEM],
            [wf, wf, wf, wb16, weight, wf, sems(18)],
            conv_flops,
            14_000_000,
            name="fourth_back",
        )
        got = exchange(st)
        half_rows = 9 * COUT // 2
        half_turned = pltpu.VMEM((WIDE // 2, CAP), bf16)
        pair_scratch = [half_turned, half_turned, wb16, wb16, pltpu.VMEM((half_rows, COUT), bf16)]

        def pair_grad(mine, theirs, dy, dy_got, name):
            return run(
                k_pair_grad,
                (mine, theirs, dy, dy_got),
                [HBM] * 4,
                shape((half_rows, COUT), bf16),
                HBM,
                [*pair_scratch, sems(13)],
                conv_flops,
                6_000_000,
                name=name,
            )

        grads_four = pair_grad(a3_mine, a3_got, dy4, sibling(dy4), "fourth_weights")
        dy3, u1, st, tot3, head_sum = run(
            k_back_third,
            (u3, y3, got, norm_params, keep0, keep3, two, u2, y2, ys, keep12, count),
            [HBM, HBM, VMEM, VMEM, VMEM, VMEM, HBM, HBM, HBM, HBM, VMEM, SMEM],
            [wide_b, wide_f, send16, packed8, send8],
            [HBM, HBM, VMEM, VMEM, VMEM],
            [wf, wf, wf, wf, wf, wb16, weight, wf, sems(20)],
            conv_flops,
            18_000_000,
            name="third_back",
        )
        got = exchange(st)
        grads_three = pair_grad(hb_mine, hb_got, dy3, sibling(dy3), "third_weights")
        dy2, dys, u0, st, tot12 = run(
            k_back_second,
            (u1, y2, ys, got, norm_params, keep0, keep12, one, y1, count),
            [HBM, HBM, HBM, VMEM, VMEM, VMEM, VMEM, HBM, HBM, SMEM],
            [wide_b, wide_b, wide_f, send8, packed16],
            [HBM, HBM, HBM, VMEM, VMEM],
            [wf, wf, wf, wf, wb16, wb16, weight, wf, sems(26)],
            conv_flops,
            18_000_000,
            name="second_back",
        )
        got = exchange(st)
        dys_got = sibling(dys)
        grads_one = run(
            k_pair_second,
            (a1_mine, a1_got, dy2, sibling(dy2), x_mine, x_got, dys, dys_got),
            [HBM] * 8,
            shape((rows_one // 2, COUT), bf16),
            HBM,
            [
                *pair_scratch,
                pltpu.VMEM((2 * CIN, CAP), bf16),
                pltpu.VMEM((2 * CIN, CAP), bf16),
                wb16,
                wb16,
                pltpu.VMEM((CIN // 2, COUT), bf16),
                sems(24),
            ],
            conv_flops,
            9_000_000,
            name="second_weights",
        )
        dy1, tot0 = run(
            k_back_first,
            (u0, y1, got, norm_params, keep0, count),
            [HBM, HBM, VMEM, VMEM, VMEM, SMEM],
            [wide_b, packed8],
            [HBM, VMEM],
            [wf, wf, wb16, sems(12)],
            0,
            5_000_000,
            name="first_back",
        )
        half_features = pltpu.VMEM((8 * CIN, CAP), bf16)
        grads_one = run(
            k_pair_first,
            (x_mine, x_got, dy1, sibling(dy1), grads_one),
            [HBM] * 5,
            shape((rows_one // 2, COUT), bf16),
            HBM,
            [
                half_features,
                half_features,
                wb16,
                wb16,
                pltpu.VMEM((9 * CIN // 2, COUT), bf16),
                sems(13),
            ],
            first_flops,
            8_000_000,
            {4: 0},
            name="first_weights",
        )
        if fast:
            grid = Grid(devices)
            rows = rows_two // devices // 2
            planes = [
                scatter_plane(grid, g.reshape(2, 2, 2, 2, rows, COUT))
                for g in (grads_three, grads_four)
            ]
            two_sum = scatter_line(grid, jnp.concatenate(planes, axis=0))
            rows = rows_one // devices // 2
            one_sum = scatter_line(
                grid, scatter_plane(grid, grads_one.reshape(4, 2, 2, 2, rows, COUT))
            )
        else:
            two_sum = reduce_halves(
                devices, side[0, 0], jnp.concatenate([grads_three, grads_four], axis=0)
            )
            one_sum = reduce_halves(devices, side[0, 0], grads_one)
        dx = run(
            k_input_grad,
            (dy1, dys, one),
            [HBM, HBM, HBM],
            shape((CAP, 16 * CIN), f32),
            HBM,
            [
                wb16,
                wb16,
                pltpu.VMEM((10 * CIN, COUT), bf16),
                pltpu.VMEM((CAP, 16 * CIN), f32),
                sems(19),
            ],
            first_flops,
            9_000_000,
            name="input_grad",
        )
        input_grad = dx.reshape(CAP, 4, 4, CIN)

        def unpacked(packed):
            return packed.reshape(-1, COUT)

        t0, t3, t4, t12 = unpacked(tot0), unpacked(tot3), unpacked(tot4), unpacked(tot12)
        norm_grad = jnp.stack(
            [
                jnp.stack([t0[0], t12[0], t12[1], t3[0], t4[0]]),
                jnp.stack([t0[1], t12[2], t12[2], t3[1], t4[1]]),
            ]
        )
        total = keep0[2, 0] * 0.25
        head_sum = head_sum.reshape(-1, LANES)[: 5 * TASKS].reshape(5, TASKS, LANES)
        task_losses = head_sum[4, :, 1] / total
        head_grad = jnp.concatenate(
            [head_sum[:4].transpose(0, 2, 1).reshape(COUT, TASKS), head_sum[4, :, 0][None]], axis=0
        ) / total
        scale_rate = math.sqrt(images_all)
        one_m, one_w, one_a = nesterov(
            one_sum,
            block_one_master,
            block_one_momentum,
            block_one_average,
            rate_conv * scale_rate,
        )
        two_m, two_w, two_a = nesterov(
            two_sum,
            block_two_master,
            block_two_momentum,
            block_two_average,
            rate_conv * scale_rate,
        )
        norm_m, norm_w, norm_a = nesterov(
            norm_grad, norm_params, norm_momentum, norm_average, rate_norm * scale_rate
        )
        head_m, head_w, head_a = nesterov(
            head_grad, head_params, head_momentum, head_average, rate_head * scale_rate
        )
        return (
            pooled,
            input_grad,
            task_losses,
            weights[0, :TASKS],
            one_m,
            one_w,
            one_a,
            one_w.astype(bf16),
            two_m,
            two_w,
            two_a,
            two_w.astype(bf16),
            norm_m,
            norm_w,
            norm_a,
            head_m,
            head_w,
            head_a,
        )

    return shards


def solution(mesh):
    devices = mesh.shape["batch"] * mesh.shape["pass"]
    fast = mesh.shape["batch"] == 8 and mesh.shape["pass"] == 4
    rows = P(AXES, None)
    in_specs = (
        P(AXES, None, None, None),
        rows,
        P("batch", "pass"),
        rows,
        rows,
        rows,
        rows,
        rows,
        rows,
        P(),
        P(),
        P(),
        P(),
        P(),
        P(),
    )
    out_specs = (
        rows,
        P(AXES, None, None, None),
        P(),
        P(),
        rows,
        rows,
        rows,
        rows,
        rows,
        rows,
        rows,
        rows,
        P(),
        P(),
        P(),
        P(),
        P(),
        P(),
    )
    return jax.shard_map(
        make_shards(devices, fast), mesh=mesh, in_specs=in_specs, out_specs=out_specs, check_vma=False
    )
```

```python
import math

import jax
import jax.numpy as jnp
from jax import lax
from jax.experimental import pallas as pl
from jax.experimental.pallas import tpu as pltpu
from jax.sharding import PartitionSpec as P

CIN = 256
COUT = 512
TASKS = 40
FW_STEPS = 20
CAP = 256
WIDE = 4 * COUT
LANES = 128
AXES = ("batch", "pass")

epsilon = 1e-05
softness = 0.01
momentum_decay = 0.9
average_decay = 0.9
rate_conv = 3.0
rate_norm = 50.0
rate_head = 0.05
highest = lax.Precision.HIGHEST

HBM = pl.BlockSpec(memory_space=pltpu.HBM)
VMEM = pl.BlockSpec(memory_space=pltpu.VMEM)
SMEM = pl.BlockSpec(memory_space=pltpu.SMEM)
f32 = jnp.float32
bf16 = jnp.bfloat16


def shape(extent, kind):
    return jax.ShapeDtypeStruct(extent, kind)


def run(
    body, args, in_specs, outs, out_specs, scratch, flops=0, moved=0, aliases=None, name=None, after=()
):
    first, last = len(args), len(args) + len(after)

    def plain(*refs):
        body(*refs[:first], *refs[last:])

    args, in_specs = (*args, *after), [*in_specs, *[HBM] * len(after)]
    return pl.pallas_call(
        plain if after else body,
        out_shape=outs,
        in_specs=in_specs,
        out_specs=out_specs,
        scratch_shapes=scratch,
        input_output_aliases=aliases or {},
        compiler_params=pltpu.CompilerParams(vmem_limit_bytes=60 * 1024 * 1024),
        cost_estimate=pl.CostEstimate(
            flops=flops // 100, bytes_accessed=moved // 100, transcendentals=0
        ),
        name=name,
    )(*args)


class Mover:
    def __init__(self, sems):
        self.sems = sems
        self.used = 0
        self.out = []

    def load(self, src, dst):
        copy = pltpu.make_async_copy(src, dst, self.sems.at[self.used])
        self.used += 1
        copy.start()
        return copy

    def store(self, src, dst):
        self.out.append(self.load(src, dst))

    def finish(self):
        for copy in self.out:
            copy.wait()


def columns(o):
    return pl.ds(o * COUT, COUT)


def split_turn(at, tb, value, place, channels):
    half = channels // 2
    tb[pl.ds(0, channels), :] = value.T
    for group in range(half // 16):
        for parity in range(2):
            at[parity, pl.ds(place * half + 16 * group, 16), :] = tb[
                pl.ds(32 * group + 16 * parity, 16), :
            ]


def hand_out(move, at, side_ref, mine_ref, theirs_ref):
    side = side_ref[0, 0]
    move.store(at.at[side], mine_ref)
    move.store(at.at[1 - side], theirs_ref)


def dot(left, right, precision=None):
    return jnp.dot(left, right, preferred_element_type=f32, precision=precision)


def dot_nt(left, right):
    return lax.dot_general(left, right, (((1,), (1,)), ((), ())), preferred_element_type=f32)


def dot_tn(left, right, precision=None):
    return lax.dot_general(
        left, right, (((0,), (0,)), ((), ())), preferred_element_type=f32, precision=precision
    )


def sigmoid(v):
    return 0.5 * jnp.tanh(0.5 * v) + 0.5


def channel_row(packed, k):
    return jnp.concatenate([packed[4 * k + b : 4 * k + b + 1, :] for b in range(4)], axis=1)


def pack(rows):
    pieces = [row[:, b * LANES : (b + 1) * LANES] for row in rows for b in range(4)]
    while len(pieces) % 8:
        pieces.append(jnp.zeros((1, LANES), f32))
    return jnp.concatenate(pieces, axis=0)


def spread(out_ref, packed):
    out_ref[...] = jnp.broadcast_to(packed[None], out_ref.shape)


def mask_of(count_ref):
    rows = lax.broadcasted_iota(jnp.int32, (CAP, COUT), 0)
    return (rows < count_ref[0, 0]).astype(f32)


def column_sum(v):
    return jnp.sum(v, axis=0, keepdims=True)


def moments(total_sum, total_square, positions):
    centre = total_sum / positions
    spread_value = total_square / positions - centre * centre
    return centre, lax.rsqrt(spread_value + epsilon)


def forward_taps(act_ref, w_ref, o, base=0):
    row_out, col_out = divmod(o, 2)
    total = None
    for row_in in range(2):
        tap = (row_in - row_out + 1) * 3 + (1 - col_out)
        part = dot(
            act_ref[:, pl.ds(row_in * 2 * COUT, 2 * COUT)],
            w_ref[pl.ds(base + tap * COUT, 2 * COUT), :],
        )
        total = part if total is None else total + part
    return total


def tap_of(i, o):
    return (i // 2 - o // 2 + 1) * 3 + (i % 2 - o % 2 + 1)


def backward_taps(dy_ref, w_ref, i):
    total = None
    for o in range(4):
        part = dot_nt(dy_ref[:, columns(o)], w_ref[pl.ds(tap_of(i, o) * COUT, COUT), :])
        total = part if total is None else total + part
    return total


def first_pairs(o):
    row_out, col_out = divmod(o, 2)
    runs = []
    for row_tap in range(3):
        row_in = 2 * row_out + row_tap - 1
        if 0 <= row_in < 4:
            col_tap = 1 if col_out == 0 else 0
            runs.append((row_in * 4 + 2 * col_out + col_tap - 1, row_tap * 3 + col_tap, 3 - col_tap))
    return runs


def pieces_of(refs):
    found = []
    for side in range(2):
        for k, bits in ((0, 0), (1, 2), (2, 4), (3, 6), (4, 6)):
            ref = refs[5 * side + k]
            for z in range(4):
                found.append((ref.at[z], 8 * z + bits + side, ref.shape[1] if k == 4 else 0))
    return found


class Rows:
    def __init__(self, move, refs, number_ref, buf, low, high):
        self.waits = []
        if len(refs) == 1:
            self.rows = buf
            self.low = low
            copy = move.load(refs[0].at[pl.ds(low, high - low)], buf.at[pl.ds(low, high - low)])
            self.waits.append((None, copy))
            return
        per = buf.shape[1]
        number = number_ref[0, 0]
        for src, bits, row in pieces_of(refs):
            owner = jnp.bitwise_xor(number, bits)
            live = jnp.logical_and(owner >= low // per, owner < -(-high // per))
            copy = pltpu.make_async_copy(
                src, buf.at[owner, pl.ds(row, src.shape[0])], move.sems.at[move.used]
            )
            move.used += 1
            pl.when(live)(copy.start)
            self.waits.append((live, copy))
        self.rows = buf.reshape(buf.shape[0] * per, COUT)

    def wait(self):
        for live, copy in self.waits:
            if live is None:
                copy.wait()
            else:
                pl.when(live)(copy.wait)
        return self.rows


def make_first(sources):
    def body(*refs):
        x_ref, *one_refs = refs[: 1 + sources]
        number_ref, count_ref, y1_ref, ys_ref, st_ref, local_ref, kept_ref, xb, wb, yb, sems = refs[
            1 + sources :
        ]
        move = Mover(sems)
        lx = move.load(x_ref, xb)
        rows = Rows(move, one_refs, number_ref, wb, 0, 10 * CIN)
        mask = mask_of(count_ref)
        lx.wait()
        wr = rows.wait()
        move.store(wr.at[pl.ds(0, 10 * CIN)], kept_ref)
        first_body(move, xb, wr, yb, mask, count_ref, y1_ref, ys_ref, st_ref, local_ref)

    return body


def first_body(move, xb, wb, yb, mask, count_ref, y1_ref, ys_ref, st_ref, local_ref):
    sums = [0.0, 0.0, 0.0, 0.0]
    for o in range(4):
        total = None
        for cell, tap, cells in first_pairs(o):
            part = dot(xb[:, pl.ds(cell * CIN, cells * CIN)], wb[pl.ds(tap * CIN, cells * CIN), :])
            total = part if total is None else total + part
        yb[0, :, columns(o)] = total
        move.store(yb.at[0, :, columns(o)], y1_ref.at[:, columns(o)])
        valid = total * mask
        sums[0] += column_sum(valid)
        sums[1] += column_sum(valid * total)
        cell = (o // 2) * 8 + (o % 2) * 2
        total = dot(xb[:, pl.ds(cell * CIN, CIN)], wb[pl.ds(9 * CIN, CIN), :])
        yb[1, :, columns(o)] = total
        move.store(yb.at[1, :, columns(o)], ys_ref.at[:, columns(o)])
        valid = total * mask
        sums[2] += column_sum(valid)
        sums[3] += column_sum(valid * total)
    counted = jnp.full((8, LANES), count_ref[0, 0].astype(f32), f32)
    spread(st_ref, jnp.concatenate([pack(sums[:2]), counted], axis=0))
    local_ref[...] = pack(sums[2:])
    move.finish()


def make_second(sources):
    def body(*refs):
        second_body(refs[:sources], *refs[sources:])

    return body


def second_body(
    one_refs, number_ref, y1_ref, recv_ref, norm_ref, local_ref, count_ref, side_ref,
    mine_ref, theirs_ref, y2_ref, st_ref, keep_ref, kept_ref,
    yin, ab, at, tb, wb, yb, sems,
):
    move = Mover(sems)
    ly = [move.load(y1_ref.at[:, columns(o)], yin.at[:, columns(o)]) for o in range(4)]
    rows = Rows(move, one_refs, number_ref, wb, 10 * CIN, 10 * CIN + 9 * COUT)
    got = jnp.sum(recv_ref[...], axis=0)
    total = got[8:9, 0:1]
    positions = 4.0 * total
    centre, inverse = moments(channel_row(got, 0), channel_row(got, 1), positions)
    keep_ref[...] = jnp.concatenate(
        [centre, inverse, jnp.broadcast_to(positions, (1, COUT)), jnp.zeros((5, COUT), f32)], axis=0
    )
    scale = norm_ref[0, 0:1, :] * inverse
    offset = norm_ref[1, 0:1, :] - centre * scale
    mask = mask_of(count_ref)
    for o in range(4):
        ly[o].wait()
        v = yin[:, columns(o)] * scale + offset
        ab[:, columns(o)] = (v * sigmoid(v)).astype(bf16)
        split_turn(at, tb, ab[:, columns(o)], o, COUT)
    hand_out(move, at, side_ref, mine_ref, theirs_ref)
    wr = rows.wait()
    move.store(wr.at[pl.ds(10 * CIN, 9 * COUT)], kept_ref)
    sums = [0.0, 0.0]
    for o in range(4):
        y = forward_taps(ab, wr, o, 10 * CIN)
        yb[:, columns(o)] = y
        move.store(yb.at[:, columns(o)], y2_ref.at[:, columns(o)])
        valid = y * mask
        sums[0] += column_sum(valid)
        sums[1] += column_sum(valid * y)
    spread(st_ref, jnp.concatenate([pack(sums), local_ref[...]], axis=0))
    move.finish()


def k_third(
    y2_ref, ys_ref, recv_ref, norm_ref, base_ref, two_ref, count_ref, side_ref,
    h1_ref, mine_ref, theirs_ref, y3_ref, st_ref, keep_ref,
    yin, sin, hout, ab, at, tb, wb, yb, sems,
):
    move = Mover(sems)
    ly, ls = [], []
    for o in range(4):
        ly.append(move.load(y2_ref.at[:, columns(o)], yin.at[:, columns(o)]))
        ls.append(move.load(ys_ref.at[:, columns(o)], sin.at[:, columns(o)]))
    lw = move.load(two_ref.at[pl.ds(0, 9 * COUT)], wb)
    got = jnp.sum(recv_ref[...], axis=0)
    positions = base_ref[2:3, :]
    c1, i1 = moments(channel_row(got, 0), channel_row(got, 1), positions)
    c2, i2 = moments(channel_row(got, 2), channel_row(got, 3), positions)
    keep_ref[...] = jnp.concatenate([c1, i1, c2, i2, jnp.zeros((4, COUT), f32)], axis=0)
    s1 = norm_ref[0, 1:2, :] * i1
    s2 = norm_ref[0, 2:3, :] * i2
    offset = norm_ref[1, 1:2, :] - c1 * s1 + (norm_ref[1, 2:3, :] - c2 * s2)
    mask = mask_of(count_ref)
    for o in range(4):
        ly[o].wait()
        ls[o].wait()
        v = yin[:, columns(o)] * s1 + sin[:, columns(o)] * s2 + offset
        h = v * sigmoid(v)
        hout[:, columns(o)] = h
        ab[:, columns(o)] = h.astype(bf16)
        move.store(hout.at[:, columns(o)], h1_ref.at[:, columns(o)])
        split_turn(at, tb, ab[:, columns(o)], o, COUT)
    hand_out(move, at, side_ref, mine_ref, theirs_ref)
    lw.wait()
    sums = [0.0, 0.0]
    for o in range(4):
        y = forward_taps(ab, wb, o)
        yb[:, columns(o)] = y
        move.store(yb.at[:, columns(o)], y3_ref.at[:, columns(o)])
        valid = y * mask
        sums[0] += column_sum(valid)
        sums[1] += column_sum(valid * y)
    spread(st_ref, pack(sums))
    move.finish()


def k_fourth(
    y3_ref, recv_ref, norm_ref, base_ref, two_ref, count_ref, side_ref,
    mine_ref, theirs_ref, y4_ref, st_ref, keep_ref,
    yin, ab, at, tb, wb, yb, sems,
):
    move = Mover(sems)
    ly = [move.load(y3_ref.at[:, columns(o)], yin.at[:, columns(o)]) for o in range(4)]
    lw = move.load(two_ref.at[pl.ds(9 * COUT, 9 * COUT)], wb)
    got = jnp.sum(recv_ref[...], axis=0)
    centre, inverse = moments(channel_row(got, 0), channel_row(got, 1), base_ref[2:3, :])
    keep_ref[...] = jnp.concatenate([centre, inverse, jnp.zeros((6, COUT), f32)], axis=0)
    scale = norm_ref[0, 3:4, :] * inverse
    offset = norm_ref[1, 3:4, :] - centre * scale
    mask = mask_of(count_ref)
    for o in range(4):
        ly[o].wait()
        v = yin[:, columns(o)] * scale + offset
        ab[:, columns(o)] = (v * sigmoid(v)).astype(bf16)
        split_turn(at, tb, ab[:, columns(o)], o, COUT)
    hand_out(move, at, side_ref, mine_ref, theirs_ref)
    lw.wait()
    sums = [0.0, 0.0]
    for o in range(4):
        y = forward_taps(ab, wb, o)
        yb[:, columns(o)] = y
        move.store(yb.at[:, columns(o)], y4_ref.at[:, columns(o)])
        valid = y * mask
        sums[0] += column_sum(valid)
        sums[1] += column_sum(valid * y)
    spread(st_ref, pack(sums))
    move.finish()


def k_heads(
    y4_ref, h1_ref, recv_ref, norm_ref, base_ref, head_ref, bias_ref, labels_ref, count_ref,
    pooled_ref, resid_ref, slope_ref, gram_ref, part_ref, keep_ref,
    yin, hin, sb, sems,
):
    move = Mover(sems)
    ly, lh = [], []
    for o in range(4):
        ly.append(move.load(y4_ref.at[:, columns(o)], yin.at[:, columns(o)]))
        lh.append(move.load(h1_ref.at[:, columns(o)], hin.at[:, columns(o)]))
    got = jnp.sum(recv_ref[...], axis=0)
    centre, inverse = moments(channel_row(got, 0), channel_row(got, 1), base_ref[2:3, :])
    keep_ref[...] = jnp.concatenate([centre, inverse, jnp.zeros((6, COUT), f32)], axis=0)
    scale = norm_ref[0, 4:5, :] * inverse
    offset = norm_ref[1, 4:5, :] - centre * scale
    total = None
    for o in range(4):
        ly[o].wait()
        lh[o].wait()
        v = yin[:, columns(o)] * scale + offset + hin[:, columns(o)]
        s = sigmoid(v)
        h = v * s
        sb[:, columns(o)] = s * (1.0 + v - h)
        move.store(sb.at[:, columns(o)], slope_ref.at[:, columns(o)])
        total = h if total is None else total + h
    pooled = total * 0.25
    pooled_ref[...] = pooled
    logits = dot(pooled, head_ref[...], highest) + bias_ref[...]
    labels = labels_ref[...]
    valid = (lax.broadcasted_iota(jnp.int32, (CAP, LANES), 0) < count_ref[0, 0]).astype(f32)
    resid = (sigmoid(logits) - labels) * valid
    resid_ref[...] = resid
    softplus = jnp.maximum(logits, 0.0) + jnp.log1p(jnp.exp(-jnp.abs(logits)))
    losses = valid * (softplus - labels * logits)
    gram = dot_tn(resid, resid, highest)
    lane = lax.broadcasted_iota(jnp.int32, (16, LANES), 1)
    packed = jnp.where(lane < TASKS, gram[0:16], jnp.where(lane < 2 * TASKS, gram[16:32], gram[32:48]))
    spread(gram_ref, packed)
    part_ref[...] = jnp.zeros(part_ref.shape, f32)
    for b in range(4):
        part_ref[pl.ds(b * TASKS, TASKS), :] = dot_tn(
            resid, pooled[:, b * LANES : (b + 1) * LANES], highest
        )[0:TASKS]
    ones = jnp.ones((CAP, LANES), f32)
    lane = lax.broadcasted_iota(jnp.int32, (TASKS, LANES), 1)
    part_ref[pl.ds(4 * TASKS, TASKS), :] = jnp.where(
        lane == 0, dot_tn(resid, ones, highest)[0:TASKS], dot_tn(losses, ones, highest)[0:TASKS]
    )
    move.finish()


def k_weights(
    recv_ref, square_ref, resid_ref, turned_ref, base_ref, keep_ref, part_ref, y4_ref, slope_ref, count_ref,
    weights_ref, u2_ref, st_ref,
    yin, sin, ub, sems,
):
    move = Mover(sems)
    ly, ls = [], []
    for o in range(4):
        ly.append(move.load(y4_ref.at[:, columns(o)], yin.at[:, columns(o)]))
        ls.append(move.load(slope_ref.at[:, columns(o)], sin.at[:, columns(o)]))
    total = base_ref[2:3, 0:1] * 0.25
    got = jnp.sum(recv_ref[...], axis=0)
    gram = jnp.concatenate(
        [
            got,
            pltpu.roll(got, LANES - TASKS, 1),
            pltpu.roll(got, LANES - 2 * TASKS, 1)[0:8],
        ],
        axis=0,
    )
    row_at = lax.broadcasted_iota(jnp.int32, (TASKS, LANES), 0)
    lane_at = lax.broadcasted_iota(jnp.int32, (TASKS, LANES), 1)
    gram = jnp.where(lane_at < TASKS, gram * square_ref[...], 0.0) / total
    trace = jnp.sum(
        jnp.sum(jnp.where(row_at == lane_at, gram, 0.0), axis=0, keepdims=True), axis=1, keepdims=True
    )
    scaled = gram / (trace / TASKS + 1e-06)
    live = lax.broadcasted_iota(jnp.int32, (1, LANES), 1) < TASKS
    weights = jnp.where(live, 1.0 / TASKS, 0.0)
    row = jnp.sum(scaled, axis=0, keepdims=True) / TASKS
    col = jnp.sum(scaled, axis=1, keepdims=True) / TASKS
    for turn in range(FW_STEPS):
        gamma = 2.0 / (turn + 3.0)
        low = jnp.min(col, axis=0, keepdims=True)
        grown_col = jnp.exp((low - col) / softness)
        grown_row = jnp.where(live, jnp.exp(jnp.where(live, (low - row) / softness, 0.0)), 0.0)
        share = gamma / jnp.sum(grown_col, axis=0, keepdims=True)
        weights = (1.0 - gamma) * weights + share * grown_row
        if turn + 1 < FW_STEPS:
            next_row = jnp.sum(scaled * grown_col, axis=0, keepdims=True)
            next_col = jnp.sum(scaled * grown_row, axis=1, keepdims=True)
            row = (1.0 - gamma) * row + share * next_row
            col = (1.0 - gamma) * col + share * next_col
    weights_ref[...] = jnp.broadcast_to(weights, (8, LANES))
    pooled_grad = dot(resid_ref[...] * (weights / total), turned_ref[...], highest) * 0.25
    centre, inverse = keep_ref[0:1, :], keep_ref[1:2, :]
    mask = mask_of(count_ref)
    sums = [0.0, 0.0]
    for o in range(4):
        ly[o].wait()
        ls[o].wait()
        u = pooled_grad * sin[:, columns(o)]
        ub[:, columns(o)] = u
        move.store(ub.at[:, columns(o)], u2_ref.at[:, columns(o)])
        valid = u * mask
        sums[0] += column_sum(valid * ((yin[:, columns(o)] - centre) * inverse))
        sums[1] += column_sum(valid)
    st_ref[:, 0:8, :] = jnp.broadcast_to(pack(sums)[None], part_ref.shape)
    st_ref[:, 8:16, :] = part_ref[...]
    move.finish()


def reverse_norm(g, y, mask, centre, inverse, gain, scale_total, shift_total, positions):
    xhat = (y - centre) * inverse
    return (gain * inverse) * (g - mask * ((shift_total + xhat * scale_total) / positions))


def k_back_fourth(
    u2_ref, y4_ref, recv_ref, norm_ref, base_ref, keep4_ref, two_ref, y3_ref, keep3_ref, count_ref,
    dy_ref, u3_ref, st_ref, tot_ref,
    uin, yin, zin, db, wb, ub, sems,
):
    move = Mover(sems)
    lu, ly = [], []
    for o in range(4):
        lu.append(move.load(u2_ref.at[:, columns(o)], uin.at[:, columns(o)]))
        ly.append(move.load(y4_ref.at[:, columns(o)], yin.at[:, columns(o)]))
    lw = move.load(two_ref.at[pl.ds(9 * COUT, 9 * COUT)], wb)
    lz = move.load(y3_ref, zin)
    got = jnp.sum(recv_ref[...], axis=0)
    tot_ref[...] = got[0:8]
    positions = base_ref[2:3, :]
    mask = mask_of(count_ref)
    scale_total, shift_total = channel_row(got, 0), channel_row(got, 1)
    for o in range(4):
        lu[o].wait()
        ly[o].wait()
        dy = reverse_norm(
            uin[:, columns(o)], yin[:, columns(o)], mask, keep4_ref[0:1, :], keep4_ref[1:2, :],
            norm_ref[0, 4:5, :], scale_total, shift_total, positions,
        )
        db[:, columns(o)] = dy.astype(bf16)
        move.store(db.at[:, columns(o)], dy_ref.at[:, columns(o)])
    lw.wait()
    lz.wait()
    centre, inverse = keep3_ref[0:1, :], keep3_ref[1:2, :]
    gain, shift = norm_ref[0, 3:4, :], norm_ref[1, 3:4, :]
    sums = [0.0, 0.0]
    for i in range(4):
        grad = backward_taps(db, wb, i)
        xhat = (zin[:, columns(i)] - centre) * inverse
        v = xhat * gain + shift
        s = sigmoid(v)
        u = grad * (s * (1.0 + v * (1.0 - s)))
        ub[:, columns(i)] = u
        move.store(ub.at[:, columns(i)], u3_ref.at[:, columns(i)])
        valid = u * mask
        sums[0] += column_sum(valid * xhat)
        sums[1] += column_sum(valid)
    spread(st_ref, jnp.concatenate([pack(sums), got[8:16]], axis=0))
    move.finish()


def k_back_third(
    u3_ref, y3_ref, recv_ref, norm_ref, base_ref, keep3_ref, two_ref, u2_ref, y2_ref, ys_ref, keep12_ref, count_ref,
    dy_ref, u1_ref, st_ref, tot_ref, head_ref,
    uin, yin, u2in, y2in, ysin, db, wb, ub, sems,
):
    move = Mover(sems)
    lu, ly = [], []
    for o in range(4):
        lu.append(move.load(u3_ref.at[:, columns(o)], uin.at[:, columns(o)]))
        ly.append(move.load(y3_ref.at[:, columns(o)], yin.at[:, columns(o)]))
    lw = move.load(two_ref.at[pl.ds(0, 9 * COUT)], wb)
    later = [move.load(u2_ref, u2in), move.load(y2_ref, y2in), move.load(ys_ref, ysin)]
    got = jnp.sum(recv_ref[:, 0:8, :], axis=0)
    tot_ref[...] = got
    head_ref[...] = recv_ref[:, 8:16, :]
    positions = base_ref[2:3, :]
    mask = mask_of(count_ref)
    scale_total, shift_total = channel_row(got, 0), channel_row(got, 1)
    for o in range(4):
        lu[o].wait()
        ly[o].wait()
        dy = reverse_norm(
            uin[:, columns(o)], yin[:, columns(o)], mask, keep3_ref[0:1, :], keep3_ref[1:2, :],
            norm_ref[0, 3:4, :], scale_total, shift_total, positions,
        )
        db[:, columns(o)] = dy.astype(bf16)
        move.store(db.at[:, columns(o)], dy_ref.at[:, columns(o)])
    lw.wait()
    for copy in later:
        copy.wait()
    c1, i1, c2, i2 = (keep12_ref[k : k + 1, :] for k in range(4))
    g1, g2 = norm_ref[0, 1:2, :], norm_ref[0, 2:3, :]
    shift = norm_ref[1, 1:2, :] + norm_ref[1, 2:3, :]
    sums = [0.0, 0.0, 0.0]
    for i in range(4):
        grad = backward_taps(db, wb, i) + u2in[:, columns(i)]
        x1 = (y2in[:, columns(i)] - c1) * i1
        x2 = (ysin[:, columns(i)] - c2) * i2
        v = x1 * g1 + x2 * g2 + shift
        s = sigmoid(v)
        u = grad * (s * (1.0 + v * (1.0 - s)))
        ub[:, columns(i)] = u
        move.store(ub.at[:, columns(i)], u1_ref.at[:, columns(i)])
        valid = u * mask
        sums[0] += column_sum(valid * x1)
        sums[1] += column_sum(valid * x2)
        sums[2] += column_sum(valid)
    spread(st_ref, pack(sums))
    move.finish()


def k_back_second(
    u1_ref, y2_ref, ys_ref, recv_ref, norm_ref, base_ref, keep12_ref, one_ref, y1_ref, count_ref,
    dy2_ref, dys_ref, u0_ref, st_ref, tot_ref,
    uin, y2in, ysin, y1in, db, dsb, wb, ub, sems,
):
    move = Mover(sems)
    first = []
    for o in range(4):
        first.append(
            [
                move.load(ref.at[:, columns(o)], buf.at[:, columns(o)])
                for ref, buf in ((u1_ref, uin), (y2_ref, y2in), (ys_ref, ysin))
            ]
        )
    lw = move.load(one_ref, wb)
    ly1 = move.load(y1_ref, y1in)
    got = jnp.sum(recv_ref[...], axis=0)
    tot_ref[...] = got
    positions = base_ref[2:3, :]
    mask = mask_of(count_ref)
    scale1, scale2, shift_total = (channel_row(got, k) for k in range(3))
    c1, i1, c2, i2 = (keep12_ref[k : k + 1, :] for k in range(4))
    for o in range(4):
        for copy in first[o]:
            copy.wait()
        u = uin[:, columns(o)]
        dy2 = reverse_norm(
            u, y2in[:, columns(o)], mask, c1, i1, norm_ref[0, 1:2, :], scale1, shift_total, positions
        )
        db[:, columns(o)] = dy2.astype(bf16)
        move.store(db.at[:, columns(o)], dy2_ref.at[:, columns(o)])
        dys = reverse_norm(
            u, ysin[:, columns(o)], mask, c2, i2, norm_ref[0, 2:3, :], scale2, shift_total, positions
        )
        dsb[:, columns(o)] = dys.astype(bf16)
        move.store(dsb.at[:, columns(o)], dys_ref.at[:, columns(o)])
    lw.wait()
    ly1.wait()
    centre, inverse = base_ref[0:1, :], base_ref[1:2, :]
    gain, shift = norm_ref[0, 0:1, :], norm_ref[1, 0:1, :]
    sums = [0.0, 0.0]
    for i in range(4):
        grad = backward_taps(db, wb, i)
        xhat = (y1in[:, columns(i)] - centre) * inverse
        v = xhat * gain + shift
        s = sigmoid(v)
        u = grad * (s * (1.0 + v * (1.0 - s)))
        ub[:, columns(i)] = u
        move.store(ub.at[:, columns(i)], u0_ref.at[:, columns(i)])
        valid = u * mask
        sums[0] += column_sum(valid * xhat)
        sums[1] += column_sum(valid)
    spread(st_ref, pack(sums))
    move.finish()


def k_back_first(
    u0_ref, y1_ref, recv_ref, norm_ref, base_ref, count_ref, dy_ref, tot_ref, uin, yin, db, sems
):
    move = Mover(sems)
    lu, ly = [], []
    for o in range(4):
        lu.append(move.load(u0_ref.at[:, columns(o)], uin.at[:, columns(o)]))
        ly.append(move.load(y1_ref.at[:, columns(o)], yin.at[:, columns(o)]))
    got = jnp.sum(recv_ref[...], axis=0)
    tot_ref[...] = got
    positions = base_ref[2:3, :]
    mask = mask_of(count_ref)
    scale_total, shift_total = channel_row(got, 0), channel_row(got, 1)
    for o in range(4):
        lu[o].wait()
        ly[o].wait()
        dy = reverse_norm(
            uin[:, columns(o)], yin[:, columns(o)], mask, base_ref[0:1, :], base_ref[1:2, :],
            norm_ref[0, 0:1, :], scale_total, shift_total, positions,
        )
        db[:, columns(o)] = dy.astype(bf16)
        move.store(db.at[:, columns(o)], dy_ref.at[:, columns(o)])
    move.finish()


def k_turn(x_ref, side_ref, mine_ref, theirs_ref, xb, at, tb, sems):
    move = Mover(sems)
    loads = [
        move.load(x_ref.at[:, columns(o)], xb.at[:, columns(o)]) for o in range(16 * CIN // COUT)
    ]
    for cell in range(16):
        if cell % 2 == 0:
            loads[cell // 2].wait()
        split_turn(at, tb, xb[:, pl.ds(cell * CIN, CIN)], cell, CIN)
    hand_out(move, at, side_ref, mine_ref, theirs_ref)
    move.finish()


def pair_taps(lefts, rights, gb, base, half, side_in, stride):
    for tap in range(9):
        total = None
        for o in range(4):
            row_in = stride * (o // 2) + tap // 3 - 1
            col_in = stride * (o % 2) + tap % 3 - 1
            if not (0 <= row_in < side_in and 0 <= col_in < side_in):
                continue
            cell = row_in * side_in + col_in
            for left, right in zip(lefts, rights):
                part = dot(left[pl.ds(cell * half, half), :], right[:, columns(o)])
                total = part if total is None else total + part
        gb[pl.ds(base + tap * half, half), :] = total.astype(bf16)


def hand_halves(move, gb, place_ref, outs):
    left_keep, left_send, right_keep, right_send = outs
    x, y = place_ref[0, 1], place_ref[0, 2]
    half = COUT // 2
    for z in range(gb.shape[0] // 4):
        for other in range(2):
            at_left, at_right = (z * 2 + other) * 2, z * 4 + other
            left, right = pl.ds(0, half), pl.ds(half, half)
            move.store(gb.at[at_left + x, :, left], left_keep.at[z, other])
            move.store(gb.at[at_left + 1 - x, :, left], left_send.at[z, other])
            move.store(gb.at[at_right + 2 * y, :, right], right_keep.at[z, other])
            move.store(gb.at[at_right + 2 * (1 - y), :, right], right_send.at[z, other])


def load_all(move, pairs):
    loads = [move.load(src, dst) for src, dst in pairs]
    for copy in loads:
        copy.wait()


def k_pair_grad(mine_ref, got_ref, dy_ref, dyg_ref, place_ref, *refs):
    *outs, mb, ob, db, dgb, gb, sems = refs
    move = Mover(sems)
    load_all(move, ((mine_ref, mb), (dy_ref, db), (got_ref, ob), (dyg_ref, dgb)))
    rows = gb.reshape(9 * COUT // 2, COUT)
    pair_taps((mb, ob), (db, dgb), rows, 0, COUT // 2, 2, 1)
    if len(outs) == 1:
        move.store(rows, outs[0])
    else:
        hand_halves(move, gb, place_ref, outs)
    move.finish()


def k_pair_second(
    mine_ref, got_ref, dy_ref, dyg_ref, xm_ref, xg_ref, dys_ref, dysg_ref, grads_ref,
    mb, ob, db, dgb, gb, xmb, xgb, dsb, dsgb, sems,
):
    move = Mover(sems)
    half = CIN // 2
    later = [move.load(dys_ref, dsb), move.load(dysg_ref, dsgb)]
    for o in range(4):
        cell = (o // 2) * 8 + (o % 2) * 2
        for src, dst in ((xm_ref, xmb), (xg_ref, xgb)):
            later.append(move.load(src.at[pl.ds(cell * half, half)], dst.at[pl.ds(o * half, half)]))
    load_all(move, ((mine_ref, mb), (dy_ref, db), (got_ref, ob), (dyg_ref, dgb)))
    pair_taps((mb, ob), (db, dgb), gb, half, COUT // 2, 2, 1)
    for copy in later:
        copy.wait()
    total = None
    for o in range(4):
        for left, right in ((xmb, dsb), (xgb, dsgb)):
            part = dot(left[pl.ds(o * half, half), :], right[:, columns(o)])
            total = part if total is None else total + part
    gb[pl.ds(0, half), :] = total.astype(bf16)
    move.store(gb, grads_ref)
    move.finish()


def k_pair_first(xm_ref, xg_ref, dy_ref, dyg_ref, late_ref, place_ref, *refs):
    *outs, mb, ob, db, dgb, gb, sems = refs
    move = Mover(sems)
    half = CIN // 2
    rows = gb.reshape(gb.shape[0] * gb.shape[1], COUT)
    late = move.load(late_ref, rows.at[pl.ds(9 * half, late_ref.shape[0])])
    load_all(move, ((xm_ref, mb), (dy_ref, db), (xg_ref, ob), (dyg_ref, dgb)))
    pair_taps((mb, ob), (db, dgb), rows, 0, half, 4, 2)
    late.wait()
    if len(outs) == 1:
        move.store(rows, outs[0])
    else:
        hand_halves(move, gb, place_ref, outs)
    move.finish()


def plus(left, right):
    return (left.astype(f32) + right.astype(f32)).astype(bf16)


def k_merge(lk_ref, lg_ref, rk_ref, rg_ref, place_ref, lk2_ref, ls2_ref, rk2_ref, rs2_ref):
    x, y = place_ref[0, 1], place_ref[0, 2]
    for z in range(lk_ref.shape[0]):
        lk2_ref[z] = plus(lk_ref[z, y], lg_ref[z, y])
        ls2_ref[z] = plus(lk_ref[z, 1 - y], lg_ref[z, 1 - y])
        rk2_ref[z] = plus(rk_ref[z, x], rg_ref[z, x])
        rs2_ref[z] = plus(rk_ref[z, 1 - x], rg_ref[z, 1 - x])


def k_line(*refs):
    *parts, place_ref, own_ref, s1_ref, s2_ref, s3_ref, held = refs
    z_here = place_ref[0, 3]
    half = COUT // 2
    at = 0
    for k in range(0, len(parts), 4):
        lk_ref, lg_ref, rk_ref, rg_ref = parts[k : k + 4]
        for z in range(lk_ref.shape[0]):
            held[at, :, 0:half] = plus(lk_ref[z], lg_ref[z])
            held[at, :, half:COUT] = plus(rk_ref[z], rg_ref[z])
            at += 1
    own_ref[...] = held[z_here]
    for other, ref in ((1, s1_ref), (2, s2_ref), (3, s3_ref)):
        ref[...] = held[jnp.bitwise_xor(z_here, other)]


def k_side(own_ref, g1_ref, g2_ref, g3_ref, place_ref, keep_ref, send_ref):
    side = place_ref[0, 0]

    def total(at):
        return (own_ref[at].astype(f32) + g1_ref[at].astype(f32)) + (
            g2_ref[at].astype(f32) + g3_ref[at].astype(f32)
        )

    keep_ref[...] = total(side)
    send_ref[...] = total(1 - side).astype(bf16)


def make_update(rate):
    def body(
        keep_ref, got_ref, place_ref, master_ref, momentum_ref, average_ref,
        moment_ref, weight_ref, mean_ref, copy_ref,
    ):
        lower = place_ref[0, 0] == 0
        for group in range(keep_ref.shape[0] // 16):
            here = keep_ref[pl.ds(16 * group, 16), :]
            there = got_ref[pl.ds(16 * group, 16), :].astype(f32)
            for parity in range(2):
                at = pl.ds(32 * group + 16 * parity, 16)
                grad = jnp.where(lower, here, there) if parity == 0 else jnp.where(lower, there, here)
                moment, fresh, mean = nesterov(
                    grad, master_ref[at, :], momentum_ref[at, :], average_ref[at, :], rate
                )
                moment_ref[at, :] = moment
                weight_ref[at, :] = fresh
                mean_ref[at, :] = mean
                copy_ref[at, :] = fresh.astype(bf16)

    return body


def k_stack(s0_ref, s1_ref, s2_ref, s3_ref, here_ref):
    for z, ref in enumerate((s0_ref, s1_ref, s2_ref, s3_ref)):
        here_ref[z] = ref[...]


def k_round(value_ref, out_ref):
    out_ref[...] = value_ref[...].astype(bf16)


def k_input_grad(dy_ref, dys_ref, one_ref, dx_ref, db, dsb, wb, xb, sems):
    move = Mover(sems)
    loads = [
        move.load(one_ref, wb),
        move.load(dy_ref, db),
        move.load(dys_ref, dsb),
    ]
    for copy in loads:
        copy.wait()
    for cell in range(16):
        row_in, col_in = divmod(cell, 4)
        total = None
        for o in range(4):
            row_tap, col_tap = row_in - 2 * (o // 2) + 1, col_in - 2 * (o % 2) + 1
            if not (0 <= row_tap < 3 and 0 <= col_tap < 3):
                continue
            part = dot_nt(db[:, columns(o)], wb[pl.ds((row_tap * 3 + col_tap) * CIN, CIN), :])
            total = part if total is None else total + part
        if row_in % 2 == 0 and col_in % 2 == 0:
            o = (row_in // 2) * 2 + col_in // 2
            total = total + dot_nt(dsb[:, columns(o)], wb[pl.ds(9 * CIN, CIN), :])
        xb[:, pl.ds(cell * CIN, CIN)] = total
        move.store(xb.at[:, pl.ds(cell * CIN, CIN)], dx_ref.at[:, pl.ds(cell * CIN, CIN)])
    move.finish()


def nesterov(grad, master, momentum, average, rate):
    moment = momentum_decay * momentum + grad
    fresh = master - rate * (grad + momentum_decay * moment)
    return (moment, fresh, average_decay * average + (1.0 - average_decay) * fresh)


def exchange(packed):
    return lax.all_to_all(packed, AXES, 0, 0, tiled=True)


def swap(value, devices, bits):
    return lax.ppermute(value, AXES, [(i, i ^ bits) for i in range(devices)])


class Grid:
    def __init__(self, devices, number):
        self.devices = devices
        parts = (number % 2, (number // 2) % 2, (number // 4) % 2, number // 8)
        self.place = jnp.stack(parts).astype(jnp.int32).reshape(1, 4)

    def swap(self, value, bits):
        return swap(value, self.devices, bits)


def gather_pieces(grid, here):
    rows = here.shape[1] // 2
    over_x = grid.swap(here, 2)
    over_y = grid.swap(here, 4)
    upper = grid.swap(over_y[:, :rows], 2)
    lower = grid.swap(over_x[:, rows:], 4)
    own = [here, over_x, over_y, upper, lower]
    return own + [grid.swap(v, 1) for v in own]


def scatter_first(grid, halves):
    left_keep, left_send, right_keep, right_send = halves
    return left_keep, grid.swap(left_send, 2), right_keep, grid.swap(right_send, 4)


def scatter_second(grid, halves):
    left_keep, left_send, right_keep, right_send = halves
    return left_keep, grid.swap(left_send, 4), right_keep, grid.swap(right_send, 2)


def merge(grid, halves, after):
    nz, _, rows, half = halves[0].shape
    return run(
        k_merge,
        (*halves, grid.place),
        [VMEM] * 4 + [SMEM],
        [shape((nz, rows, half), bf16)] * 4,
        [VMEM] * 4,
        [],
        moved=1_000_000,
        name="merge",
        after=after,
    )


def line(grid, parts, after):
    rows = parts[0].shape[1]
    own, s1, s2, s3 = run(
        k_line,
        (*parts, grid.place),
        [VMEM] * len(parts) + [SMEM],
        [shape((rows, COUT), bf16)] * 4,
        [VMEM] * 4,
        [pltpu.VMEM((4, rows, COUT), bf16)],
        moved=1_000_000,
        name="line",
        after=after,
    )
    return own, grid.swap(s1, 8), grid.swap(s2, 16), grid.swap(s3, 24)


def sides(grid, parts, after=()):
    rows = parts[0].shape[0] // 2
    keep, send = run(
        k_side,
        (*(v.reshape(2, rows, COUT) for v in parts), grid.place),
        [VMEM] * 4 + [SMEM],
        [shape((rows, COUT), f32), shape((rows, COUT), bf16)],
        [VMEM] * 2,
        [],
        moved=1_000_000,
        name="sides",
        after=after,
    )
    return keep, grid.swap(send, 1)


def update(grid, parts, states, rate, after=()):
    kept = shape(states[0].shape, f32)
    return run(
        make_update(rate),
        (*parts, grid.place, *states),
        [VMEM, VMEM, SMEM, VMEM, VMEM, VMEM],
        [kept, kept, kept, shape(states[0].shape, bf16)],
        [VMEM] * 4,
        [],
        moved=1_000_000,
        name="update",
        after=after,
    )


def reduce_halves(devices, side, half_grad):
    groups = half_grad.reshape(-1, 16, COUT)
    empty = jnp.zeros_like(groups)
    full = jnp.stack(
        [jnp.where(side == 0, groups, empty), jnp.where(side == 0, empty, groups)], axis=1
    ).reshape(-1, COUT)
    return lax.psum_scatter(full, AXES, scatter_dimension=0, tiled=True).astype(f32)


def make_shards(devices, fast):
    def shards(
        features,
        labels,
        image_counts,
        block_one_master,
        block_one_momentum,
        block_one_average,
        block_two_master,
        block_two_momentum,
        block_two_average,
        norm_params,
        norm_momentum,
        norm_average,
        head_params,
        head_momentum,
        head_average,
    ):
        images_all = CAP * devices
        count = image_counts
        side = (lax.axis_index("pass") % 2).astype(jnp.int32).reshape(1, 1)
        number = lax.axis_index("batch") * lax.axis_size("pass") + lax.axis_index("pass")
        number = number.astype(jnp.int32)
        grid = Grid(devices, number) if fast else None
        number = number.reshape(1, 1)
        place = grid.place if fast else number
        shard = block_one_master.astype(bf16)
        x = features.reshape(CAP, 16 * CIN)

        rows_one, rows_two = devices * shard.shape[0], devices * block_two_master.shape[0]
        wide_f, wide_b = shape((CAP, WIDE), f32), shape((CAP, WIDE), bf16)
        wf, wb16 = pltpu.VMEM((CAP, WIDE), f32), pltpu.VMEM((CAP, WIDE), bf16)
        weight = pltpu.VMEM((9 * COUT, COUT), bf16)
        small = shape((8, COUT), f32)
        packed8, packed16 = shape((8, LANES), f32), shape((16, LANES), f32)
        send8, send16 = shape((devices, 8, LANES), f32), shape((devices, 16, LANES), f32)

        def sems(n):
            return pltpu.SemaphoreType.DMA((n,))

        conv_flops = 2 * 16 * CAP * COUT * COUT
        first_flops = 2 * 29 * CAP * CIN * COUT
        head_rows = head_params[:COUT]
        pad = LANES - 3 * TASKS

        def thrice(v):
            return jnp.concatenate([v, v, v, jnp.zeros((v.shape[0], pad), v.dtype)], axis=1)

        head_wide = thrice(head_rows)
        bias_wide = thrice(head_params[COUT:])
        labels_wide = thrice(labels.astype(f32))
        turned = jnp.pad(head_rows.T, ((0, LANES - TASKS), (0, 0)))
        square = jnp.pad(
            jnp.dot(head_rows.T, head_rows, precision=highest), ((0, 0), (0, LANES - TASKS))
        )

        turned_half = shape((WIDE // 2, CAP), bf16)
        turn_scratch = [pltpu.VMEM((2, WIDE // 2, CAP), bf16), pltpu.VMEM((COUT, CAP), bf16)]

        def sibling(value):
            return swap(value, devices, 1)

        x_mine, x_theirs = run(
            k_turn,
            (x, side),
            [HBM, SMEM],
            [shape((8 * CIN, CAP), bf16)] * 2,
            [HBM, HBM],
            [
                pltpu.VMEM((CAP, 16 * CIN), bf16),
                pltpu.VMEM((2, 8 * CIN, CAP), bf16),
                pltpu.VMEM((COUT, CAP), bf16),
                sems(10),
            ],
            0,
            4_000_000,
            name="turn_features",
        )
        x_got = sibling(x_theirs)
        if fast:
            here = run(
                k_stack,
                (shard, *(grid.swap(shard, 8 * other) for other in (1, 2, 3))),
                [VMEM] * 4,
                shape((4, *shard.shape), bf16),
                VMEM,
                [],
                moved=1_000_000,
                name="stack",
                after=(x_mine,),
            )
            one = gather_pieces(grid, here)
            held = pltpu.VMEM((devices, *shard.shape), bf16)
            shard_two = run(
                k_round,
                (block_two_master,),
                [VMEM],
                shape(block_two_master.shape, bf16),
                VMEM,
                [],
                moved=1_000_000,
                name="round",
                after=(here,),
            )
        else:
            one = [lax.all_gather(shard, AXES, axis=0, tiled=True)]
            held = pltpu.VMEM((devices * shard.shape[0], COUT), bf16)
            shard_two = block_two_master.astype(bf16)
        two = lax.all_gather(shard_two, AXES, axis=0, tiled=True)
        y1, ys, st, local, w_one = run(
            make_first(len(one)),
            (x, *one, number, count),
            [HBM] * (1 + len(one)) + [SMEM, SMEM],
            [wide_f, wide_f, send16, packed8, shape((10 * CIN, COUT), bf16)],
            [HBM, HBM, VMEM, VMEM, HBM],
            [
                pltpu.VMEM((CAP, 16 * CIN), bf16),
                held,
                pltpu.VMEM((2, CAP, WIDE), f32),
                sems(50),
            ],
            first_flops,
            9_000_000,
            name="first_conv",
            after=(x_mine,),
        )
        got = exchange(st)
        a1_mine, a1_theirs, y2, st, keep0, w_second = run(
            make_second(len(one)),
            (*one, number, y1, got, norm_params, local, count, side),
            [HBM] * len(one) + [SMEM, HBM, VMEM, VMEM, VMEM, SMEM, SMEM],
            [turned_half, turned_half, wide_f, send16, small, shape((9 * COUT, COUT), bf16)],
            [HBM, HBM, HBM, VMEM, VMEM, HBM],
            [wf, wb16, *turn_scratch, held, wf, sems(51)],
            conv_flops,
            10_000_000,
            name="second_conv",
        )
        got = exchange(st)
        a1_got = sibling(a1_theirs)
        h1, hb_mine, hb_theirs, y3, st, keep12 = run(
            k_third,
            (y2, ys, got, norm_params, keep0, two, count, side),
            [HBM, HBM, VMEM, VMEM, VMEM, HBM, SMEM, SMEM],
            [wide_f, turned_half, turned_half, wide_f, send8, small],
            [HBM, HBM, HBM, HBM, VMEM, VMEM],
            [wf, wf, wf, wb16, *turn_scratch, weight, wf, sems(19)],
            conv_flops,
            14_000_000,
            name="third_conv",
        )
        got = exchange(st)
        hb_got = sibling(hb_theirs)
        a3_mine, a3_theirs, y4, st, keep3 = run(
            k_fourth,
            (y3, got, norm_params, keep0, two, count, side),
            [HBM, VMEM, VMEM, VMEM, HBM, SMEM, SMEM],
            [turned_half, turned_half, wide_f, send8, small],
            [HBM, HBM, HBM, VMEM, VMEM],
            [wf, wb16, *turn_scratch, weight, wf, sems(11)],
            conv_flops,
            10_000_000,
            name="fourth_conv",
        )
        got = exchange(st)
        a3_got = sibling(a3_theirs)
        wide_lanes = shape((CAP, LANES), f32)
        pooled, resid, slope, st, part, keep4 = run(
            k_heads,
            (y4, h1, got, norm_params, keep0, head_wide, bias_wide, labels_wide, count),
            [HBM, HBM, VMEM, VMEM, VMEM, VMEM, VMEM, VMEM, SMEM],
            [
                shape((CAP, COUT), f32),
                wide_lanes,
                wide_f,
                send16,
                shape((8 * devices, LANES), f32),
                small,
            ],
            [VMEM, VMEM, HBM, VMEM, VMEM, VMEM],
            [wf, wf, wf, sems(12)],
            1_000_000_000,
            7_000_000,
            name="heads",
        )
        got = exchange(st)
        weights, u2, st = run(
            k_weights,
            (
                got, square, resid, turned, keep0, keep4, part.reshape(devices, 8, LANES), y4, slope, count,
            ),
            [VMEM, VMEM, VMEM, VMEM, VMEM, VMEM, VMEM, HBM, HBM, SMEM],
            [packed8, wide_f, send16],
            [VMEM, HBM, VMEM],
            [wf, wf, wf, sems(12)],
            1_000_000_000,
            7_000_000,
            name="task_weights",
        )

        got = exchange(st)
        dy4, u3, st, tot4 = run(
            k_back_fourth,
            (u2, y4, got, norm_params, keep0, keep4, two, y3, keep3, count),
            [HBM, HBM, VMEM, VMEM, VMEM, VMEM, HBM, HBM, VMEM, SMEM],
            [wide_b, wide_f, send16, packed8],
            [HBM, HBM, VMEM, VMEM],
            [wf, wf, wf, wb16, weight, wf, sems(18)],
            conv_flops,
            14_000_000,
            name="fourth_back",
        )
        got = exchange(st)
        half_rows = 9 * COUT // 2
        half_turned = pltpu.VMEM((WIDE // 2, CAP), bf16)
        pair_scratch = [half_turned, half_turned, wb16, wb16]
        part_two, part_one = rows_two // devices, rows_one // devices

        def halves_of(nz, rows):
            if not fast:
                return shape((half_rows, COUT), bf16), HBM
            return [shape((nz, 2, rows, COUT // 2), bf16)] * 4, [HBM] * 4

        def pair_grad(mine, theirs, dy, dy_got, name, after=()):
            outs, out_specs = halves_of(2, part_two)
            blocks = (8, part_two, COUT) if fast else (1, half_rows, COUT)
            return run(
                k_pair_grad,
                (mine, theirs, dy, dy_got, place),
                [HBM] * 4 + [SMEM],
                outs,
                out_specs,
                [*pair_scratch, pltpu.VMEM(blocks, bf16), sems(36)],
                conv_flops,
                6_000_000,
                name=name,
                after=after,
            )

        def ties(value):
            return (value[0],) if fast else (value,)

        grads_four = pair_grad(a3_mine, a3_got, dy4, sibling(dy4), "fourth_weights")
        if fast:
            first_four = scatter_first(grid, grads_four)
        dy3, u1, st, tot3, head_sum = run(
            k_back_third,
            (u3, y3, got, norm_params, keep0, keep3, two, u2, y2, ys, keep12, count),
            [HBM, HBM, VMEM, VMEM, VMEM, VMEM, HBM, HBM, HBM, HBM, VMEM, SMEM],
            [wide_b, wide_f, send16, packed8, send8],
            [HBM, HBM, VMEM, VMEM, VMEM],
            [wf, wf, wf, wf, wf, wb16, weight, wf, sems(20)],
            conv_flops,
            18_000_000,
            name="third_back",
            after=ties(grads_four),
        )
        got = exchange(st)
        grads_three = pair_grad(hb_mine, hb_got, dy3, sibling(dy3), "third_weights")
        if fast:
            first_three = scatter_first(grid, grads_three)
            second_four = merge(grid, first_four, ties(grads_three))
            tie = ties(second_four)
            second_four = scatter_second(grid, second_four)
        else:
            tie = ties(grads_three)
        dy2, dys, u0, st, tot12 = run(
            k_back_second,
            (u1, y2, ys, got, norm_params, keep0, keep12, w_second, y1, count),
            [HBM, HBM, HBM, VMEM, VMEM, VMEM, VMEM, HBM, HBM, SMEM],
            [wide_b, wide_b, wide_f, send8, packed16],
            [HBM, HBM, HBM, VMEM, VMEM],
            [wf, wf, wf, wf, wb16, wb16, weight, wf, sems(26)],
            conv_flops,
            18_000_000,
            name="second_back",
            after=tie,
        )
        got = exchange(st)
        dys_got = sibling(dys)
        grads_late = run(
            k_pair_second,
            (a1_mine, a1_got, dy2, sibling(dy2), x_mine, x_got, dys, dys_got),
            [HBM] * 8,
            shape((half_rows + CIN // 2, COUT), bf16),
            HBM,
            [
                *pair_scratch,
                pltpu.VMEM((half_rows + CIN // 2, COUT), bf16),
                pltpu.VMEM((2 * CIN, CAP), bf16),
                pltpu.VMEM((2 * CIN, CAP), bf16),
                wb16,
                wb16,
                sems(15),
            ],
            conv_flops,
            9_000_000,
            name="second_weights",
        )
        tie = (grads_late,)
        if fast:
            second_three = merge(grid, first_three, tie)
            tie = ties(second_three)
            second_three = scatter_second(grid, second_three)
        dy1, tot0 = run(
            k_back_first,
            (u0, y1, got, norm_params, keep0, count),
            [HBM, HBM, VMEM, VMEM, VMEM, SMEM],
            [wide_b, packed8],
            [HBM, VMEM],
            [wf, wf, wb16, sems(12)],
            0,
            5_000_000,
            name="first_back",
            after=tie,
        )
        dy1_got = sibling(dy1)
        tie = ()
        if fast:
            third_two = line(grid, (*second_three, *second_four), (dy1,))
            tie = ties(third_two)
        half_features = pltpu.VMEM((8 * CIN, CAP), bf16)
        if fast:
            outs, out_specs = [shape((4, 2, part_one, COUT // 2), bf16)] * 4, [HBM] * 4
        else:
            outs, out_specs = shape((rows_one // 2, COUT), bf16), HBM
        blocks = (16, part_one, COUT) if fast else (1, rows_one // 2, COUT)
        grads_one = run(
            k_pair_first,
            (x_mine, x_got, dy1, dy1_got, grads_late, place),
            [HBM] * 5 + [SMEM],
            outs,
            out_specs,
            [half_features, half_features, wb16, wb16, pltpu.VMEM(blocks, bf16), sems(40)],
            first_flops,
            8_000_000,
            name="first_weights",
            after=tie,
        )
        def back_to_features():
            dx = run(
                k_input_grad,
                (dy1, dys, w_one),
                [HBM, HBM, HBM],
                shape((CAP, 16 * CIN), f32),
                HBM,
                [
                    wb16,
                    wb16,
                    pltpu.VMEM((10 * CIN, COUT), bf16),
                    pltpu.VMEM((CAP, 16 * CIN), f32),
                    sems(19),
                ],
                first_flops,
                9_000_000,
                name="input_grad",
            )
            return dx, dx.reshape(CAP, 4, 4, CIN)

        states_one = (block_one_master, block_one_momentum, block_one_average)
        states_two = (block_two_master, block_two_momentum, block_two_average)
        rate = rate_conv * math.sqrt(images_all)
        if fast:
            first_one = scatter_first(grid, grads_one)
            fourth_two = sides(grid, third_two, ties(grads_one))
            dx, input_grad = back_to_features()
            second_one = merge(grid, first_one, (dx,))
            second_one = scatter_second(grid, second_one)
            third_one = line(grid, second_one, (input_grad,))
            two_m, two_w, two_a, two_c = update(grid, fourth_two, states_two, rate)
            fourth_one = sides(grid, third_one, (two_m,))
            one_m, one_w, one_a, one_c = update(grid, fourth_one, states_one, rate)
        else:
            two_sum = reduce_halves(
                devices, side[0, 0], jnp.concatenate([grads_three, grads_four], axis=0)
            )
            one_sum = reduce_halves(devices, side[0, 0], grads_one)
            one_m, one_w, one_a = nesterov(one_sum, *states_one, rate)
            two_m, two_w, two_a = nesterov(two_sum, *states_two, rate)
            one_c, two_c = one_w.astype(bf16), two_w.astype(bf16)
            _, input_grad = back_to_features()
        def unpacked(packed):
            return packed.reshape(-1, COUT)

        t0, t3, t4, t12 = unpacked(tot0), unpacked(tot3), unpacked(tot4), unpacked(tot12)
        norm_grad = jnp.stack(
            [
                jnp.stack([t0[0], t12[0], t12[1], t3[0], t4[0]]),
                jnp.stack([t0[1], t12[2], t12[2], t3[1], t4[1]]),
            ]
        )
        total = keep0[2, 0] * 0.25
        head_sum = head_sum.reshape(-1, LANES)[: 5 * TASKS].reshape(5, TASKS, LANES)
        task_losses = head_sum[4, :, 1] / total
        head_grad = jnp.concatenate(
            [head_sum[:4].transpose(0, 2, 1).reshape(COUT, TASKS), head_sum[4, :, 0][None]], axis=0
        ) / total
        scale_rate = math.sqrt(images_all)
        norm_m, norm_w, norm_a = nesterov(
            norm_grad, norm_params, norm_momentum, norm_average, rate_norm * scale_rate
        )
        head_m, head_w, head_a = nesterov(
            head_grad, head_params, head_momentum, head_average, rate_head * scale_rate
        )
        return (
            pooled,
            input_grad,
            task_losses,
            weights[0, :TASKS],
            one_m,
            one_w,
            one_a,
            one_c,
            two_m,
            two_w,
            two_a,
            two_c,
            norm_m,
            norm_w,
            norm_a,
            head_m,
            head_w,
            head_a,
        )

    return shards


def solution(mesh):
    devices = mesh.shape["batch"] * mesh.shape["pass"]
    fast = mesh.shape["batch"] == 8 and mesh.shape["pass"] == 4
    rows = P(AXES, None)
    in_specs = (
        P(AXES, None, None, None),
        rows,
        P("batch", "pass"),
        rows,
        rows,
        rows,
        rows,
        rows,
        rows,
        P(),
        P(),
        P(),
        P(),
        P(),
        P(),
    )
    out_specs = (
        rows,
        P(AXES, None, None, None),
        P(),
        P(),
        rows,
        rows,
        rows,
        rows,
        rows,
        rows,
        rows,
        rows,
        P(),
        P(),
        P(),
        P(),
        P(),
        P(),
    )
    return jax.shard_map(
        make_shards(devices, fast), mesh=mesh, in_specs=in_specs, out_specs=out_specs, check_vma=False
    )
```

```python
import math

import jax
import jax.numpy as jnp
from jax import lax
from jax.experimental import pallas as pl
from jax.experimental.pallas import tpu as pltpu
from jax.sharding import PartitionSpec as P

CIN = 256
COUT = 512
TASKS = 40
FW_STEPS = 20
CAP = 256
WIDE = 4 * COUT
LANES = 128
AXES = ("batch", "pass")

epsilon = 1e-05
softness = 0.01
momentum_decay = 0.9
average_decay = 0.9
rate_conv = 3.0
rate_norm = 50.0
rate_head = 0.05
highest = lax.Precision.HIGHEST

HBM = pl.BlockSpec(memory_space=pltpu.HBM)
VMEM = pl.BlockSpec(memory_space=pltpu.VMEM)
SMEM = pl.BlockSpec(memory_space=pltpu.SMEM)
f32 = jnp.float32
bf16 = jnp.bfloat16


def shape(extent, kind):
    return jax.ShapeDtypeStruct(extent, kind)


def run(
    body, args, in_specs, outs, out_specs, scratch, flops=0, moved=0, aliases=None, name=None, after=(), through=None,
    share=1,
):
    first, last = len(args), len(args) + len(after)
    args, in_specs = (*args, *after), [*in_specs, *[HBM] * len(after)]
    aliases = dict(aliases or {})
    if through is not None:
        outs, out_specs = [*outs, shape(through.shape, through.dtype)], [*out_specs, HBM]
        aliases[len(args)] = len(outs) - 1
        args, in_specs = (*args, through), [*in_specs, HBM]
    count, results = len(args), len(outs) if isinstance(outs, list) else 1

    def plain(*refs):
        made = refs[count : count + results - (through is not None)]
        body(*refs[:first], *made, *refs[count + results :])

    return pl.pallas_call(
        plain if count > first else body,
        out_shape=outs,
        in_specs=in_specs,
        out_specs=out_specs,
        scratch_shapes=scratch,
        input_output_aliases=aliases,
        compiler_params=pltpu.CompilerParams(vmem_limit_bytes=67_000_000),
        cost_estimate=pl.CostEstimate(
            flops=flops // share, bytes_accessed=moved // share, transcendentals=0
        ),
        name=name,
    )(*args)


class Mover:
    def __init__(self, sems):
        self.sems = sems
        self.used = 0
        self.out = []

    def load(self, src, dst):
        copy = pltpu.make_async_copy(src, dst, self.sems.at[self.used])
        self.used += 1
        copy.start()
        return copy

    def store(self, src, dst):
        self.out.append(self.load(src, dst))

    def finish(self):
        for copy in self.out:
            copy.wait()


def columns(o):
    return pl.ds(o * COUT, COUT)


def split_turn(at, tb, value, place, channels):
    half = channels // 2
    tb[pl.ds(0, channels), :] = value.T
    for group in range(half // 16):
        for parity in range(2):
            at[parity, pl.ds(place * half + 16 * group, 16), :] = tb[
                pl.ds(32 * group + 16 * parity, 16), :
            ]


def hand_out(move, at, side_ref, mine_ref, theirs_ref):
    side = side_ref[0, 0]
    move.store(at.at[side], mine_ref)
    move.store(at.at[1 - side], theirs_ref)


def dot(left, right, precision=None):
    return jnp.dot(left, right, preferred_element_type=f32, precision=precision)


def dot_nt(left, right):
    return lax.dot_general(left, right, (((1,), (1,)), ((), ())), preferred_element_type=f32)


def dot_tn(left, right, precision=None):
    return lax.dot_general(
        left, right, (((0,), (0,)), ((), ())), preferred_element_type=f32, precision=precision
    )


def sigmoid(v):
    return 0.5 * jnp.tanh(0.5 * v) + 0.5


def channel_row(packed, k):
    return jnp.concatenate([packed[4 * k + b : 4 * k + b + 1, :] for b in range(4)], axis=1)


def pack(rows):
    pieces = [row[:, b * LANES : (b + 1) * LANES] for row in rows for b in range(4)]
    while len(pieces) % 8:
        pieces.append(jnp.zeros((1, LANES), f32))
    return jnp.concatenate(pieces, axis=0)


def spread(out_ref, packed):
    out_ref[...] = jnp.broadcast_to(packed[None], out_ref.shape)


def mask_of(count_ref):
    rows = lax.broadcasted_iota(jnp.int32, (CAP, COUT), 0)
    return (rows < count_ref[0, 0]).astype(f32)


def column_sum(v):
    return jnp.sum(v, axis=0, keepdims=True)


def moments(total_sum, total_square, positions):
    centre = total_sum / positions
    spread_value = total_square / positions - centre * centre
    return centre, lax.rsqrt(spread_value + epsilon)


class Taps:
    def __init__(self, move, src, base, buf, order):
        self.buf = buf
        self.copies = {
            tap: move.load(
                src.at[pl.ds(base + tap * COUT, COUT)], buf.at[pl.ds(tap * COUT, COUT)]
            )
            for tap in order
        }

    def rows(self, first, count=1):
        for tap in range(first, first + count):
            copy = self.copies.pop(tap, None)
            if copy is not None:
                copy.wait()
        return self.buf[pl.ds(first * COUT, count * COUT), :]


FORWARD = (4, 5, 7, 8, 3, 6, 1, 2, 0)
BACKWARD = (4, 3, 1, 0, 5, 2, 7, 6, 8)


def forward_taps(act_ref, w_ref, o):
    row_out, col_out = divmod(o, 2)
    total = None
    for row_in in range(2):
        tap = (row_in - row_out + 1) * 3 + (1 - col_out)
        weights = w_ref.rows(tap, 2) if isinstance(w_ref, Taps) else w_ref[pl.ds(tap * COUT, 2 * COUT), :]
        part = dot(act_ref[:, pl.ds(row_in * 2 * COUT, 2 * COUT)], weights)
        total = part if total is None else total + part
    return total


def tap_of(i, o):
    return (i // 2 - o // 2 + 1) * 3 + (i % 2 - o % 2 + 1)


def backward_taps(dy_ref, w_ref, i):
    total = None
    for o in range(4):
        part = dot_nt(dy_ref[:, columns(o)], w_ref.rows(tap_of(i, o)))
        total = part if total is None else total + part
    return total


def first_pairs(o):
    row_out, col_out = divmod(o, 2)
    runs = []
    for row_tap in range(3):
        row_in = 2 * row_out + row_tap - 1
        if 0 <= row_in < 4:
            col_tap = 1 if col_out == 0 else 0
            runs.append((row_in * 4 + 2 * col_out + col_tap - 1, row_tap * 3 + col_tap, 3 - col_tap))
    return runs


def pieces_of(refs, number, groups):
    found = []
    for at, (fixed, zs) in enumerate(groups):
        for side in range(2):
            for k, bits in ((0, 0), (1, 2), (2, 4), (3, 6), (4, 6)):
                ref = refs[10 * at + 5 * side + k]
                for part, z in enumerate(zs):
                    if fixed:
                        owner = 8 * z + jnp.bitwise_xor(jnp.bitwise_and(number, 7), bits + side)
                    else:
                        owner = jnp.bitwise_xor(number, 8 * z + bits + side)
                    found.append((ref.at[part], owner, ref.shape[1] if k == 4 else 0))
    return found


NEAR_FAR = ((False, (0, 1, 2, 3)),)
LOW = ((True, (0, 1)),)
LOW_HIGH = ((True, (0, 1)), (True, (2, 3)))


class Rows:
    def __init__(self, move, refs, number_ref, buf, low, high, groups, first=0):
        self.waits = []
        if len(refs) == 1:
            self.rows = buf
            at = pl.ds(low - first, high - low)
            self.waits.append((None, move.load(refs[0].at[pl.ds(low, high - low)], buf.at[at])))
            return
        per = buf.shape[1]
        number = number_ref[0, 0]
        for src, owner, row in pieces_of(refs, number, groups):
            live = jnp.logical_and(owner >= low // per, owner < -(-high // per))
            at = jnp.where(live, owner - first // per, 0)
            copy = pltpu.make_async_copy(
                src, buf.at[at, pl.ds(row, src.shape[0])], move.sems.at[move.used]
            )
            move.used += 1
            pl.when(live)(copy.start)
            self.waits.append((live, copy))
        self.rows = buf.reshape(buf.shape[0] * per, COUT)

    def wait(self):
        for live, copy in self.waits:
            if live is None:
                copy.wait()
            else:
                pl.when(live)(copy.wait)
        return self.rows


def make_assemble(groups):
    def body(*refs):
        *pieces, number_ref, whole_ref, buf, sems = refs
        move = Mover(sems)
        rows = Rows(move, pieces, number_ref, buf, 0, whole_ref.shape[0], groups).wait()
        move.store(rows, whole_ref)
        move.finish()

    return body


def make_first(sources):
    def body(*refs):
        x_ref, *one_refs = refs[: 1 + sources]
        number_ref, count_ref, y1_ref, ys_ref, st_ref, local_ref, xb, wb, yb, sems = refs[
            1 + sources :
        ]
        move = Mover(sems)
        lx = move.load(x_ref, xb)
        rows = Rows(move, one_refs, number_ref, wb, 0, 10 * CIN, NEAR_FAR)
        mask = mask_of(count_ref)
        lx.wait()
        wr = rows.wait()
        first_body(move, xb, wr, yb, mask, count_ref, y1_ref, ys_ref, st_ref, local_ref)

    return body


def first_body(move, xb, wb, yb, mask, count_ref, y1_ref, ys_ref, st_ref, local_ref):
    sums = [0.0, 0.0, 0.0, 0.0]
    for o in range(4):
        total = None
        for cell, tap, cells in first_pairs(o):
            part = dot(xb[:, pl.ds(cell * CIN, cells * CIN)], wb[pl.ds(tap * CIN, cells * CIN), :])
            total = part if total is None else total + part
        yb[0, :, columns(o)] = total
        move.store(yb.at[0, :, columns(o)], y1_ref.at[:, columns(o)])
        valid = total * mask
        sums[0] += column_sum(valid)
        sums[1] += column_sum(valid * total)
        cell = (o // 2) * 8 + (o % 2) * 2
        total = dot(xb[:, pl.ds(cell * CIN, CIN)], wb[pl.ds(9 * CIN, CIN), :])
        yb[1, :, columns(o)] = total
        move.store(yb.at[1, :, columns(o)], ys_ref.at[:, columns(o)])
        valid = total * mask
        sums[2] += column_sum(valid)
        sums[3] += column_sum(valid * total)
    counted = jnp.full((8, LANES), count_ref[0, 0].astype(f32), f32)
    spread(st_ref, jnp.concatenate([pack(sums[:2]), counted], axis=0))
    local_ref[...] = pack(sums[2:])
    move.finish()


def k_second(
    y1_ref, recv_ref, norm_ref, local_ref, one_ref, count_ref, side_ref,
    mine_ref, theirs_ref, y2_ref, st_ref, keep_ref,
    yin, ab, at, tb, wb, yb, sems,
):
    move = Mover(sems)
    ly = [move.load(y1_ref.at[:, columns(o)], yin.at[:, columns(o)]) for o in range(4)]
    lw = Taps(move, one_ref, 10 * CIN, wb, FORWARD)
    got = jnp.sum(recv_ref[...], axis=0)
    total = got[8:9, 0:1]
    positions = 4.0 * total
    centre, inverse = moments(channel_row(got, 0), channel_row(got, 1), positions)
    keep_ref[...] = jnp.concatenate(
        [centre, inverse, jnp.broadcast_to(positions, (1, COUT)), jnp.zeros((5, COUT), f32)], axis=0
    )
    scale = norm_ref[0, 0:1, :] * inverse
    offset = norm_ref[1, 0:1, :] - centre * scale
    mask = mask_of(count_ref)
    for o in range(4):
        ly[o].wait()
        v = yin[:, columns(o)] * scale + offset
        ab[:, columns(o)] = (v * sigmoid(v)).astype(bf16)
        split_turn(at, tb, ab[:, columns(o)], o, COUT)
    hand_out(move, at, side_ref, mine_ref, theirs_ref)
    sums = [0.0, 0.0]
    for o in range(4):
        y = forward_taps(ab, lw, o)
        yb[:, columns(o)] = y
        move.store(yb.at[:, columns(o)], y2_ref.at[:, columns(o)])
        valid = y * mask
        sums[0] += column_sum(valid)
        sums[1] += column_sum(valid * y)
    spread(st_ref, jnp.concatenate([pack(sums), local_ref[...]], axis=0))
    move.finish()


def make_third(sources):
    def body(*refs):
        third_body(refs[:sources], *refs[sources:])

    return body


def third_body(
    two_refs, number_ref, y2_ref, ys_ref, recv_ref, norm_ref, base_ref, count_ref, side_ref,
    h1_ref, mine_ref, theirs_ref, y3_ref, st_ref, keep_ref,
    yin, sin, hout, ab, at, tb, wb, yb, sems,
):
    move = Mover(sems)
    ly, ls = [], []
    for o in range(4):
        ly.append(move.load(y2_ref.at[:, columns(o)], yin.at[:, columns(o)]))
        ls.append(move.load(ys_ref.at[:, columns(o)], sin.at[:, columns(o)]))
    rows = Rows(move, two_refs, number_ref, wb, 0, 9 * COUT, LOW)
    got = jnp.sum(recv_ref[...], axis=0)
    positions = base_ref[2:3, :]
    c1, i1 = moments(channel_row(got, 0), channel_row(got, 1), positions)
    c2, i2 = moments(channel_row(got, 2), channel_row(got, 3), positions)
    keep_ref[...] = jnp.concatenate([c1, i1, c2, i2, jnp.zeros((4, COUT), f32)], axis=0)
    s1 = norm_ref[0, 1:2, :] * i1
    s2 = norm_ref[0, 2:3, :] * i2
    offset = norm_ref[1, 1:2, :] - c1 * s1 + (norm_ref[1, 2:3, :] - c2 * s2)
    mask = mask_of(count_ref)
    for o in range(4):
        ly[o].wait()
        ls[o].wait()
        v = yin[:, columns(o)] * s1 + sin[:, columns(o)] * s2 + offset
        h = v * sigmoid(v)
        hout[:, columns(o)] = h
        ab[:, columns(o)] = h.astype(bf16)
        move.store(hout.at[:, columns(o)], h1_ref.at[:, columns(o)])
        split_turn(at, tb, ab[:, columns(o)], o, COUT)
    hand_out(move, at, side_ref, mine_ref, theirs_ref)
    wr = rows.wait()
    sums = [0.0, 0.0]
    for o in range(4):
        y = forward_taps(ab, wr, o)
        yb[:, columns(o)] = y
        move.store(yb.at[:, columns(o)], y3_ref.at[:, columns(o)])
        valid = y * mask
        sums[0] += column_sum(valid)
        sums[1] += column_sum(valid * y)
    spread(st_ref, pack(sums))
    move.finish()


def k_fourth(
    y3_ref, recv_ref, norm_ref, base_ref, two_ref, count_ref, side_ref,
    mine_ref, theirs_ref, y4_ref, st_ref, keep_ref,
    yin, ab, at, tb, wb, yb, sems,
):
    move = Mover(sems)
    ly = [move.load(y3_ref.at[:, columns(o)], yin.at[:, columns(o)]) for o in range(4)]
    lw = Taps(move, two_ref, 9 * COUT, wb, FORWARD)
    got = jnp.sum(recv_ref[...], axis=0)
    centre, inverse = moments(channel_row(got, 0), channel_row(got, 1), base_ref[2:3, :])
    keep_ref[...] = jnp.concatenate([centre, inverse, jnp.zeros((6, COUT), f32)], axis=0)
    scale = norm_ref[0, 3:4, :] * inverse
    offset = norm_ref[1, 3:4, :] - centre * scale
    mask = mask_of(count_ref)
    for o in range(4):
        ly[o].wait()
        v = yin[:, columns(o)] * scale + offset
        ab[:, columns(o)] = (v * sigmoid(v)).astype(bf16)
        split_turn(at, tb, ab[:, columns(o)], o, COUT)
    hand_out(move, at, side_ref, mine_ref, theirs_ref)
    sums = [0.0, 0.0]
    for o in range(4):
        y = forward_taps(ab, lw, o)
        yb[:, columns(o)] = y
        move.store(yb.at[:, columns(o)], y4_ref.at[:, columns(o)])
        valid = y * mask
        sums[0] += column_sum(valid)
        sums[1] += column_sum(valid * y)
    spread(st_ref, pack(sums))
    move.finish()


def k_heads(
    y4_ref, h1_ref, recv_ref, norm_ref, base_ref, head_ref, bias_ref, labels_ref, count_ref,
    pooled_ref, resid_ref, slope_ref, gram_ref, part_ref, keep_ref,
    yin, hin, sb, sems,
):
    move = Mover(sems)
    ly, lh = [], []
    for o in range(4):
        ly.append(move.load(y4_ref.at[:, columns(o)], yin.at[:, columns(o)]))
        lh.append(move.load(h1_ref.at[:, columns(o)], hin.at[:, columns(o)]))
    got = jnp.sum(recv_ref[...], axis=0)
    centre, inverse = moments(channel_row(got, 0), channel_row(got, 1), base_ref[2:3, :])
    keep_ref[...] = jnp.concatenate([centre, inverse, jnp.zeros((6, COUT), f32)], axis=0)
    scale = norm_ref[0, 4:5, :] * inverse
    offset = norm_ref[1, 4:5, :] - centre * scale
    total = None
    for o in range(4):
        ly[o].wait()
        lh[o].wait()
        v = yin[:, columns(o)] * scale + offset + hin[:, columns(o)]
        s = sigmoid(v)
        h = v * s
        sb[:, columns(o)] = s * (1.0 + v - h)
        move.store(sb.at[:, columns(o)], slope_ref.at[:, columns(o)])
        total = h if total is None else total + h
    pooled = total * 0.25
    pooled_ref[...] = pooled
    logits = dot(pooled, head_ref[...], highest) + bias_ref[...]
    labels = labels_ref[...]
    valid = (lax.broadcasted_iota(jnp.int32, (CAP, LANES), 0) < count_ref[0, 0]).astype(f32)
    resid = (sigmoid(logits) - labels) * valid
    resid_ref[...] = resid
    softplus = jnp.maximum(logits, 0.0) + jnp.log1p(jnp.exp(-jnp.abs(logits)))
    losses = valid * (softplus - labels * logits)
    gram = dot_tn(resid, resid, highest)
    lane = lax.broadcasted_iota(jnp.int32, (16, LANES), 1)
    packed = jnp.where(lane < TASKS, gram[0:16], jnp.where(lane < 2 * TASKS, gram[16:32], gram[32:48]))
    spread(gram_ref, packed)
    part_ref[...] = jnp.zeros(part_ref.shape, f32)
    for b in range(4):
        part_ref[pl.ds(b * TASKS, TASKS), :] = dot_tn(
            resid, pooled[:, b * LANES : (b + 1) * LANES], highest
        )[0:TASKS]
    ones = jnp.ones((CAP, LANES), f32)
    lane = lax.broadcasted_iota(jnp.int32, (TASKS, LANES), 1)
    part_ref[pl.ds(4 * TASKS, TASKS), :] = jnp.where(
        lane == 0, dot_tn(resid, ones, highest)[0:TASKS], dot_tn(losses, ones, highest)[0:TASKS]
    )
    move.finish()


def k_weights(
    recv_ref, square_ref, resid_ref, turned_ref, base_ref, keep_ref, part_ref, y4_ref, slope_ref, count_ref,
    weights_ref, u2_ref, st_ref,
    yin, sin, ub, sems,
):
    move = Mover(sems)
    ly, ls = [], []
    for o in range(4):
        ly.append(move.load(y4_ref.at[:, columns(o)], yin.at[:, columns(o)]))
        ls.append(move.load(slope_ref.at[:, columns(o)], sin.at[:, columns(o)]))
    total = base_ref[2:3, 0:1] * 0.25
    got = jnp.sum(recv_ref[...], axis=0)
    gram = jnp.concatenate(
        [
            got,
            pltpu.roll(got, LANES - TASKS, 1),
            pltpu.roll(got, LANES - 2 * TASKS, 1)[0:8],
        ],
        axis=0,
    )
    row_at = lax.broadcasted_iota(jnp.int32, (TASKS, LANES), 0)
    lane_at = lax.broadcasted_iota(jnp.int32, (TASKS, LANES), 1)
    gram = jnp.where(lane_at < TASKS, gram * square_ref[...], 0.0) / total
    trace = jnp.sum(
        jnp.sum(jnp.where(row_at == lane_at, gram, 0.0), axis=0, keepdims=True), axis=1, keepdims=True
    )
    scaled = gram / (trace / TASKS + 1e-06)
    live = lax.broadcasted_iota(jnp.int32, (1, LANES), 1) < TASKS
    weights = jnp.where(live, 1.0 / TASKS, 0.0)
    row = jnp.sum(scaled, axis=0, keepdims=True) / TASKS
    col = jnp.sum(scaled, axis=1, keepdims=True) / TASKS
    for turn in range(FW_STEPS):
        gamma = 2.0 / (turn + 3.0)
        low = jnp.min(col, axis=0, keepdims=True)
        grown_col = jnp.exp((low - col) / softness)
        grown_row = jnp.where(live, jnp.exp(jnp.where(live, (low - row) / softness, 0.0)), 0.0)
        share = gamma / jnp.sum(grown_col, axis=0, keepdims=True)
        weights = (1.0 - gamma) * weights + share * grown_row
        if turn + 1 < FW_STEPS:
            next_row = jnp.sum(scaled * grown_col, axis=0, keepdims=True)
            next_col = jnp.sum(scaled * grown_row, axis=1, keepdims=True)
            row = (1.0 - gamma) * row + share * next_row
            col = (1.0 - gamma) * col + share * next_col
    weights_ref[...] = jnp.broadcast_to(weights, (8, LANES))
    pooled_grad = dot(resid_ref[...] * (weights / total), turned_ref[...], highest) * 0.25
    centre, inverse = keep_ref[0:1, :], keep_ref[1:2, :]
    mask = mask_of(count_ref)
    sums = [0.0, 0.0]
    for o in range(4):
        ly[o].wait()
        ls[o].wait()
        u = pooled_grad * sin[:, columns(o)]
        ub[:, columns(o)] = u
        move.store(ub.at[:, columns(o)], u2_ref.at[:, columns(o)])
        valid = u * mask
        sums[0] += column_sum(valid * ((yin[:, columns(o)] - centre) * inverse))
        sums[1] += column_sum(valid)
    st_ref[:, 0:8, :] = jnp.broadcast_to(pack(sums)[None], part_ref.shape)
    st_ref[:, 8:16, :] = part_ref[...]
    move.finish()


def reverse_norm(g, y, mask, centre, inverse, gain, scale_total, shift_total, positions):
    xhat = (y - centre) * inverse
    return (gain * inverse) * (g - mask * ((shift_total + xhat * scale_total) / positions))


def k_back_fourth(
    u2_ref, y4_ref, recv_ref, norm_ref, base_ref, keep4_ref, two_ref, y3_ref, keep3_ref, count_ref,
    dy0_ref, dy1_ref, dy2_ref, dy3_ref, u3_ref, st_ref, tot_ref,
    uin, yin, zin, db, wb, ub, sems,
):
    move = Mover(sems)
    lu, ly = [], []
    for o in range(4):
        lu.append(move.load(u2_ref.at[:, columns(o)], uin.at[:, columns(o)]))
        ly.append(move.load(y4_ref.at[:, columns(o)], yin.at[:, columns(o)]))
    lw = Taps(move, two_ref, 9 * COUT, wb, BACKWARD)
    lz = [move.load(y3_ref.at[:, columns(i)], zin.at[:, columns(i)]) for i in range(4)]
    got = jnp.sum(recv_ref[...], axis=0)
    tot_ref[...] = got[0:8]
    positions = base_ref[2:3, :]
    mask = mask_of(count_ref)
    scale_total, shift_total = channel_row(got, 0), channel_row(got, 1)
    for o in range(4):
        lu[o].wait()
        ly[o].wait()
        dy = reverse_norm(
            uin[:, columns(o)], yin[:, columns(o)], mask, keep4_ref[0:1, :], keep4_ref[1:2, :],
            norm_ref[0, 4:5, :], scale_total, shift_total, positions,
        )
        db[:, columns(o)] = dy.astype(bf16)
        move.store(db.at[:, columns(o)], (dy0_ref, dy1_ref, dy2_ref, dy3_ref)[o])
    centre, inverse = keep3_ref[0:1, :], keep3_ref[1:2, :]
    gain, shift = norm_ref[0, 3:4, :], norm_ref[1, 3:4, :]
    sums = [0.0, 0.0]
    for i in range(4):
        grad = backward_taps(db, lw, i)
        lz[i].wait()
        xhat = (zin[:, columns(i)] - centre) * inverse
        v = xhat * gain + shift
        s = sigmoid(v)
        u = grad * (s * (1.0 + v * (1.0 - s)))
        ub[:, columns(i)] = u
        move.store(ub.at[:, columns(i)], u3_ref.at[:, columns(i)])
        valid = u * mask
        sums[0] += column_sum(valid * xhat)
        sums[1] += column_sum(valid)
    spread(st_ref, jnp.concatenate([pack(sums), got[8:16]], axis=0))
    move.finish()


def k_back_third(
    u3_ref, y3_ref, recv_ref, norm_ref, base_ref, keep3_ref, two_ref, u2_ref, y2_ref, ys_ref, keep12_ref, count_ref,
    dy0_ref, dy1_ref, dy2_ref, dy3_ref, u1_ref, st_ref, tot_ref, head_ref,
    uin, yin, u2in, y2in, ysin, db, wb, ub, sems,
):
    move = Mover(sems)
    lu, ly = [], []
    for o in range(4):
        lu.append(move.load(u3_ref.at[:, columns(o)], uin.at[:, columns(o)]))
        ly.append(move.load(y3_ref.at[:, columns(o)], yin.at[:, columns(o)]))
    lw = Taps(move, two_ref, 0, wb, BACKWARD)
    later = [
        [
            move.load(ref.at[:, columns(i)], buf.at[:, columns(i)])
            for ref, buf in ((u2_ref, u2in), (y2_ref, y2in), (ys_ref, ysin))
        ]
        for i in range(4)
    ]
    got = jnp.sum(recv_ref[:, 0:8, :], axis=0)
    tot_ref[...] = got
    head_ref[...] = recv_ref[:, 8:16, :]
    positions = base_ref[2:3, :]
    mask = mask_of(count_ref)
    scale_total, shift_total = channel_row(got, 0), channel_row(got, 1)
    for o in range(4):
        lu[o].wait()
        ly[o].wait()
        dy = reverse_norm(
            uin[:, columns(o)], yin[:, columns(o)], mask, keep3_ref[0:1, :], keep3_ref[1:2, :],
            norm_ref[0, 3:4, :], scale_total, shift_total, positions,
        )
        db[:, columns(o)] = dy.astype(bf16)
        move.store(db.at[:, columns(o)], (dy0_ref, dy1_ref, dy2_ref, dy3_ref)[o])
    c1, i1, c2, i2 = (keep12_ref[k : k + 1, :] for k in range(4))
    g1, g2 = norm_ref[0, 1:2, :], norm_ref[0, 2:3, :]
    shift = norm_ref[1, 1:2, :] + norm_ref[1, 2:3, :]
    sums = [0.0, 0.0, 0.0]
    for i in range(4):
        grad = backward_taps(db, lw, i)
        for copy in later[i]:
            copy.wait()
        grad = grad + u2in[:, columns(i)]
        x1 = (y2in[:, columns(i)] - c1) * i1
        x2 = (ysin[:, columns(i)] - c2) * i2
        v = x1 * g1 + x2 * g2 + shift
        s = sigmoid(v)
        u = grad * (s * (1.0 + v * (1.0 - s)))
        ub[:, columns(i)] = u
        move.store(ub.at[:, columns(i)], u1_ref.at[:, columns(i)])
        valid = u * mask
        sums[0] += column_sum(valid * x1)
        sums[1] += column_sum(valid * x2)
        sums[2] += column_sum(valid)
    spread(st_ref, pack(sums))
    move.finish()


def k_back_second(
    u1_ref, y2_ref, ys_ref, recv_ref, norm_ref, base_ref, keep12_ref, one_ref, y1_ref, count_ref,
    dy0_ref, dy1_ref, dy2_ref, dy3_ref, dys_ref, u0_ref, st_ref, tot_ref,
    uin, y2in, ysin, y1in, db, dsb, wb, ub, sems,
):
    move = Mover(sems)
    first = []
    for o in range(4):
        first.append(
            [
                move.load(ref.at[:, columns(o)], buf.at[:, columns(o)])
                for ref, buf in ((u1_ref, uin), (y2_ref, y2in), (ys_ref, ysin))
            ]
        )
    lw = Taps(move, one_ref, 10 * CIN, wb, BACKWARD)
    ly1 = [move.load(y1_ref.at[:, columns(i)], y1in.at[:, columns(i)]) for i in range(4)]
    got = jnp.sum(recv_ref[...], axis=0)
    tot_ref[...] = got
    positions = base_ref[2:3, :]
    mask = mask_of(count_ref)
    scale1, scale2, shift_total = (channel_row(got, k) for k in range(3))
    c1, i1, c2, i2 = (keep12_ref[k : k + 1, :] for k in range(4))
    for o in range(4):
        for copy in first[o]:
            copy.wait()
        u = uin[:, columns(o)]
        dy2 = reverse_norm(
            u, y2in[:, columns(o)], mask, c1, i1, norm_ref[0, 1:2, :], scale1, shift_total, positions
        )
        db[:, columns(o)] = dy2.astype(bf16)
        move.store(db.at[:, columns(o)], (dy0_ref, dy1_ref, dy2_ref, dy3_ref)[o])
        dys = reverse_norm(
            u, ysin[:, columns(o)], mask, c2, i2, norm_ref[0, 2:3, :], scale2, shift_total, positions
        )
        dsb[:, columns(o)] = dys.astype(bf16)
        move.store(dsb.at[:, columns(o)], dys_ref.at[:, columns(o)])
    centre, inverse = base_ref[0:1, :], base_ref[1:2, :]
    gain, shift = norm_ref[0, 0:1, :], norm_ref[1, 0:1, :]
    sums = [0.0, 0.0]
    for i in range(4):
        grad = backward_taps(db, lw, i)
        ly1[i].wait()
        xhat = (y1in[:, columns(i)] - centre) * inverse
        v = xhat * gain + shift
        s = sigmoid(v)
        u = grad * (s * (1.0 + v * (1.0 - s)))
        ub[:, columns(i)] = u
        move.store(ub.at[:, columns(i)], u0_ref.at[:, columns(i)])
        valid = u * mask
        sums[0] += column_sum(valid * xhat)
        sums[1] += column_sum(valid)
    spread(st_ref, pack(sums))
    move.finish()


def k_back_first(
    u0_ref, y1_ref, recv_ref, norm_ref, base_ref, count_ref,
    dy_ref, tot_ref, uin, yin, db, sems,
):
    move = Mover(sems)
    lu, ly = [], []
    for o in range(4):
        lu.append(move.load(u0_ref.at[:, columns(o)], uin.at[:, columns(o)]))
        ly.append(move.load(y1_ref.at[:, columns(o)], yin.at[:, columns(o)]))
    got = jnp.sum(recv_ref[...], axis=0)
    tot_ref[...] = got
    positions = base_ref[2:3, :]
    mask = mask_of(count_ref)
    scale_total, shift_total = channel_row(got, 0), channel_row(got, 1)
    for o in range(4):
        lu[o].wait()
        ly[o].wait()
        dy = reverse_norm(
            uin[:, columns(o)], yin[:, columns(o)], mask, base_ref[0:1, :], base_ref[1:2, :],
            norm_ref[0, 0:1, :], scale_total, shift_total, positions,
        )
        db[:, columns(o)] = dy.astype(bf16)
        move.store(db.at[:, columns(o)], dy_ref.at[:, columns(o)])
    move.finish()


def k_turn(x_ref, side_ref, mine_ref, theirs_ref, xb, at, tb, sems):
    move = Mover(sems)
    loads = [
        move.load(x_ref.at[:, columns(o)], xb.at[:, columns(o)]) for o in range(16 * CIN // COUT)
    ]
    for cell in range(16):
        if cell % 2 == 0:
            loads[cell // 2].wait()
        split_turn(at, tb, xb[:, pl.ds(cell * CIN, CIN)], cell, CIN)
    hand_out(move, at, side_ref, mine_ref, theirs_ref)
    move.finish()


def pair_taps(lefts, rights, gb, base, half, side_in, stride, ready=None):
    for tap in range(9):
        total = None
        for o in range(4):
            row_in = stride * (o // 2) + tap // 3 - 1
            col_in = stride * (o % 2) + tap % 3 - 1
            if not (0 <= row_in < side_in and 0 <= col_in < side_in):
                continue
            cell = row_in * side_in + col_in
            for left, right in zip(lefts, rights):
                part = dot(left[pl.ds(cell * half, half), :], right[:, columns(o)])
                total = part if total is None else total + part
        gb[pl.ds(base + tap * half, half), :] = total.astype(bf16)
        if ready is not None:
            ready(base + (tap + 1) * half)


class Halves:
    def __init__(self, move, gb, place_ref, outs, first_row=0):
        self.move, self.gb, self.outs = move, gb, outs
        self.x, self.y = place_ref[0, 1], place_ref[0, 2]
        self.done, self.first_row = 0, first_row

    def choose(self, src, keep, kept, sent):
        move = self.move
        sem = move.sems.at[move.used]
        move.used += 1
        pl.when(keep)(pltpu.make_async_copy(src, kept, sem).start)
        pl.when(jnp.logical_not(keep))(pltpu.make_async_copy(src, sent, sem).start)
        move.out.append(pltpu.make_async_copy(src, kept, sem))

    def ready(self, rows):
        left_keep, left_send, right_keep, right_send = self.outs
        half = COUT // 2
        blocks, per, _ = self.gb.shape
        while self.done < blocks and self.first_row + (self.done + 1) * per <= rows:
            z, y, x = self.done // 4, self.done // 2 % 2, self.done % 2
            src = self.gb.at[self.done]
            self.choose(
                src.at[:, pl.ds(0, half)], self.x == x, left_keep.at[z, y], left_send.at[z, y]
            )
            self.choose(
                src.at[:, pl.ds(half, half)], self.y == y, right_keep.at[z, x], right_send.at[z, x]
            )
            self.done += 1


def load_all(move, pairs):
    loads = [move.load(src, dst) for src, dst in pairs]
    for copy in loads:
        copy.wait()


def side_by_side(refs, buf):
    return [(ref, buf.at[:, columns(o)]) for o, ref in enumerate(refs)]


class Taker:
    def __init__(self, refs):
        self.refs = list(refs)

    def __call__(self, count):
        taken, self.refs = self.refs[:count], self.refs[count:]
        return taken


def make_pair_grad(outputs):
    def body(*refs):
        take = Taker(refs)
        (mine_ref, got_ref), dy_refs, dyg_refs, (place_ref,) = take(2), take(4), take(4), take(1)
        outs, (mb, ob, db, dgb, gb, sems) = take(outputs), take(6)
        move = Mover(sems)
        load_all(
            move,
            ((mine_ref, mb), *side_by_side(dy_refs, db), (got_ref, ob), *side_by_side(dyg_refs, dgb)),
        )
        rows = gb.reshape(9 * COUT // 2, COUT)
        ready = Halves(move, gb, place_ref, outs).ready if len(outs) == 4 else None
        pair_taps((mb, ob), (db, dgb), rows, 0, COUT // 2, 2, 1, ready)
        if ready is None:
            move.store(rows, outs[0])
        move.finish()

    return body


def make_pair_second():
    return lambda *refs: pair_second_body(Taker(refs))


def pair_second_body(take):
    (mine_ref, got_ref), dy_refs, dyg_refs = take(2), take(4), take(4)
    xm_ref, xt_ref, dys_ref, place_ref, late_ref, other_ref = take(6)
    *outs, mb, ob, db, dgb, gb, xmb, xtb, dsb, other, sems = take.refs
    move = Mover(sems)
    half = CIN // 2
    later = [move.load(dys_ref, dsb)]
    for o in range(4):
        cell = (o // 2) * 8 + (o % 2) * 2
        for src, dst in ((xm_ref, xmb), (xt_ref, xtb)):
            later.append(move.load(src.at[pl.ds(cell * half, half)], dst.at[pl.ds(o * half, half)]))
    load_all(
        move,
        ((mine_ref, mb), *side_by_side(dy_refs, db), (got_ref, ob), *side_by_side(dyg_refs, dgb)),
    )
    late_rows = late_ref.shape[0]
    ready = None
    if outs:
        blocks, per = outs[0].shape[0] * 4, gb.shape[1]
        rows = gb.reshape(gb.shape[0] * per, COUT)
        start = gb.shape[0] * per - blocks * per
        ready = Halves(move, gb.at[pl.ds(gb.shape[0] - blocks, blocks)], place_ref, outs, start).ready
        base = start - late_rows
    else:
        rows, base = gb, 0
    pair_taps((mb, ob), (db, dgb), rows, base + half, COUT // 2, 2, 1, ready)
    for copy in later:
        copy.wait()
    for left, out in ((xmb, rows.at[pl.ds(base, half)]), (xtb, other)):
        total = None
        for o in range(4):
            part = dot(left[pl.ds(o * half, half), :], dsb[:, columns(o)])
            total = part if total is None else total + part
        out[...] = total.astype(bf16)
    move.store(rows.at[pl.ds(base, late_rows)], late_ref)
    move.store(other, other_ref)
    move.finish()


def k_pair_first(*refs):
    take = Taker(refs)
    xm_ref, xg_ref, dy_ref, dyg_ref, late_ref, other_ref, place_ref = take(7)
    *outs, mb, ob, db, dgb, gb, other, sems = take.refs
    move = Mover(sems)
    half = CIN // 2
    rows = gb.reshape(gb.shape[0] * gb.shape[1], COUT)
    late = [
        move.load(late_ref, rows.at[pl.ds(9 * half, late_ref.shape[0])]),
        move.load(other_ref, other),
    ]
    load_all(move, ((xm_ref, mb), (dy_ref, db), (xg_ref, ob), (dyg_ref, dgb)))
    for copy in late:
        copy.wait()
    short = pl.ds(9 * half, half)
    rows[short, :] = plus(rows[short, :], other[...])
    ready = Halves(move, gb, place_ref, outs).ready if len(outs) == 4 else None
    pair_taps((mb, ob), (db, dgb), rows, 0, half, 4, 2, ready)
    if ready is None:
        move.store(rows, outs[0])
    else:
        ready(gb.shape[0] * gb.shape[1])
    move.finish()


def plus(left, right):
    return (left.astype(f32) + right.astype(f32)).astype(bf16)


def k_merge(*refs):
    *parts, place_ref, lk2_ref, ls2_ref, rk2_ref, rs2_ref = refs
    x, y = place_ref[0, 1], place_ref[0, 2]
    at = 0
    for k in range(0, len(parts), 4):
        lk_ref, lg_ref, rk_ref, rg_ref = parts[k : k + 4]
        for z in range(lk_ref.shape[0]):
            lk2_ref[at] = plus(lk_ref[z, y], lg_ref[z, y])
            ls2_ref[at] = plus(lk_ref[z, 1 - y], lg_ref[z, 1 - y])
            rk2_ref[at] = plus(rk_ref[z, x], rg_ref[z, x])
            rs2_ref[at] = plus(rk_ref[z, 1 - x], rg_ref[z, 1 - x])
            at += 1


def k_line(*refs):
    *parts, place_ref, own_ref, s1_ref, s2_ref, s3_ref, held = refs
    z_here = place_ref[0, 3]
    half = COUT // 2
    at = 0
    for k in range(0, len(parts), 4):
        lk_ref, lg_ref, rk_ref, rg_ref = parts[k : k + 4]
        for z in range(lk_ref.shape[0]):
            held[at, :, 0:half] = plus(lk_ref[z], lg_ref[z])
            held[at, :, half:COUT] = plus(rk_ref[z], rg_ref[z])
            at += 1
    own_ref[...] = held[z_here]
    for other, ref in ((1, s1_ref), (2, s2_ref), (3, s3_ref)):
        ref[...] = held[jnp.bitwise_xor(z_here, other)]


def k_side(own_ref, g1_ref, g2_ref, g3_ref, place_ref, keep_ref, send_ref):
    side = place_ref[0, 0]

    def total(at):
        return (own_ref[at].astype(f32) + g1_ref[at].astype(f32)) + (
            g2_ref[at].astype(f32) + g3_ref[at].astype(f32)
        )

    keep_ref[...] = total(side)
    send_ref[...] = total(1 - side).astype(bf16)


def make_update(rate):
    def body(
        keep_ref, got_ref, place_ref, master_ref, momentum_ref, average_ref,
        moment_ref, weight_ref, mean_ref, copy_ref,
    ):
        lower = place_ref[0, 0] == 0
        for group in range(keep_ref.shape[0] // 16):
            here = keep_ref[pl.ds(16 * group, 16), :]
            there = got_ref[pl.ds(16 * group, 16), :].astype(f32)
            for parity in range(2):
                at = pl.ds(32 * group + 16 * parity, 16)
                grad = jnp.where(lower, here, there) if parity == 0 else jnp.where(lower, there, here)
                moment, fresh, mean = nesterov(
                    grad, master_ref[at, :], momentum_ref[at, :], average_ref[at, :], rate
                )
                moment_ref[at, :] = moment
                weight_ref[at, :] = fresh
                mean_ref[at, :] = mean
                copy_ref[at, :] = fresh.astype(bf16)

    return body


def k_stack(*refs):
    *parts, value_ref, here_ref, out_ref = refs
    for z, ref in enumerate(parts):
        here_ref[z] = ref[...]
    out_ref[...] = value_ref[...].astype(bf16)


def k_pick(own_ref, r1_ref, r2_ref, r3_ref, place_ref, low_ref, high_ref):
    z_here = place_ref[0, 3]
    for z in range(4):
        out, at = (low_ref, z) if z < 2 else (high_ref, z - 2)
        for other, ref in enumerate((own_ref, r1_ref, r2_ref, r3_ref)):

            def copy(ref=ref, out=out, at=at):
                out[at] = ref[...]

            pl.when(jnp.bitwise_xor(z_here, z) == other)(copy)


def k_cut(over_x_ref, over_y_ref, lower_ref, upper_ref):
    rows = upper_ref.shape[1]
    lower_ref[...] = over_x_ref[:, rows:, :]
    upper_ref[...] = over_y_ref[:, :rows, :]


def k_input_grad(dy_ref, dys_ref, one_ref, dx_ref, db, dsb, wb, xb, sems):
    move = Mover(sems)
    loads = [
        move.load(one_ref.at[pl.ds(0, 10 * CIN)], wb),
        move.load(dy_ref, db),
        move.load(dys_ref, dsb),
    ]
    for copy in loads:
        copy.wait()
    for cell in range(16):
        row_in, col_in = divmod(cell, 4)
        total = None
        for o in range(4):
            row_tap, col_tap = row_in - 2 * (o // 2) + 1, col_in - 2 * (o % 2) + 1
            if not (0 <= row_tap < 3 and 0 <= col_tap < 3):
                continue
            part = dot_nt(db[:, columns(o)], wb[pl.ds((row_tap * 3 + col_tap) * CIN, CIN), :])
            total = part if total is None else total + part
        if row_in % 2 == 0 and col_in % 2 == 0:
            o = (row_in // 2) * 2 + col_in // 2
            total = total + dot_nt(dsb[:, columns(o)], wb[pl.ds(9 * CIN, CIN), :])
        xb[:, pl.ds(cell * CIN, CIN)] = total
        move.store(xb.at[:, pl.ds(cell * CIN, CIN)], dx_ref.at[:, pl.ds(cell * CIN, CIN)])
    move.finish()


def nesterov(grad, master, momentum, average, rate):
    moment = momentum_decay * momentum + grad
    fresh = master - rate * (grad + momentum_decay * moment)
    return (moment, fresh, average_decay * average + (1.0 - average_decay) * fresh)


def exchange(packed):
    return lax.all_to_all(packed, AXES, 0, 0, tiled=True)


def swap(value, devices, bits):
    return lax.ppermute(value, AXES, [(i, i ^ bits) for i in range(devices)])


class Grid:
    def __init__(self, devices, number):
        self.devices = devices
        parts = (number % 2, (number // 2) % 2, (number // 4) % 2, number // 8)
        self.place = jnp.stack(parts).astype(jnp.int32).reshape(1, 4)

    def swap(self, value, bits):
        return swap(value, self.devices, bits)


def stack(parts, value, after):
    return run(
        k_stack,
        (*parts, value),
        [VMEM] * (len(parts) + 1),
        [shape((len(parts), *parts[0].shape), bf16), shape(value.shape, bf16)],
        [VMEM] * 2,
        [],
        moved=1_000_000,
        name="stack",
        after=after,
    )


def cut(grid, over, after):
    parts, rows, _ = over[0].shape
    return run(
        k_cut,
        over,
        [VMEM] * 2,
        [shape((parts, rows // 2, COUT), bf16)] * 2,
        [VMEM] * 2,
        [],
        moved=1_000_000,
        name="cut",
        after=after,
    )


def gather_pieces(grid, here, over_x, over_y, cut=None):
    rows = here.shape[1] // 2
    lower, upper = cut or (over_x[:, rows:], over_y[:, :rows])
    own = [here, over_x, over_y, grid.swap(upper, 2), grid.swap(lower, 4)]
    return own + [grid.swap(v, 1) for v in own]


def assemble(pieces, number, held, groups, after):
    devices, rows, _ = held.shape
    return run(
        make_assemble(groups),
        (*pieces, number),
        [HBM] * len(pieces) + [SMEM],
        shape((devices * rows, COUT), bf16),
        HBM,
        [held, pltpu.SemaphoreType.DMA((41,))],
        moved=1_000_000,
        name="assemble",
        after=after,
    )


def scatter_first(grid, halves):
    left_keep, left_send, right_keep, right_send = halves
    return left_keep, grid.swap(left_send, 2), right_keep, grid.swap(right_send, 4)


def scatter_second(grid, halves):
    left_keep, left_send, right_keep, right_send = halves
    return left_keep, grid.swap(left_send, 4), right_keep, grid.swap(right_send, 2)


def merge(grid, parts, after=()):
    arrays = [v for part in parts for v in part]
    _, _, rows, half = arrays[0].shape
    nz = sum(part[0].shape[0] for part in parts)
    return run(
        k_merge,
        (*arrays, grid.place),
        [VMEM] * len(arrays) + [SMEM],
        [shape((nz, rows, half), bf16)] * 4,
        [VMEM] * 4,
        [],
        moved=1_000_000,
        name="merge",
        after=after,
    )


def line(grid, parts, after):
    rows = parts[0].shape[1]
    own, s1, s2, s3 = run(
        k_line,
        (*parts, grid.place),
        [VMEM] * len(parts) + [SMEM],
        [shape((rows, COUT), bf16)] * 4,
        [VMEM] * 4,
        [pltpu.VMEM((4, rows, COUT), bf16)],
        moved=1_000_000,
        name="line",
        after=after,
    )
    return own, grid.swap(s1, 8), grid.swap(s2, 16), grid.swap(s3, 24)


def sides(grid, parts, after=()):
    rows = parts[0].shape[0] // 2
    keep, send = run(
        k_side,
        (*(v.reshape(2, rows, COUT) for v in parts), grid.place),
        [VMEM] * 4 + [SMEM],
        [shape((rows, COUT), f32), shape((rows, COUT), bf16)],
        [VMEM] * 2,
        [],
        moved=1_000_000,
        name="sides",
        after=after,
    )
    return keep, grid.swap(send, 1)


def update(grid, parts, states, rate, after=()):
    kept = shape(states[0].shape, f32)
    return run(
        make_update(rate),
        (*parts, grid.place, *states),
        [VMEM, VMEM, SMEM, VMEM, VMEM, VMEM],
        [kept, kept, kept, shape(states[0].shape, bf16)],
        [VMEM] * 4,
        [],
        moved=1_000_000,
        name="update",
        after=after,
    )


def reduce_halves(devices, side, half_grad):
    groups = half_grad.reshape(-1, 16, COUT)
    empty = jnp.zeros_like(groups)
    full = jnp.stack(
        [jnp.where(side == 0, groups, empty), jnp.where(side == 0, empty, groups)], axis=1
    ).reshape(-1, COUT)
    return lax.psum_scatter(full, AXES, scatter_dimension=0, tiled=True).astype(f32)


def make_shards(devices, fast):
    def shards(
        features,
        labels,
        image_counts,
        block_one_master,
        block_one_momentum,
        block_one_average,
        block_two_master,
        block_two_momentum,
        block_two_average,
        norm_params,
        norm_momentum,
        norm_average,
        head_params,
        head_momentum,
        head_average,
    ):
        images_all = CAP * devices
        count = image_counts
        side = (lax.axis_index("pass") % 2).astype(jnp.int32).reshape(1, 1)
        number = lax.axis_index("batch") * lax.axis_size("pass") + lax.axis_index("pass")
        number = number.astype(jnp.int32)
        grid = Grid(devices, number) if fast else None
        number = number.reshape(1, 1)
        place = grid.place if fast else number
        shard = block_one_master.astype(bf16)
        x = features.reshape(CAP, 16 * CIN)

        rows_one, rows_two = devices * shard.shape[0], devices * block_two_master.shape[0]
        wide_f, wide_b = shape((CAP, WIDE), f32), shape((CAP, WIDE), bf16)
        wf, wb16 = pltpu.VMEM((CAP, WIDE), f32), pltpu.VMEM((CAP, WIDE), bf16)
        weight = pltpu.VMEM((9 * COUT, COUT), bf16)
        small = shape((8, COUT), f32)
        packed8, packed16 = shape((8, LANES), f32), shape((16, LANES), f32)
        send8, send16 = shape((devices, 8, LANES), f32), shape((devices, 16, LANES), f32)

        def sems(n):
            return pltpu.SemaphoreType.DMA((n,))

        conv_flops = 2 * 16 * CAP * COUT * COUT
        first_flops = 2 * 29 * CAP * CIN * COUT
        head_rows = head_params[:COUT]
        pad = LANES - 3 * TASKS

        def thrice(v):
            return jnp.concatenate([v, v, v, jnp.zeros((v.shape[0], pad), v.dtype)], axis=1)

        head_wide = thrice(head_rows)
        bias_wide = thrice(head_params[COUT:])
        labels_wide = thrice(labels.astype(f32))
        turned = jnp.pad(head_rows.T, ((0, LANES - TASKS), (0, 0)))
        square = jnp.pad(
            jnp.dot(head_rows.T, head_rows, precision=highest), ((0, 0), (0, LANES - TASKS))
        )

        turned_half = shape((WIDE // 2, CAP), bf16)
        turn_scratch = [pltpu.VMEM((2, WIDE // 2, CAP), bf16), pltpu.VMEM((COUT, CAP), bf16)]

        def sibling(value):
            return swap(value, devices, 1)

        x_mine, x_theirs = run(
            k_turn,
            (x, side),
            [HBM, SMEM],
            [shape((8 * CIN, CAP), bf16)] * 2,
            [HBM, HBM],
            [
                pltpu.VMEM((CAP, 16 * CIN), bf16),
                pltpu.VMEM((2, 8 * CIN, CAP), bf16),
                pltpu.VMEM((COUT, CAP), bf16),
                sems(19),
            ],
            0,
            4_000_000,
            name="turn_features",
        )
        x_got = sibling(x_theirs)
        if fast:
            far = [grid.swap(shard, 8 * other) for other in (1, 2, 3)]
            here, shard_two = stack((shard, *far), block_two_master, (x_mine,))
            one = far = gather_pieces(grid, here, grid.swap(here, 2), grid.swap(here, 4))
            low, high = run(
                k_pick,
                (
                    shard_two,
                    *(grid.swap(shard_two, 8 * other) for other in (1, 2, 3)),
                    grid.place,
                ),
                [VMEM] * 4 + [SMEM],
                [shape((2, *shard_two.shape), bf16)] * 2,
                [VMEM] * 2,
                [],
                moved=1_000_000,
                name="pick",
                after=(far[3], far[4]),
            )
            over_low = grid.swap(low, 2), grid.swap(low, 4)
            held = pltpu.VMEM((devices, *shard.shape), bf16)
            held_two = pltpu.VMEM((devices // 2, *shard_two.shape), bf16)
            whole_two = pltpu.VMEM((devices, *shard_two.shape), bf16)
            first_after = (x_mine, low)
        else:
            one = [lax.all_gather(shard, AXES, axis=0, tiled=True)]
            two = [lax.all_gather(block_two_master.astype(bf16), AXES, axis=0, tiled=True)]
            held = pltpu.VMEM((devices * shard.shape[0], COUT), bf16)
            held_two = weight
            first_after = (x_mine,)
            second_after = third_after = ()
        y1, ys, st, local = run(
            make_first(len(one)),
            (x, *one, number, count),
            [HBM] * (1 + len(one)) + [SMEM, SMEM],
            [wide_f, wide_f, send16, packed8],
            [HBM, HBM, VMEM, VMEM],
            [
                pltpu.VMEM((CAP, 16 * CIN), bf16),
                held,
                pltpu.VMEM((2, CAP, WIDE), f32),
                sems(50),
            ],
            first_flops,
            9_000_000,
            name="first_conv",
            after=first_after,
        )
        if fast:
            cut_low = cut(grid, over_low, (y1,))
            second_after = cut_low[:1]
            two = gather_pieces(grid, low, *over_low, cut_low)
            over_high = grid.swap(high, 2), grid.swap(high, 4)
        got = exchange(st)
        w_one = assemble(one, number, held, NEAR_FAR, (y1,)) if fast else one[0]
        a1_mine, a1_theirs, y2, st, keep0 = run(
            k_second,
            (y1, got, norm_params, local, w_one, count, side),
            [HBM, VMEM, VMEM, VMEM, HBM, SMEM, SMEM],
            [turned_half, turned_half, wide_f, send16, small],
            [HBM, HBM, HBM, VMEM, VMEM],
            [wf, wb16, *turn_scratch, weight, wf, sems(20)],
            conv_flops,
            10_000_000,
            name="second_conv",
            after=second_after,
        )
        if fast:
            cut_high = cut(grid, over_high, (y2,))
            third_after = cut_high[:1]
            two_high = gather_pieces(grid, high, *over_high, cut_high)
        got = exchange(st)
        a1_got = sibling(a1_theirs)
        h1, hb_mine, hb_theirs, y3, st, keep12 = run(
            make_third(len(two)),
            (*two, number, y2, ys, got, norm_params, keep0, count, side),
            [HBM] * len(two) + [SMEM, HBM, HBM, VMEM, VMEM, VMEM, SMEM, SMEM],
            [wide_f, turned_half, turned_half, wide_f, send8, small],
            [HBM, HBM, HBM, HBM, VMEM, VMEM],
            [wf, wf, wf, wb16, *turn_scratch, held_two, wf, sems(58)],
            conv_flops,
            14_000_000,
            name="third_conv",
            after=(*third_after, a1_got),
        )
        got = exchange(st)
        w_two = assemble(two + two_high, number, whole_two, LOW_HIGH, (y3,)) if fast else two[0]
        hb_got = sibling(hb_theirs)
        a3_mine, a3_theirs, y4, st, keep3 = run(
            k_fourth,
            (y3, got, norm_params, keep0, w_two, count, side),
            [HBM, VMEM, VMEM, VMEM, HBM, SMEM, SMEM],
            [turned_half, turned_half, wide_f, send8, small],
            [HBM, HBM, HBM, VMEM, VMEM],
            [wf, wb16, *turn_scratch, weight, wf, sems(20)],
            conv_flops,
            10_000_000,
            name="fourth_conv",
            after=(hb_got,),
        )
        got = exchange(st)
        a3_got = sibling(a3_theirs)
        wide_lanes = shape((CAP, LANES), f32)
        pooled, resid, slope, st, part, keep4 = run(
            k_heads,
            (y4, h1, got, norm_params, keep0, head_wide, bias_wide, labels_wide, count),
            [HBM, HBM, VMEM, VMEM, VMEM, VMEM, VMEM, VMEM, SMEM],
            [
                shape((CAP, COUT), f32),
                wide_lanes,
                wide_f,
                send16,
                shape((8 * devices, LANES), f32),
                small,
            ],
            [VMEM, VMEM, HBM, VMEM, VMEM, VMEM],
            [wf, wf, wf, sems(21)],
            1_000_000_000,
            7_000_000,
            name="heads",
            after=(a3_got,),
        )
        got = exchange(st)
        weights, u2, st = run(
            k_weights,
            (
                got, square, resid, turned, keep0, keep4, part.reshape(devices, 8, LANES), y4, slope, count,
            ),
            [VMEM, VMEM, VMEM, VMEM, VMEM, VMEM, VMEM, HBM, HBM, SMEM],
            [packed8, wide_f, send16],
            [VMEM, HBM, VMEM],
            [wf, wf, wf, sems(21)],
            1_000_000_000,
            7_000_000,
            name="task_weights",
        )

        got = exchange(st)
        narrow = [shape((CAP, COUT), bf16)] * 4
        *dy4, u3, st, tot4 = run(
            k_back_fourth,
            (u2, y4, got, norm_params, keep0, keep4, w_two, y3, keep3, count),
            [HBM, HBM, VMEM, VMEM, VMEM, VMEM, HBM, HBM, VMEM, SMEM],
            [*narrow, wide_f, send16, packed8],
            [HBM] * 5 + [VMEM, VMEM],
            [wf, wf, wf, wb16, weight, wf, sems(30)],
            conv_flops,
            14_000_000,
            name="fourth_back",
        )
        got = exchange(st)
        half_rows = 9 * COUT // 2
        half_turned = pltpu.VMEM((WIDE // 2, CAP), bf16)
        pair_scratch = [half_turned, half_turned, wb16, wb16]
        part_two, part_one = rows_two // devices, rows_one // devices

        def halves_of(nz, rows):
            if not fast:
                return shape((half_rows, COUT), bf16), HBM
            return [shape((nz, 2, rows, COUT // 2), bf16)] * 4, [HBM] * 4

        def siblings(values):
            return [sibling(v) for v in values]

        def pair_grad(mine, theirs, dy, dy_got, name, after=()):
            outs, out_specs = halves_of(2, part_two)
            blocks = (8, part_two, COUT) if fast else (1, half_rows, COUT)
            return run(
                make_pair_grad(4 if fast else 1),
                (mine, theirs, *dy, *dy_got, place),
                [HBM] * 10 + [SMEM],
                outs,
                out_specs,
                [*pair_scratch, pltpu.VMEM(blocks, bf16), sems(45)],
                conv_flops,
                6_000_000,
                name=name,
                after=after,
            )

        def ties(value):
            return (value[0],) if fast else (value,)

        grads_four = pair_grad(a3_mine, a3_got, dy4, siblings(dy4), "fourth_weights")
        if fast:
            first_four = scatter_first(grid, grads_four)
        *dy3, u1, st, tot3, head_sum = run(
            k_back_third,
            (u3, y3, got, norm_params, keep0, keep3, w_two, u2, y2, ys, keep12, count),
            [HBM, HBM, VMEM, VMEM, VMEM, VMEM, HBM, HBM, HBM, HBM, VMEM, SMEM],
            [*narrow, wide_f, send16, packed8, send8],
            [HBM] * 5 + [VMEM, VMEM, VMEM],
            [wf, wf, wf, wf, wf, wb16, weight, wf, sems(38)],
            conv_flops,
            18_000_000,
            name="third_back",
            share=1,
            after=ties(grads_four),
        )
        got = exchange(st)
        tie = first_four[1::2] if fast else ()
        grads_three = pair_grad(hb_mine, hb_got, dy3, siblings(dy3), "third_weights", tie)
        if fast:
            first_three = scatter_first(grid, grads_three)
        tie = ties(grads_three)
        *dy2, dys, u0, st, tot12 = run(
            k_back_second,
            (u1, y2, ys, got, norm_params, keep0, keep12, w_one, y1, count),
            [HBM, HBM, HBM, VMEM, VMEM, VMEM, VMEM, HBM, HBM, SMEM],
            [*narrow, wide_b, wide_f, send8, packed16],
            [HBM] * 6 + [VMEM, VMEM],
            [wf, wf, wf, wf, wb16, wb16, weight, wf, sems(38)],
            conv_flops,
            18_000_000,
            name="second_back",
            share=1,
            after=tie,
        )
        got = exchange(st)
        tie = ()
        if fast:
            second_two = merge(grid, (first_three, first_four), (u0,))
            tie = ties(second_two)
            second_two = scatter_second(grid, second_two)
        dy2_got = siblings(dy2)
        dy1, tot0 = run(
            k_back_first,
            (u0, y1, got, norm_params, keep0, count),
            [HBM, HBM, VMEM, VMEM, VMEM, SMEM],
            [wide_b, packed8],
            [HBM, VMEM],
            [wf, wf, wb16, sems(21)],
            0,
            5_000_000,
            name="first_back",
            after=(*tie, *dy2_got),
        )
        dy1_got = sibling(dy1)
        late_rows = rows_one // 4 - 9 * CIN // 2 if fast else half_rows + CIN // 2
        half_short = (CIN // 2, COUT)
        outs, out_specs = [shape((late_rows, COUT), bf16), shape(half_short, bf16)], [HBM] * 2
        late_buf = pltpu.VMEM((late_rows, COUT), bf16)
        if fast:
            quarter = [shape((2, 2, part_one, COUT // 2), bf16)] * 4
            outs, out_specs = [*outs, *quarter], [HBM] * 6
            late_buf = pltpu.VMEM((16, part_one, COUT), bf16)
        grads_late, short, *grads_last = run(
            make_pair_second(),
            (a1_mine, a1_got, *dy2, *dy2_got, x_mine, x_theirs, dys, place),
            [HBM] * 13 + [SMEM],
            outs,
            out_specs,
            [
                *pair_scratch,
                late_buf,
                pltpu.VMEM((2 * CIN, CAP), bf16),
                pltpu.VMEM((2 * CIN, CAP), bf16),
                wb16,
                pltpu.VMEM(half_short, bf16),
                sems(48),
            ],
            conv_flops,
            9_000_000,
            name="second_weights",
            after=(dy1,),
        )
        tie = (grads_late,)
        if fast:
            first_last = scatter_first(grid, grads_last)
            third_two = line(grid, second_two, (grads_late,))
            tie = ties(third_two)
        short_got = sibling(short)
        half_features = pltpu.VMEM((8 * CIN, CAP), bf16)
        if fast:
            outs, out_specs = quarter, [HBM] * 4
        else:
            outs, out_specs = shape((rows_one // 2, COUT), bf16), HBM
        blocks = (8, part_one, COUT) if fast else (1, rows_one // 2, COUT)
        grads_one = run(
            k_pair_first,
            (x_mine, x_got, dy1, dy1_got, grads_late, short_got, place),
            [HBM] * 6 + [SMEM],
            outs,
            out_specs,
            [
                half_features,
                half_features,
                wb16,
                wb16,
                pltpu.VMEM(blocks, bf16),
                pltpu.VMEM(half_short, bf16),
                sems(48),
            ],
            first_flops,
            8_000_000,
            name="first_weights",
            after=tie,
        )
        def back_to_features():
            dx = run(
                k_input_grad,
                (dy1, dys, w_one),
                [HBM] * 3,
                shape((CAP, 16 * CIN), f32),
                HBM,
                [
                    wb16,
                    wb16,
                    pltpu.VMEM((10 * CIN, COUT), bf16),
                    pltpu.VMEM((CAP, 16 * CIN), f32),
                    sems(28),
                ],
                first_flops,
                9_000_000,
                name="input_grad",
            )
            return dx, dx.reshape(CAP, 4, 4, CIN)

        states_one = (block_one_master, block_one_momentum, block_one_average)
        states_two = (block_two_master, block_two_momentum, block_two_average)
        rate = rate_conv * math.sqrt(images_all)
        if fast:
            first_one = scatter_first(grid, grads_one)
            dx, input_grad = back_to_features()
            second_one = scatter_second(grid, merge(grid, (first_one, first_last), (dx,)))
            fourth_two = sides(grid, third_two, second_one[:1])
            third_one = line(grid, second_one, (fourth_two[0],))
            two_m, two_w, two_a, two_c = update(grid, fourth_two, states_two, rate)
            fourth_one = sides(grid, third_one, (two_m, input_grad))
            one_m, one_w, one_a, one_c = update(grid, fourth_one, states_one, rate)
        else:
            two_sum = reduce_halves(
                devices, side[0, 0], jnp.concatenate([grads_three, grads_four], axis=0)
            )
            one_sum = reduce_halves(devices, side[0, 0], grads_one)
            one_m, one_w, one_a = nesterov(one_sum, *states_one, rate)
            two_m, two_w, two_a = nesterov(two_sum, *states_two, rate)
            one_c, two_c = one_w.astype(bf16), two_w.astype(bf16)
            _, input_grad = back_to_features()
        def unpacked(packed):
            return packed.reshape(-1, COUT)

        t0, t3, t4, t12 = unpacked(tot0), unpacked(tot3), unpacked(tot4), unpacked(tot12)
        norm_grad = jnp.stack(
            [
                jnp.stack([t0[0], t12[0], t12[1], t3[0], t4[0]]),
                jnp.stack([t0[1], t12[2], t12[2], t3[1], t4[1]]),
            ]
        )
        total = keep0[2, 0] * 0.25
        head_sum = head_sum.reshape(-1, LANES)[: 5 * TASKS].reshape(5, TASKS, LANES)
        task_losses = head_sum[4, :, 1] / total
        head_grad = jnp.concatenate(
            [head_sum[:4].transpose(0, 2, 1).reshape(COUT, TASKS), head_sum[4, :, 0][None]], axis=0
        ) / total
        scale_rate = math.sqrt(images_all)
        norm_m, norm_w, norm_a = nesterov(
            norm_grad, norm_params, norm_momentum, norm_average, rate_norm * scale_rate
        )
        head_m, head_w, head_a = nesterov(
            head_grad, head_params, head_momentum, head_average, rate_head * scale_rate
        )
        return (
            pooled,
            input_grad,
            task_losses,
            weights[0, :TASKS],
            one_m,
            one_w,
            one_a,
            one_c,
            two_m,
            two_w,
            two_a,
            two_c,
            norm_m,
            norm_w,
            norm_a,
            head_m,
            head_w,
            head_a,
        )

    return shards


def solution(mesh):
    devices = mesh.shape["batch"] * mesh.shape["pass"]
    fast = mesh.shape["batch"] == 8 and mesh.shape["pass"] == 4
    rows = P(AXES, None)
    in_specs = (
        P(AXES, None, None, None),
        rows,
        P("batch", "pass"),
        rows,
        rows,
        rows,
        rows,
        rows,
        rows,
        P(),
        P(),
        P(),
        P(),
        P(),
        P(),
    )
    out_specs = (
        rows,
        P(AXES, None, None, None),
        P(),
        P(),
        rows,
        rows,
        rows,
        rows,
        rows,
        rows,
        rows,
        rows,
        P(),
        P(),
        P(),
        P(),
        P(),
        P(),
    )
    return jax.shard_map(
        make_shards(devices, fast), mesh=mesh, in_specs=in_specs, out_specs=out_specs, check_vma=False
    )
```

```python
import math

import jax
import jax.numpy as jnp
from jax import lax
from jax.experimental import pallas as pl
from jax.experimental.pallas import tpu as pltpu
from jax.sharding import PartitionSpec as P

CIN = 256
COUT = 512
TASKS = 40
FW_STEPS = 20
CAP = 256
WIDE = 4 * COUT
LANES = 128
AXES = ("batch", "pass")

epsilon = 1e-05
softness = 0.01
momentum_decay = 0.9
average_decay = 0.9
rate_conv = 3.0
rate_norm = 50.0
rate_head = 0.05
highest = lax.Precision.HIGHEST

HBM = pl.BlockSpec(memory_space=pltpu.HBM)
VMEM = pl.BlockSpec(memory_space=pltpu.VMEM)
SMEM = pl.BlockSpec(memory_space=pltpu.SMEM)
f32 = jnp.float32
bf16 = jnp.bfloat16


def shape(extent, kind):
    return jax.ShapeDtypeStruct(extent, kind)


def run(
    body, args, in_specs, outs, out_specs, scratch, flops=0, moved=0, aliases=None, name=None, after=(), through=None,
    share=1,
):
    first, last = len(args), len(args) + len(after)
    args, in_specs = (*args, *after), [*in_specs, *[HBM] * len(after)]
    aliases = dict(aliases or {})
    if through is not None:
        outs, out_specs = [*outs, shape(through.shape, through.dtype)], [*out_specs, HBM]
        aliases[len(args)] = len(outs) - 1
        args, in_specs = (*args, through), [*in_specs, HBM]
    count, results = len(args), len(outs) if isinstance(outs, list) else 1

    def plain(*refs):
        made = refs[count : count + results - (through is not None)]
        body(*refs[:first], *made, *refs[count + results :])

    return pl.pallas_call(
        plain if count > first else body,
        out_shape=outs,
        in_specs=in_specs,
        out_specs=out_specs,
        scratch_shapes=scratch,
        input_output_aliases=aliases,
        compiler_params=pltpu.CompilerParams(vmem_limit_bytes=67_000_000),
        cost_estimate=pl.CostEstimate(
            flops=flops // share, bytes_accessed=moved // share, transcendentals=0
        ),
        name=name,
    )(*args)


class Mover:
    def __init__(self, sems):
        self.sems = sems
        self.used = 0
        self.out = []

    def load(self, src, dst):
        copy = pltpu.make_async_copy(src, dst, self.sems.at[self.used])
        self.used += 1
        copy.start()
        return copy

    def store(self, src, dst):
        self.out.append(self.load(src, dst))

    def finish(self):
        for copy in self.out:
            copy.wait()


def columns(o):
    return pl.ds(o * COUT, COUT)


def split_turn(at, tb, value, place, channels):
    half = channels // 2
    tb[pl.ds(0, channels), :] = value.T
    for group in range(half // 16):
        for parity in range(2):
            at[parity, pl.ds(place * half + 16 * group, 16), :] = tb[
                pl.ds(32 * group + 16 * parity, 16), :
            ]


def hand_out(move, at, side_ref, mine_ref, theirs_ref):
    side = side_ref[0, 0]
    move.store(at.at[side], mine_ref)
    move.store(at.at[1 - side], theirs_ref)


def dot(left, right, precision=None):
    return jnp.dot(left, right, preferred_element_type=f32, precision=precision)


def dot_nt(left, right):
    return lax.dot_general(left, right, (((1,), (1,)), ((), ())), preferred_element_type=f32)


def dot_tn(left, right, precision=None):
    return lax.dot_general(
        left, right, (((0,), (0,)), ((), ())), preferred_element_type=f32, precision=precision
    )


def sigmoid(v):
    return 0.5 * jnp.tanh(0.5 * v) + 0.5


def channel_row(packed, k):
    return jnp.concatenate([packed[4 * k + b : 4 * k + b + 1, :] for b in range(4)], axis=1)


def pack(rows):
    pieces = [row[:, b * LANES : (b + 1) * LANES] for row in rows for b in range(4)]
    while len(pieces) % 8:
        pieces.append(jnp.zeros((1, LANES), f32))
    return jnp.concatenate(pieces, axis=0)


def spread(out_ref, packed):
    out_ref[...] = jnp.broadcast_to(packed[None], out_ref.shape)


def mask_of(count_ref):
    rows = lax.broadcasted_iota(jnp.int32, (CAP, COUT), 0)
    return (rows < count_ref[0, 0]).astype(f32)


def column_sum(v):
    return jnp.sum(v, axis=0, keepdims=True)


def moments(total_sum, total_square, positions):
    centre = total_sum / positions
    spread_value = total_square / positions - centre * centre
    return centre, lax.rsqrt(spread_value + epsilon)


class Taps:
    def __init__(self, move, src, base, buf, order):
        self.buf = buf
        self.copies = {
            tap: move.load(
                src.at[pl.ds(base + tap * COUT, COUT)], buf.at[pl.ds(tap * COUT, COUT)]
            )
            for tap in order
        }

    def rows(self, first, count=1):
        for tap in range(first, first + count):
            copy = self.copies.pop(tap, None)
            if copy is not None:
                copy.wait()
        return self.buf[pl.ds(first * COUT, count * COUT), :]


FORWARD = (4, 5, 7, 8, 3, 6, 1, 2, 0)
BACKWARD = (4, 3, 1, 0, 5, 2, 7, 6, 8)


def forward_taps(act_ref, w_ref, o):
    row_out, col_out = divmod(o, 2)
    total = None
    for row_in in range(2):
        tap = (row_in - row_out + 1) * 3 + (1 - col_out)
        weights = w_ref.rows(tap, 2) if isinstance(w_ref, Taps) else w_ref[pl.ds(tap * COUT, 2 * COUT), :]
        part = dot(act_ref[:, pl.ds(row_in * 2 * COUT, 2 * COUT)], weights)
        total = part if total is None else total + part
    return total


def tap_of(i, o):
    return (i // 2 - o // 2 + 1) * 3 + (i % 2 - o % 2 + 1)


def backward_taps(dy_ref, w_ref, i):
    total = None
    for o in range(4):
        part = dot_nt(dy_ref[:, columns(o)], w_ref.rows(tap_of(i, o)))
        total = part if total is None else total + part
    return total


def first_pairs(o):
    row_out, col_out = divmod(o, 2)
    runs = []
    for row_tap in range(3):
        row_in = 2 * row_out + row_tap - 1
        if 0 <= row_in < 4:
            col_tap = 1 if col_out == 0 else 0
            runs.append((row_in * 4 + 2 * col_out + col_tap - 1, row_tap * 3 + col_tap, 3 - col_tap))
    return runs


def pieces_of(refs, number, groups):
    found = []
    for at, (fixed, zs) in enumerate(groups):
        for side in range(2):
            for k, bits in ((0, 0), (1, 2), (2, 4), (3, 6), (4, 6)):
                ref = refs[10 * at + 5 * side + k]
                for part, z in enumerate(zs):
                    if fixed:
                        owner = 8 * z + jnp.bitwise_xor(jnp.bitwise_and(number, 7), bits + side)
                    else:
                        owner = jnp.bitwise_xor(number, 8 * z + bits + side)
                    found.append((ref.at[part], owner, ref.shape[1] if k == 4 else 0))
    return found


NEAR_FAR = ((False, (0, 1, 2, 3)),)
LOW = ((True, (0, 1)),)
LOW_HIGH = ((True, (0, 1)), (True, (2, 3)))


class Rows:
    def __init__(self, move, refs, number_ref, buf, low, high, groups, first=0):
        self.waits = []
        if len(refs) == 1:
            self.rows = buf
            at = pl.ds(low - first, high - low)
            self.waits.append((None, move.load(refs[0].at[pl.ds(low, high - low)], buf.at[at])))
            return
        per = buf.shape[1]
        number = number_ref[0, 0]
        for src, owner, row in pieces_of(refs, number, groups):
            live = jnp.logical_and(owner >= low // per, owner < -(-high // per))
            at = jnp.where(live, owner - first // per, 0)
            copy = pltpu.make_async_copy(
                src, buf.at[at, pl.ds(row, src.shape[0])], move.sems.at[move.used]
            )
            move.used += 1
            pl.when(live)(copy.start)
            self.waits.append((live, copy))
        self.rows = buf.reshape(buf.shape[0] * per, COUT)

    def wait(self):
        for live, copy in self.waits:
            if live is None:
                copy.wait()
            else:
                pl.when(live)(copy.wait)
        return self.rows


def make_assemble(groups):
    def body(*refs):
        *pieces, number_ref, whole_ref, buf, sems = refs
        move = Mover(sems)
        rows = Rows(move, pieces, number_ref, buf, 0, whole_ref.shape[0], groups).wait()
        move.store(rows, whole_ref)
        move.finish()

    return body


def make_first(sources):
    def body(*refs):
        x_ref, *one_refs = refs[: 1 + sources]
        number_ref, count_ref, y1_ref, ys_ref, st_ref, local_ref, xb, wb, yb, sems = refs[
            1 + sources :
        ]
        move = Mover(sems)
        lx = move.load(x_ref, xb)
        rows = Rows(move, one_refs, number_ref, wb, 0, 10 * CIN, NEAR_FAR)
        mask = mask_of(count_ref)
        lx.wait()
        wr = rows.wait()
        first_body(move, xb, wr, yb, mask, count_ref, y1_ref, ys_ref, st_ref, local_ref)

    return body


def first_body(move, xb, wb, yb, mask, count_ref, y1_ref, ys_ref, st_ref, local_ref):
    sums = [0.0, 0.0, 0.0, 0.0]
    for o in range(4):
        total = None
        for cell, tap, cells in first_pairs(o):
            part = dot(xb[:, pl.ds(cell * CIN, cells * CIN)], wb[pl.ds(tap * CIN, cells * CIN), :])
            total = part if total is None else total + part
        yb[0, :, columns(o)] = total
        move.store(yb.at[0, :, columns(o)], y1_ref.at[:, columns(o)])
        valid = total * mask
        sums[0] += column_sum(valid)
        sums[1] += column_sum(valid * total)
        cell = (o // 2) * 8 + (o % 2) * 2
        total = dot(xb[:, pl.ds(cell * CIN, CIN)], wb[pl.ds(9 * CIN, CIN), :])
        yb[1, :, columns(o)] = total
        move.store(yb.at[1, :, columns(o)], ys_ref.at[:, columns(o)])
        valid = total * mask
        sums[2] += column_sum(valid)
        sums[3] += column_sum(valid * total)
    counted = jnp.full((8, LANES), count_ref[0, 0].astype(f32), f32)
    spread(st_ref, jnp.concatenate([pack(sums[:2]), counted], axis=0))
    local_ref[...] = pack(sums[2:])
    move.finish()


def k_second(
    y1_ref, recv_ref, norm_ref, local_ref, one_ref, count_ref, side_ref,
    mine_ref, theirs_ref, y2_ref, st_ref, keep_ref,
    yin, ab, at, tb, wb, yb, sems,
):
    move = Mover(sems)
    ly = [move.load(y1_ref.at[:, columns(o)], yin.at[:, columns(o)]) for o in range(4)]
    lw = Taps(move, one_ref, 10 * CIN, wb, FORWARD)
    got = jnp.sum(recv_ref[...], axis=0)
    total = got[8:9, 0:1]
    positions = 4.0 * total
    centre, inverse = moments(channel_row(got, 0), channel_row(got, 1), positions)
    keep_ref[...] = jnp.concatenate(
        [centre, inverse, jnp.broadcast_to(positions, (1, COUT)), jnp.zeros((5, COUT), f32)], axis=0
    )
    scale = norm_ref[0, 0:1, :] * inverse
    offset = norm_ref[1, 0:1, :] - centre * scale
    mask = mask_of(count_ref)
    for o in range(4):
        ly[o].wait()
        v = yin[:, columns(o)] * scale + offset
        ab[:, columns(o)] = (v * sigmoid(v)).astype(bf16)
        split_turn(at, tb, ab[:, columns(o)], o, COUT)
    hand_out(move, at, side_ref, mine_ref, theirs_ref)
    sums = [0.0, 0.0]
    for o in range(4):
        y = forward_taps(ab, lw, o)
        yb[:, columns(o)] = y
        move.store(yb.at[:, columns(o)], y2_ref.at[:, columns(o)])
        valid = y * mask
        sums[0] += column_sum(valid)
        sums[1] += column_sum(valid * y)
    spread(st_ref, jnp.concatenate([pack(sums), local_ref[...]], axis=0))
    move.finish()


def make_third(sources):
    def body(*refs):
        third_body(refs[:sources], *refs[sources:])

    return body


def third_body(
    two_refs, number_ref, y2_ref, ys_ref, recv_ref, norm_ref, base_ref, count_ref, side_ref,
    h1_ref, mine_ref, theirs_ref, y3_ref, st_ref, keep_ref,
    yin, sin, hout, ab, at, tb, wb, yb, sems,
):
    move = Mover(sems)
    ly, ls = [], []
    for o in range(4):
        ly.append(move.load(y2_ref.at[:, columns(o)], yin.at[:, columns(o)]))
        ls.append(move.load(ys_ref.at[:, columns(o)], sin.at[:, columns(o)]))
    rows = Rows(move, two_refs, number_ref, wb, 0, 9 * COUT, LOW)
    got = jnp.sum(recv_ref[...], axis=0)
    positions = base_ref[2:3, :]
    c1, i1 = moments(channel_row(got, 0), channel_row(got, 1), positions)
    c2, i2 = moments(channel_row(got, 2), channel_row(got, 3), positions)
    keep_ref[...] = jnp.concatenate([c1, i1, c2, i2, jnp.zeros((4, COUT), f32)], axis=0)
    s1 = norm_ref[0, 1:2, :] * i1
    s2 = norm_ref[0, 2:3, :] * i2
    offset = norm_ref[1, 1:2, :] - c1 * s1 + (norm_ref[1, 2:3, :] - c2 * s2)
    mask = mask_of(count_ref)
    for o in range(4):
        ly[o].wait()
        ls[o].wait()
        v = yin[:, columns(o)] * s1 + sin[:, columns(o)] * s2 + offset
        h = v * sigmoid(v)
        hout[:, columns(o)] = h
        ab[:, columns(o)] = h.astype(bf16)
        move.store(hout.at[:, columns(o)], h1_ref.at[:, columns(o)])
        split_turn(at, tb, ab[:, columns(o)], o, COUT)
    hand_out(move, at, side_ref, mine_ref, theirs_ref)
    wr = rows.wait()
    sums = [0.0, 0.0]
    for o in range(4):
        y = forward_taps(ab, wr, o)
        yb[:, columns(o)] = y
        move.store(yb.at[:, columns(o)], y3_ref.at[:, columns(o)])
        valid = y * mask
        sums[0] += column_sum(valid)
        sums[1] += column_sum(valid * y)
    spread(st_ref, pack(sums))
    move.finish()


def k_fourth(
    y3_ref, recv_ref, norm_ref, base_ref, two_ref, count_ref, side_ref,
    mine_ref, theirs_ref, y4_ref, st_ref, keep_ref,
    yin, ab, at, tb, wb, yb, sems,
):
    move = Mover(sems)
    ly = [move.load(y3_ref.at[:, columns(o)], yin.at[:, columns(o)]) for o in range(4)]
    lw = Taps(move, two_ref, 9 * COUT, wb, FORWARD)
    got = jnp.sum(recv_ref[...], axis=0)
    centre, inverse = moments(channel_row(got, 0), channel_row(got, 1), base_ref[2:3, :])
    keep_ref[...] = jnp.concatenate([centre, inverse, jnp.zeros((6, COUT), f32)], axis=0)
    scale = norm_ref[0, 3:4, :] * inverse
    offset = norm_ref[1, 3:4, :] - centre * scale
    mask = mask_of(count_ref)
    for o in range(4):
        ly[o].wait()
        v = yin[:, columns(o)] * scale + offset
        ab[:, columns(o)] = (v * sigmoid(v)).astype(bf16)
        split_turn(at, tb, ab[:, columns(o)], o, COUT)
    hand_out(move, at, side_ref, mine_ref, theirs_ref)
    sums = [0.0, 0.0]
    for o in range(4):
        y = forward_taps(ab, lw, o)
        yb[:, columns(o)] = y
        move.store(yb.at[:, columns(o)], y4_ref.at[:, columns(o)])
        valid = y * mask
        sums[0] += column_sum(valid)
        sums[1] += column_sum(valid * y)
    spread(st_ref, pack(sums))
    move.finish()


def k_heads(
    y4_ref, h1_ref, recv_ref, norm_ref, base_ref, head_ref, bias_ref, labels_ref, count_ref,
    pooled_ref, resid_ref, slope_ref, gram_ref, part_ref, keep_ref,
    yin, hin, sb, sems,
):
    move = Mover(sems)
    ly, lh = [], []
    for o in range(4):
        ly.append(move.load(y4_ref.at[:, columns(o)], yin.at[:, columns(o)]))
        lh.append(move.load(h1_ref.at[:, columns(o)], hin.at[:, columns(o)]))
    got = jnp.sum(recv_ref[...], axis=0)
    centre, inverse = moments(channel_row(got, 0), channel_row(got, 1), base_ref[2:3, :])
    keep_ref[...] = jnp.concatenate([centre, inverse, jnp.zeros((6, COUT), f32)], axis=0)
    scale = norm_ref[0, 4:5, :] * inverse
    offset = norm_ref[1, 4:5, :] - centre * scale
    total = None
    for o in range(4):
        ly[o].wait()
        lh[o].wait()
        v = yin[:, columns(o)] * scale + offset + hin[:, columns(o)]
        s = sigmoid(v)
        h = v * s
        sb[:, columns(o)] = s * (1.0 + v - h)
        move.store(sb.at[:, columns(o)], slope_ref.at[:, columns(o)])
        total = h if total is None else total + h
    pooled = total * 0.25
    pooled_ref[...] = pooled
    logits = dot(pooled, head_ref[...], highest) + bias_ref[...]
    labels = labels_ref[...]
    valid = (lax.broadcasted_iota(jnp.int32, (CAP, LANES), 0) < count_ref[0, 0]).astype(f32)
    resid = (sigmoid(logits) - labels) * valid
    resid_ref[...] = resid
    softplus = jnp.maximum(logits, 0.0) + jnp.log1p(jnp.exp(-jnp.abs(logits)))
    losses = valid * (softplus - labels * logits)
    gram = dot_tn(resid, resid, highest)
    lane = lax.broadcasted_iota(jnp.int32, (16, LANES), 1)
    packed = jnp.where(lane < TASKS, gram[0:16], jnp.where(lane < 2 * TASKS, gram[16:32], gram[32:48]))
    spread(gram_ref, packed)
    part_ref[...] = jnp.zeros(part_ref.shape, f32)
    for b in range(4):
        part_ref[pl.ds(b * TASKS, TASKS), :] = dot_tn(
            resid, pooled[:, b * LANES : (b + 1) * LANES], highest
        )[0:TASKS]
    ones = jnp.ones((CAP, LANES), f32)
    lane = lax.broadcasted_iota(jnp.int32, (TASKS, LANES), 1)
    part_ref[pl.ds(4 * TASKS, TASKS), :] = jnp.where(
        lane == 0, dot_tn(resid, ones, highest)[0:TASKS], dot_tn(losses, ones, highest)[0:TASKS]
    )
    move.finish()


def k_weights(
    recv_ref, square_ref, resid_ref, turned_ref, base_ref, keep_ref, part_ref, y4_ref, slope_ref, count_ref,
    weights_ref, u2_ref, st_ref,
    yin, sin, ub, sems,
):
    move = Mover(sems)
    ly, ls = [], []
    for o in range(4):
        ly.append(move.load(y4_ref.at[:, columns(o)], yin.at[:, columns(o)]))
        ls.append(move.load(slope_ref.at[:, columns(o)], sin.at[:, columns(o)]))
    total = base_ref[2:3, 0:1] * 0.25
    got = jnp.sum(recv_ref[...], axis=0)
    gram = jnp.concatenate(
        [
            got,
            pltpu.roll(got, LANES - TASKS, 1),
            pltpu.roll(got, LANES - 2 * TASKS, 1)[0:8],
        ],
        axis=0,
    )
    row_at = lax.broadcasted_iota(jnp.int32, (TASKS, LANES), 0)
    lane_at = lax.broadcasted_iota(jnp.int32, (TASKS, LANES), 1)
    gram = jnp.where(lane_at < TASKS, gram * square_ref[...], 0.0) / total
    trace = jnp.sum(
        jnp.sum(jnp.where(row_at == lane_at, gram, 0.0), axis=0, keepdims=True), axis=1, keepdims=True
    )
    scaled = gram / (trace / TASKS + 1e-06)
    live = lax.broadcasted_iota(jnp.int32, (1, LANES), 1) < TASKS
    weights = jnp.where(live, 1.0 / TASKS, 0.0)
    row = jnp.sum(scaled, axis=0, keepdims=True) / TASKS
    col = jnp.sum(scaled, axis=1, keepdims=True) / TASKS
    for turn in range(FW_STEPS):
        gamma = 2.0 / (turn + 3.0)
        low = jnp.min(col, axis=0, keepdims=True)
        grown_col = jnp.exp((low - col) / softness)
        grown_row = jnp.where(live, jnp.exp(jnp.where(live, (low - row) / softness, 0.0)), 0.0)
        share = gamma / jnp.sum(grown_col, axis=0, keepdims=True)
        weights = (1.0 - gamma) * weights + share * grown_row
        if turn + 1 < FW_STEPS:
            next_row = jnp.sum(scaled * grown_col, axis=0, keepdims=True)
            next_col = jnp.sum(scaled * grown_row, axis=1, keepdims=True)
            row = (1.0 - gamma) * row + share * next_row
            col = (1.0 - gamma) * col + share * next_col
    weights_ref[...] = jnp.broadcast_to(weights, (8, LANES))
    pooled_grad = dot(resid_ref[...] * (weights / total), turned_ref[...], highest) * 0.25
    centre, inverse = keep_ref[0:1, :], keep_ref[1:2, :]
    mask = mask_of(count_ref)
    sums = [0.0, 0.0]
    for o in range(4):
        ly[o].wait()
        ls[o].wait()
        u = pooled_grad * sin[:, columns(o)]
        ub[:, columns(o)] = u
        move.store(ub.at[:, columns(o)], u2_ref.at[:, columns(o)])
        valid = u * mask
        sums[0] += column_sum(valid * ((yin[:, columns(o)] - centre) * inverse))
        sums[1] += column_sum(valid)
    st_ref[:, 0:8, :] = jnp.broadcast_to(pack(sums)[None], part_ref.shape)
    st_ref[:, 8:16, :] = part_ref[...]
    move.finish()


def reverse_norm(g, y, mask, centre, inverse, gain, scale_total, shift_total, positions):
    xhat = (y - centre) * inverse
    return (gain * inverse) * (g - mask * ((shift_total + xhat * scale_total) / positions))


def k_back_fourth(
    u2_ref, y4_ref, recv_ref, norm_ref, base_ref, keep4_ref, two_ref, y3_ref, keep3_ref, count_ref,
    dy0_ref, dy1_ref, dy2_ref, dy3_ref, u3_ref, st_ref, tot_ref,
    uin, yin, zin, db, wb, ub, sems,
):
    move = Mover(sems)
    lu, ly = [], []
    for o in range(4):
        lu.append(move.load(u2_ref.at[:, columns(o)], uin.at[:, columns(o)]))
        ly.append(move.load(y4_ref.at[:, columns(o)], yin.at[:, columns(o)]))
    lw = Taps(move, two_ref, 9 * COUT, wb, BACKWARD)
    lz = [move.load(y3_ref.at[:, columns(i)], zin.at[:, columns(i)]) for i in range(4)]
    got = jnp.sum(recv_ref[...], axis=0)
    tot_ref[...] = got[0:8]
    positions = base_ref[2:3, :]
    mask = mask_of(count_ref)
    scale_total, shift_total = channel_row(got, 0), channel_row(got, 1)
    for o in range(4):
        lu[o].wait()
        ly[o].wait()
        dy = reverse_norm(
            uin[:, columns(o)], yin[:, columns(o)], mask, keep4_ref[0:1, :], keep4_ref[1:2, :],
            norm_ref[0, 4:5, :], scale_total, shift_total, positions,
        )
        db[:, columns(o)] = dy.astype(bf16)
        move.store(db.at[:, columns(o)], (dy0_ref, dy1_ref, dy2_ref, dy3_ref)[o])
    centre, inverse = keep3_ref[0:1, :], keep3_ref[1:2, :]
    gain, shift = norm_ref[0, 3:4, :], norm_ref[1, 3:4, :]
    sums = [0.0, 0.0]
    for i in range(4):
        grad = backward_taps(db, lw, i)
        lz[i].wait()
        xhat = (zin[:, columns(i)] - centre) * inverse
        v = xhat * gain + shift
        s = sigmoid(v)
        u = grad * (s * (1.0 + v * (1.0 - s)))
        ub[:, columns(i)] = u
        move.store(ub.at[:, columns(i)], u3_ref.at[:, columns(i)])
        valid = u * mask
        sums[0] += column_sum(valid * xhat)
        sums[1] += column_sum(valid)
    spread(st_ref, jnp.concatenate([pack(sums), got[8:16]], axis=0))
    move.finish()


def k_back_third(
    u3_ref, y3_ref, recv_ref, norm_ref, base_ref, keep3_ref, two_ref, u2_ref, y2_ref, ys_ref, keep12_ref, count_ref,
    dy0_ref, dy1_ref, dy2_ref, dy3_ref, u1_ref, st_ref, tot_ref, head_ref,
    uin, yin, u2in, y2in, ysin, db, wb, ub, sems,
):
    move = Mover(sems)
    lu, ly = [], []
    for o in range(4):
        lu.append(move.load(u3_ref.at[:, columns(o)], uin.at[:, columns(o)]))
        ly.append(move.load(y3_ref.at[:, columns(o)], yin.at[:, columns(o)]))
    lw = Taps(move, two_ref, 0, wb, BACKWARD)
    later = [
        [
            move.load(ref.at[:, columns(i)], buf.at[:, columns(i)])
            for ref, buf in ((u2_ref, u2in), (y2_ref, y2in), (ys_ref, ysin))
        ]
        for i in range(4)
    ]
    got = jnp.sum(recv_ref[:, 0:8, :], axis=0)
    tot_ref[...] = got
    head_ref[...] = recv_ref[:, 8:16, :]
    positions = base_ref[2:3, :]
    mask = mask_of(count_ref)
    scale_total, shift_total = channel_row(got, 0), channel_row(got, 1)
    for o in range(4):
        lu[o].wait()
        ly[o].wait()
        dy = reverse_norm(
            uin[:, columns(o)], yin[:, columns(o)], mask, keep3_ref[0:1, :], keep3_ref[1:2, :],
            norm_ref[0, 3:4, :], scale_total, shift_total, positions,
        )
        db[:, columns(o)] = dy.astype(bf16)
        move.store(db.at[:, columns(o)], (dy0_ref, dy1_ref, dy2_ref, dy3_ref)[o])
    c1, i1, c2, i2 = (keep12_ref[k : k + 1, :] for k in range(4))
    g1, g2 = norm_ref[0, 1:2, :], norm_ref[0, 2:3, :]
    shift = norm_ref[1, 1:2, :] + norm_ref[1, 2:3, :]
    sums = [0.0, 0.0, 0.0]
    for i in range(4):
        grad = backward_taps(db, lw, i)
        for copy in later[i]:
            copy.wait()
        grad = grad + u2in[:, columns(i)]
        x1 = (y2in[:, columns(i)] - c1) * i1
        x2 = (ysin[:, columns(i)] - c2) * i2
        v = x1 * g1 + x2 * g2 + shift
        s = sigmoid(v)
        u = grad * (s * (1.0 + v * (1.0 - s)))
        ub[:, columns(i)] = u
        move.store(ub.at[:, columns(i)], u1_ref.at[:, columns(i)])
        valid = u * mask
        sums[0] += column_sum(valid * x1)
        sums[1] += column_sum(valid * x2)
        sums[2] += column_sum(valid)
    spread(st_ref, pack(sums))
    move.finish()


def k_back_second(
    u1_ref, y2_ref, ys_ref, recv_ref, norm_ref, base_ref, keep12_ref, one_ref, y1_ref, count_ref,
    dy0_ref, dy1_ref, dy2_ref, dy3_ref, dys_ref, u0_ref, st_ref, tot_ref,
    uin, y2in, ysin, y1in, db, dsb, wb, ub, sems,
):
    move = Mover(sems)
    first = []
    for o in range(4):
        first.append(
            [
                move.load(ref.at[:, columns(o)], buf.at[:, columns(o)])
                for ref, buf in ((u1_ref, uin), (y2_ref, y2in), (ys_ref, ysin))
            ]
        )
    lw = Taps(move, one_ref, 10 * CIN, wb, BACKWARD)
    ly1 = [move.load(y1_ref.at[:, columns(i)], y1in.at[:, columns(i)]) for i in range(4)]
    got = jnp.sum(recv_ref[...], axis=0)
    tot_ref[...] = got
    positions = base_ref[2:3, :]
    mask = mask_of(count_ref)
    scale1, scale2, shift_total = (channel_row(got, k) for k in range(3))
    c1, i1, c2, i2 = (keep12_ref[k : k + 1, :] for k in range(4))
    for o in range(4):
        for copy in first[o]:
            copy.wait()
        u = uin[:, columns(o)]
        dy2 = reverse_norm(
            u, y2in[:, columns(o)], mask, c1, i1, norm_ref[0, 1:2, :], scale1, shift_total, positions
        )
        db[:, columns(o)] = dy2.astype(bf16)
        move.store(db.at[:, columns(o)], (dy0_ref, dy1_ref, dy2_ref, dy3_ref)[o])
        dys = reverse_norm(
            u, ysin[:, columns(o)], mask, c2, i2, norm_ref[0, 2:3, :], scale2, shift_total, positions
        )
        dsb[:, columns(o)] = dys.astype(bf16)
        move.store(dsb.at[:, columns(o)], dys_ref.at[:, columns(o)])
    centre, inverse = base_ref[0:1, :], base_ref[1:2, :]
    gain, shift = norm_ref[0, 0:1, :], norm_ref[1, 0:1, :]
    sums = [0.0, 0.0]
    for i in range(4):
        grad = backward_taps(db, lw, i)
        ly1[i].wait()
        xhat = (y1in[:, columns(i)] - centre) * inverse
        v = xhat * gain + shift
        s = sigmoid(v)
        u = grad * (s * (1.0 + v * (1.0 - s)))
        ub[:, columns(i)] = u
        move.store(ub.at[:, columns(i)], u0_ref.at[:, columns(i)])
        valid = u * mask
        sums[0] += column_sum(valid * xhat)
        sums[1] += column_sum(valid)
    spread(st_ref, pack(sums))
    move.finish()


def k_back_first(
    u0_ref, y1_ref, recv_ref, norm_ref, base_ref, count_ref,
    dy_ref, tot_ref, uin, yin, db, sems,
):
    move = Mover(sems)
    lu, ly = [], []
    for o in range(4):
        lu.append(move.load(u0_ref.at[:, columns(o)], uin.at[:, columns(o)]))
        ly.append(move.load(y1_ref.at[:, columns(o)], yin.at[:, columns(o)]))
    got = jnp.sum(recv_ref[...], axis=0)
    tot_ref[...] = got
    positions = base_ref[2:3, :]
    mask = mask_of(count_ref)
    scale_total, shift_total = channel_row(got, 0), channel_row(got, 1)
    for o in range(4):
        lu[o].wait()
        ly[o].wait()
        dy = reverse_norm(
            uin[:, columns(o)], yin[:, columns(o)], mask, base_ref[0:1, :], base_ref[1:2, :],
            norm_ref[0, 0:1, :], scale_total, shift_total, positions,
        )
        db[:, columns(o)] = dy.astype(bf16)
        move.store(db.at[:, columns(o)], dy_ref.at[:, columns(o)])
    move.finish()


def k_turn(x_ref, side_ref, mine_ref, theirs_ref, xb, at, tb, sems):
    move = Mover(sems)
    loads = [
        move.load(x_ref.at[:, columns(o)], xb.at[:, columns(o)]) for o in range(16 * CIN // COUT)
    ]
    for cell in range(16):
        if cell % 2 == 0:
            loads[cell // 2].wait()
        split_turn(at, tb, xb[:, pl.ds(cell * CIN, CIN)], cell, CIN)
    hand_out(move, at, side_ref, mine_ref, theirs_ref)
    move.finish()


def pair_taps(lefts, rights, gb, base, half, side_in, stride, ready=None):
    for tap in range(9):
        total = None
        for o in range(4):
            row_in = stride * (o // 2) + tap // 3 - 1
            col_in = stride * (o % 2) + tap % 3 - 1
            if not (0 <= row_in < side_in and 0 <= col_in < side_in):
                continue
            cell = row_in * side_in + col_in
            for left, right in zip(lefts, rights):
                part = dot(left[pl.ds(cell * half, half), :], right[:, columns(o)])
                total = part if total is None else total + part
        gb[pl.ds(base + tap * half, half), :] = total.astype(bf16)
        if ready is not None:
            ready(base + (tap + 1) * half)


class Halves:
    def __init__(self, move, gb, place_ref, outs, first_row=0):
        self.move, self.gb, self.outs = move, gb, outs
        self.x, self.y = place_ref[0, 1], place_ref[0, 2]
        self.done, self.first_row = 0, first_row

    def choose(self, src, keep, kept, sent):
        move = self.move
        sem = move.sems.at[move.used]
        move.used += 1
        pl.when(keep)(pltpu.make_async_copy(src, kept, sem).start)
        pl.when(jnp.logical_not(keep))(pltpu.make_async_copy(src, sent, sem).start)
        move.out.append(pltpu.make_async_copy(src, kept, sem))

    def ready(self, rows):
        left_keep, left_send, right_keep, right_send = self.outs
        half = COUT // 2
        blocks, per, _ = self.gb.shape
        while self.done < blocks and self.first_row + (self.done + 1) * per <= rows:
            z, y, x = self.done // 4, self.done // 2 % 2, self.done % 2
            src = self.gb.at[self.done]
            self.choose(
                src.at[:, pl.ds(0, half)], self.x == x, left_keep.at[z, y], left_send.at[z, y]
            )
            self.choose(
                src.at[:, pl.ds(half, half)], self.y == y, right_keep.at[z, x], right_send.at[z, x]
            )
            self.done += 1


def load_all(move, pairs):
    loads = [move.load(src, dst) for src, dst in pairs]
    for copy in loads:
        copy.wait()


def side_by_side(refs, buf):
    return [(ref, buf.at[:, columns(o)]) for o, ref in enumerate(refs)]


class Taker:
    def __init__(self, refs):
        self.refs = list(refs)

    def __call__(self, count):
        taken, self.refs = self.refs[:count], self.refs[count:]
        return taken


def make_pair_grad(outputs):
    def body(*refs):
        take = Taker(refs)
        (mine_ref, got_ref), dy_refs, dyg_refs, (place_ref,) = take(2), take(4), take(4), take(1)
        outs, (mb, ob, db, dgb, gb, sems) = take(outputs), take(6)
        move = Mover(sems)
        load_all(
            move,
            ((mine_ref, mb), *side_by_side(dy_refs, db), (got_ref, ob), *side_by_side(dyg_refs, dgb)),
        )
        rows = gb.reshape(9 * COUT // 2, COUT)
        ready = Halves(move, gb, place_ref, outs).ready if len(outs) == 4 else None
        pair_taps((mb, ob), (db, dgb), rows, 0, COUT // 2, 2, 1, ready)
        if ready is None:
            move.store(rows, outs[0])
        move.finish()

    return body


def make_pair_second():
    return lambda *refs: pair_second_body(Taker(refs))


def pair_second_body(take):
    (mine_ref, got_ref), dy_refs, dyg_refs = take(2), take(4), take(4)
    xm_ref, xt_ref, dys_ref, place_ref, late_ref, other_ref = take(6)
    *outs, mb, ob, db, dgb, gb, xmb, xtb, dsb, other, sems = take.refs
    move = Mover(sems)
    half = CIN // 2
    later = [move.load(dys_ref, dsb)]
    for o in range(4):
        cell = (o // 2) * 8 + (o % 2) * 2
        for src, dst in ((xm_ref, xmb), (xt_ref, xtb)):
            later.append(move.load(src.at[pl.ds(cell * half, half)], dst.at[pl.ds(o * half, half)]))
    load_all(
        move,
        ((mine_ref, mb), *side_by_side(dy_refs, db), (got_ref, ob), *side_by_side(dyg_refs, dgb)),
    )
    late_rows = late_ref.shape[0]
    ready = None
    if outs:
        blocks, per = outs[0].shape[0] * 4, gb.shape[1]
        rows = gb.reshape(gb.shape[0] * per, COUT)
        start = gb.shape[0] * per - blocks * per
        ready = Halves(move, gb.at[pl.ds(gb.shape[0] - blocks, blocks)], place_ref, outs, start).ready
        base = start - late_rows
    else:
        rows, base = gb, 0
    pair_taps((mb, ob), (db, dgb), rows, base + half, COUT // 2, 2, 1, ready)
    for copy in later:
        copy.wait()
    for left, out in ((xmb, rows.at[pl.ds(base, half)]), (xtb, other)):
        total = None
        for o in range(4):
            part = dot(left[pl.ds(o * half, half), :], dsb[:, columns(o)])
            total = part if total is None else total + part
        out[...] = total.astype(bf16)
    move.store(rows.at[pl.ds(base, late_rows)], late_ref)
    move.store(other, other_ref)
    move.finish()


def k_pair_first(*refs):
    take = Taker(refs)
    xm_ref, xg_ref, dy_ref, dyg_ref, late_ref, other_ref, place_ref = take(7)
    *outs, mb, ob, db, dgb, gb, other, sems = take.refs
    move = Mover(sems)
    half = CIN // 2
    rows = gb.reshape(gb.shape[0] * gb.shape[1], COUT)
    late = [
        move.load(late_ref, rows.at[pl.ds(9 * half, late_ref.shape[0])]),
        move.load(other_ref, other),
    ]
    load_all(move, ((xm_ref, mb), (dy_ref, db), (xg_ref, ob), (dyg_ref, dgb)))
    for copy in late:
        copy.wait()
    short = pl.ds(9 * half, half)
    rows[short, :] = plus(rows[short, :], other[...])
    ready = Halves(move, gb, place_ref, outs).ready if len(outs) == 4 else None
    pair_taps((mb, ob), (db, dgb), rows, 0, half, 4, 2, ready)
    if ready is None:
        move.store(rows, outs[0])
    else:
        ready(gb.shape[0] * gb.shape[1])
    move.finish()


def plus(left, right):
    return (left.astype(f32) + right.astype(f32)).astype(bf16)


def k_merge(*refs):
    *parts, place_ref, lk2_ref, ls2_ref, rk2_ref, rs2_ref = refs
    x, y = place_ref[0, 1], place_ref[0, 2]
    at = 0
    for k in range(0, len(parts), 4):
        lk_ref, lg_ref, rk_ref, rg_ref = parts[k : k + 4]
        for z in range(lk_ref.shape[0]):
            lk2_ref[at] = plus(lk_ref[z, y], lg_ref[z, y])
            ls2_ref[at] = plus(lk_ref[z, 1 - y], lg_ref[z, 1 - y])
            rk2_ref[at] = plus(rk_ref[z, x], rg_ref[z, x])
            rs2_ref[at] = plus(rk_ref[z, 1 - x], rg_ref[z, 1 - x])
            at += 1


def k_line(*refs):
    *parts, place_ref, own_ref, s1_ref, s2_ref, s3_ref, held = refs
    z_here = place_ref[0, 3]
    half = COUT // 2
    at = 0
    for k in range(0, len(parts), 4):
        lk_ref, lg_ref, rk_ref, rg_ref = parts[k : k + 4]
        for z in range(lk_ref.shape[0]):
            held[at, :, 0:half] = plus(lk_ref[z], lg_ref[z])
            held[at, :, half:COUT] = plus(rk_ref[z], rg_ref[z])
            at += 1
    own_ref[...] = held[z_here]
    for other, ref in ((1, s1_ref), (2, s2_ref), (3, s3_ref)):
        ref[...] = held[jnp.bitwise_xor(z_here, other)]


def k_side(own_ref, g1_ref, g2_ref, g3_ref, place_ref, keep_ref, send_ref):
    side = place_ref[0, 0]

    def total(at):
        return (own_ref[at].astype(f32) + g1_ref[at].astype(f32)) + (
            g2_ref[at].astype(f32) + g3_ref[at].astype(f32)
        )

    keep_ref[...] = total(side)
    send_ref[...] = total(1 - side).astype(bf16)


def make_update(rate):
    def body(
        keep_ref, got_ref, place_ref, master_ref, momentum_ref, average_ref,
        moment_ref, weight_ref, mean_ref, copy_ref,
    ):
        lower = place_ref[0, 0] == 0
        for group in range(keep_ref.shape[0] // 16):
            here = keep_ref[pl.ds(16 * group, 16), :]
            there = got_ref[pl.ds(16 * group, 16), :].astype(f32)
            for parity in range(2):
                at = pl.ds(32 * group + 16 * parity, 16)
                grad = jnp.where(lower, here, there) if parity == 0 else jnp.where(lower, there, here)
                moment, fresh, mean = nesterov(
                    grad, master_ref[at, :], momentum_ref[at, :], average_ref[at, :], rate
                )
                moment_ref[at, :] = moment
                weight_ref[at, :] = fresh
                mean_ref[at, :] = mean
                copy_ref[at, :] = fresh.astype(bf16)

    return body


def k_stack(*refs):
    *parts, value_ref, here_ref, out_ref = refs
    for z, ref in enumerate(parts):
        here_ref[z] = ref[...]
    out_ref[...] = value_ref[...].astype(bf16)


def k_pick(own_ref, r1_ref, r2_ref, r3_ref, place_ref, low_ref, high_ref):
    z_here = place_ref[0, 3]
    for z in range(4):
        out, at = (low_ref, z) if z < 2 else (high_ref, z - 2)
        for other, ref in enumerate((own_ref, r1_ref, r2_ref, r3_ref)):

            def copy(ref=ref, out=out, at=at):
                out[at] = ref[...]

            pl.when(jnp.bitwise_xor(z_here, z) == other)(copy)


def k_cut(over_x_ref, over_y_ref, lower_ref, upper_ref):
    rows = upper_ref.shape[1]
    lower_ref[...] = over_x_ref[:, rows:, :]
    upper_ref[...] = over_y_ref[:, :rows, :]


def k_input_grad(dy_ref, dys_ref, one_ref, dx_ref, db, dsb, wb, xb, sems):
    move = Mover(sems)
    loads = [
        move.load(one_ref.at[pl.ds(0, 10 * CIN)], wb),
        move.load(dy_ref, db),
        move.load(dys_ref, dsb),
    ]
    for copy in loads:
        copy.wait()
    for cell in range(16):
        row_in, col_in = divmod(cell, 4)
        total = None
        for o in range(4):
            row_tap, col_tap = row_in - 2 * (o // 2) + 1, col_in - 2 * (o % 2) + 1
            if not (0 <= row_tap < 3 and 0 <= col_tap < 3):
                continue
            part = dot_nt(db[:, columns(o)], wb[pl.ds((row_tap * 3 + col_tap) * CIN, CIN), :])
            total = part if total is None else total + part
        if row_in % 2 == 0 and col_in % 2 == 0:
            o = (row_in // 2) * 2 + col_in // 2
            total = total + dot_nt(dsb[:, columns(o)], wb[pl.ds(9 * CIN, CIN), :])
        xb[:, pl.ds(cell * CIN, CIN)] = total
        move.store(xb.at[:, pl.ds(cell * CIN, CIN)], dx_ref.at[:, pl.ds(cell * CIN, CIN)])
    move.finish()


def nesterov(grad, master, momentum, average, rate):
    moment = momentum_decay * momentum + grad
    fresh = master - rate * (grad + momentum_decay * moment)
    return (moment, fresh, average_decay * average + (1.0 - average_decay) * fresh)


def exchange(packed):
    return lax.all_to_all(packed, AXES, 0, 0, tiled=True)


def swap(value, devices, bits):
    return lax.ppermute(value, AXES, [(i, i ^ bits) for i in range(devices)])


class Grid:
    def __init__(self, devices, number):
        self.devices = devices
        parts = (number % 2, (number // 2) % 2, (number // 4) % 2, number // 8)
        self.place = jnp.stack(parts).astype(jnp.int32).reshape(1, 4)

    def swap(self, value, bits):
        return swap(value, self.devices, bits)


def stack(parts, value, after):
    return run(
        k_stack,
        (*parts, value),
        [VMEM] * (len(parts) + 1),
        [shape((len(parts), *parts[0].shape), bf16), shape(value.shape, bf16)],
        [VMEM] * 2,
        [],
        moved=1_000_000,
        name="stack",
        after=after,
    )


def cut(grid, over, after):
    parts, rows, _ = over[0].shape
    return run(
        k_cut,
        over,
        [VMEM] * 2,
        [shape((parts, rows // 2, COUT), bf16)] * 2,
        [VMEM] * 2,
        [],
        moved=1_000_000,
        name="cut",
        after=after,
    )


def gather_pieces(grid, here, over_x, over_y, cut=None):
    rows = here.shape[1] // 2
    lower, upper = cut or (over_x[:, rows:], over_y[:, :rows])
    own = [here, over_x, over_y, grid.swap(upper, 2), grid.swap(lower, 4)]
    return own + [grid.swap(v, 1) for v in own]


def assemble(pieces, number, held, groups, after):
    devices, rows, _ = held.shape
    return run(
        make_assemble(groups),
        (*pieces, number),
        [HBM] * len(pieces) + [SMEM],
        shape((devices * rows, COUT), bf16),
        HBM,
        [held, pltpu.SemaphoreType.DMA((41,))],
        moved=1_000_000,
        name="assemble",
        after=after,
    )


def scatter_first(grid, halves):
    left_keep, left_send, right_keep, right_send = halves
    return left_keep, grid.swap(left_send, 2), right_keep, grid.swap(right_send, 4)


def scatter_second(grid, halves):
    left_keep, left_send, right_keep, right_send = halves
    return left_keep, grid.swap(left_send, 4), right_keep, grid.swap(right_send, 2)


def merge(grid, parts, after=()):
    arrays = [v for part in parts for v in part]
    _, _, rows, half = arrays[0].shape
    nz = sum(part[0].shape[0] for part in parts)
    return run(
        k_merge,
        (*arrays, grid.place),
        [VMEM] * len(arrays) + [SMEM],
        [shape((nz, rows, half), bf16)] * 4,
        [VMEM] * 4,
        [],
        moved=1_000_000,
        name="merge",
        after=after,
    )


def line(grid, parts, after):
    rows = parts[0].shape[1]
    own, s1, s2, s3 = run(
        k_line,
        (*parts, grid.place),
        [VMEM] * len(parts) + [SMEM],
        [shape((rows, COUT), bf16)] * 4,
        [VMEM] * 4,
        [pltpu.VMEM((4, rows, COUT), bf16)],
        moved=1_000_000,
        name="line",
        after=after,
    )
    return own, grid.swap(s1, 8), grid.swap(s2, 16), grid.swap(s3, 24)


def sides(grid, parts, after=()):
    rows = parts[0].shape[0] // 2
    keep, send = run(
        k_side,
        (*(v.reshape(2, rows, COUT) for v in parts), grid.place),
        [VMEM] * 4 + [SMEM],
        [shape((rows, COUT), f32), shape((rows, COUT), bf16)],
        [VMEM] * 2,
        [],
        moved=1_000_000,
        name="sides",
        after=after,
    )
    return keep, grid.swap(send, 1)


def update(grid, parts, states, rate, after=()):
    kept = shape(states[0].shape, f32)
    return run(
        make_update(rate),
        (*parts, grid.place, *states),
        [VMEM, VMEM, SMEM, VMEM, VMEM, VMEM],
        [kept, kept, kept, shape(states[0].shape, bf16)],
        [VMEM] * 4,
        [],
        moved=1_000_000,
        name="update",
        after=after,
    )


def reduce_halves(devices, side, half_grad):
    groups = half_grad.reshape(-1, 16, COUT)
    empty = jnp.zeros_like(groups)
    full = jnp.stack(
        [jnp.where(side == 0, groups, empty), jnp.where(side == 0, empty, groups)], axis=1
    ).reshape(-1, COUT)
    return lax.psum_scatter(full, AXES, scatter_dimension=0, tiled=True).astype(f32)


def make_shards(devices, fast):
    def shards(
        features,
        labels,
        image_counts,
        block_one_master,
        block_one_momentum,
        block_one_average,
        block_two_master,
        block_two_momentum,
        block_two_average,
        norm_params,
        norm_momentum,
        norm_average,
        head_params,
        head_momentum,
        head_average,
    ):
        images_all = CAP * devices
        count = image_counts
        side = (lax.axis_index("pass") % 2).astype(jnp.int32).reshape(1, 1)
        number = lax.axis_index("batch") * lax.axis_size("pass") + lax.axis_index("pass")
        number = number.astype(jnp.int32)
        grid = Grid(devices, number) if fast else None
        number = number.reshape(1, 1)
        place = grid.place if fast else number
        shard = block_one_master.astype(bf16)
        x = features.reshape(CAP, 16 * CIN)

        rows_one, rows_two = devices * shard.shape[0], devices * block_two_master.shape[0]
        wide_f, wide_b = shape((CAP, WIDE), f32), shape((CAP, WIDE), bf16)
        wf, wb16 = pltpu.VMEM((CAP, WIDE), f32), pltpu.VMEM((CAP, WIDE), bf16)
        weight = pltpu.VMEM((9 * COUT, COUT), bf16)
        small = shape((8, COUT), f32)
        packed8, packed16 = shape((8, LANES), f32), shape((16, LANES), f32)
        send8, send16 = shape((devices, 8, LANES), f32), shape((devices, 16, LANES), f32)

        def sems(n):
            return pltpu.SemaphoreType.DMA((n,))

        conv_flops = 2 * 16 * CAP * COUT * COUT
        first_flops = 2 * 29 * CAP * CIN * COUT
        head_rows = head_params[:COUT]
        pad = LANES - 3 * TASKS

        def thrice(v):
            return jnp.concatenate([v, v, v, jnp.zeros((v.shape[0], pad), v.dtype)], axis=1)

        head_wide = thrice(head_rows)
        bias_wide = thrice(head_params[COUT:])
        labels_wide = thrice(labels.astype(f32))
        turned = jnp.pad(head_rows.T, ((0, LANES - TASKS), (0, 0)))
        square = jnp.pad(
            jnp.dot(head_rows.T, head_rows, precision=highest), ((0, 0), (0, LANES - TASKS))
        )

        turned_half = shape((WIDE // 2, CAP), bf16)
        turn_scratch = [pltpu.VMEM((2, WIDE // 2, CAP), bf16), pltpu.VMEM((COUT, CAP), bf16)]

        def sibling(value):
            return swap(value, devices, 1)

        x_mine, x_theirs = run(
            k_turn,
            (x, side),
            [HBM, SMEM],
            [shape((8 * CIN, CAP), bf16)] * 2,
            [HBM, HBM],
            [
                pltpu.VMEM((CAP, 16 * CIN), bf16),
                pltpu.VMEM((2, 8 * CIN, CAP), bf16),
                pltpu.VMEM((COUT, CAP), bf16),
                sems(19),
            ],
            0,
            4_000_000,
            name="turn_features",
        )
        x_got = sibling(x_theirs)
        if fast:
            far = [grid.swap(shard, 8 * other) for other in (1, 2, 3)]
            here, shard_two = stack((shard, *far), block_two_master, (x_mine,))
            one = far = gather_pieces(grid, here, grid.swap(here, 2), grid.swap(here, 4))
            low, high = run(
                k_pick,
                (
                    shard_two,
                    *(grid.swap(shard_two, 8 * other) for other in (1, 2, 3)),
                    grid.place,
                ),
                [VMEM] * 4 + [SMEM],
                [shape((2, *shard_two.shape), bf16)] * 2,
                [VMEM] * 2,
                [],
                moved=1_000_000,
                name="pick",
                after=(far[3], far[4]),
            )
            over_low = grid.swap(low, 2), grid.swap(low, 4)
            held = pltpu.VMEM((devices, *shard.shape), bf16)
            held_two = pltpu.VMEM((devices // 2, *shard_two.shape), bf16)
            whole_two = pltpu.VMEM((devices, *shard_two.shape), bf16)
            first_after = (x_mine, low)
        else:
            one = [lax.all_gather(shard, AXES, axis=0, tiled=True)]
            two = [lax.all_gather(block_two_master.astype(bf16), AXES, axis=0, tiled=True)]
            held = pltpu.VMEM((devices * shard.shape[0], COUT), bf16)
            held_two = weight
            first_after = (x_mine,)
            second_after = third_after = ()
        y1, ys, st, local = run(
            make_first(len(one)),
            (x, *one, number, count),
            [HBM] * (1 + len(one)) + [SMEM, SMEM],
            [wide_f, wide_f, send16, packed8],
            [HBM, HBM, VMEM, VMEM],
            [
                pltpu.VMEM((CAP, 16 * CIN), bf16),
                held,
                pltpu.VMEM((2, CAP, WIDE), f32),
                sems(50),
            ],
            first_flops,
            9_000_000,
            name="first_conv",
            after=first_after,
        )
        if fast:
            cut_low = cut(grid, over_low, (y1,))
            second_after = cut_low[:1]
            two = gather_pieces(grid, low, *over_low, cut_low)
            over_high = grid.swap(high, 2), grid.swap(high, 4)
        got = exchange(st)
        w_one = assemble(one, number, held, NEAR_FAR, (y1,)) if fast else one[0]
        a1_mine, a1_theirs, y2, st, keep0 = run(
            k_second,
            (y1, got, norm_params, local, w_one, count, side),
            [HBM, VMEM, VMEM, VMEM, HBM, SMEM, SMEM],
            [turned_half, turned_half, wide_f, send16, small],
            [HBM, HBM, HBM, VMEM, VMEM],
            [wf, wb16, *turn_scratch, weight, wf, sems(20)],
            conv_flops,
            10_000_000,
            name="second_conv",
            after=second_after,
        )
        if fast:
            cut_high = cut(grid, over_high, (y2,))
            third_after = cut_high[:1]
            two_high = gather_pieces(grid, high, *over_high, cut_high)
        got = exchange(st)
        a1_got = sibling(a1_theirs)
        h1, hb_mine, hb_theirs, y3, st, keep12 = run(
            make_third(len(two)),
            (*two, number, y2, ys, got, norm_params, keep0, count, side),
            [HBM] * len(two) + [SMEM, HBM, HBM, VMEM, VMEM, VMEM, SMEM, SMEM],
            [wide_f, turned_half, turned_half, wide_f, send8, small],
            [HBM, HBM, HBM, HBM, VMEM, VMEM],
            [wf, wf, wf, wb16, *turn_scratch, held_two, wf, sems(58)],
            conv_flops,
            14_000_000,
            name="third_conv",
            after=(*third_after, a1_got),
        )
        got = exchange(st)
        w_two = assemble(two + two_high, number, whole_two, LOW_HIGH, (y3,)) if fast else two[0]
        hb_got = sibling(hb_theirs)
        a3_mine, a3_theirs, y4, st, keep3 = run(
            k_fourth,
            (y3, got, norm_params, keep0, w_two, count, side),
            [HBM, VMEM, VMEM, VMEM, HBM, SMEM, SMEM],
            [turned_half, turned_half, wide_f, send8, small],
            [HBM, HBM, HBM, VMEM, VMEM],
            [wf, wb16, *turn_scratch, weight, wf, sems(20)],
            conv_flops,
            10_000_000,
            name="fourth_conv",
            after=(hb_got,),
        )
        got = exchange(st)
        a3_got = sibling(a3_theirs)
        wide_lanes = shape((CAP, LANES), f32)
        pooled, resid, slope, st, part, keep4 = run(
            k_heads,
            (y4, h1, got, norm_params, keep0, head_wide, bias_wide, labels_wide, count),
            [HBM, HBM, VMEM, VMEM, VMEM, VMEM, VMEM, VMEM, SMEM],
            [
                shape((CAP, COUT), f32),
                wide_lanes,
                wide_f,
                send16,
                shape((8 * devices, LANES), f32),
                small,
            ],
            [VMEM, VMEM, HBM, VMEM, VMEM, VMEM],
            [wf, wf, wf, sems(21)],
            1_000_000_000,
            7_000_000,
            name="heads",
            after=(a3_got,),
        )
        got = exchange(st)
        weights, u2, st = run(
            k_weights,
            (
                got, square, resid, turned, keep0, keep4, part.reshape(devices, 8, LANES), y4, slope, count,
            ),
            [VMEM, VMEM, VMEM, VMEM, VMEM, VMEM, VMEM, HBM, HBM, SMEM],
            [packed8, wide_f, send16],
            [VMEM, HBM, VMEM],
            [wf, wf, wf, sems(21)],
            1_000_000_000,
            7_000_000,
            name="task_weights",
        )

        got = exchange(st)
        narrow = [shape((CAP, COUT), bf16)] * 4
        *dy4, u3, st, tot4 = run(
            k_back_fourth,
            (u2, y4, got, norm_params, keep0, keep4, w_two, y3, keep3, count),
            [HBM, HBM, VMEM, VMEM, VMEM, VMEM, HBM, HBM, VMEM, SMEM],
            [*narrow, wide_f, send16, packed8],
            [HBM] * 5 + [VMEM, VMEM],
            [wf, wf, wf, wb16, weight, wf, sems(30)],
            conv_flops,
            14_000_000,
            name="fourth_back",
        )
        got = exchange(st)
        half_rows = 9 * COUT // 2
        half_turned = pltpu.VMEM((WIDE // 2, CAP), bf16)
        pair_scratch = [half_turned, half_turned, wb16, wb16]
        part_two, part_one = rows_two // devices, rows_one // devices

        def halves_of(nz, rows):
            if not fast:
                return shape((half_rows, COUT), bf16), HBM
            return [shape((nz, 2, rows, COUT // 2), bf16)] * 4, [HBM] * 4

        def siblings(values):
            return [sibling(v) for v in values]

        def pair_grad(mine, theirs, dy, dy_got, name, after=()):
            outs, out_specs = halves_of(2, part_two)
            blocks = (8, part_two, COUT) if fast else (1, half_rows, COUT)
            return run(
                make_pair_grad(4 if fast else 1),
                (mine, theirs, *dy, *dy_got, place),
                [HBM] * 10 + [SMEM],
                outs,
                out_specs,
                [*pair_scratch, pltpu.VMEM(blocks, bf16), sems(45)],
                conv_flops,
                6_000_000,
                name=name,
                after=after,
            )

        def ties(value):
            return (value[0],) if fast else (value,)

        grads_four = pair_grad(a3_mine, a3_got, dy4, siblings(dy4), "fourth_weights")
        if fast:
            first_four = scatter_first(grid, grads_four)
        *dy3, u1, st, tot3, head_sum = run(
            k_back_third,
            (u3, y3, got, norm_params, keep0, keep3, w_two, u2, y2, ys, keep12, count),
            [HBM, HBM, VMEM, VMEM, VMEM, VMEM, HBM, HBM, HBM, HBM, VMEM, SMEM],
            [*narrow, wide_f, send16, packed8, send8],
            [HBM] * 5 + [VMEM, VMEM, VMEM],
            [wf, wf, wf, wf, wf, wb16, weight, wf, sems(38)],
            conv_flops,
            18_000_000,
            name="third_back",
            share=1,
            after=ties(grads_four),
        )
        got = exchange(st)
        tie = first_four[1::2] if fast else ()
        grads_three = pair_grad(hb_mine, hb_got, dy3, siblings(dy3), "third_weights", tie)
        if fast:
            first_three = scatter_first(grid, grads_three)
        tie = ties(grads_three)
        *dy2, dys, u0, st, tot12 = run(
            k_back_second,
            (u1, y2, ys, got, norm_params, keep0, keep12, w_one, y1, count),
            [HBM, HBM, HBM, VMEM, VMEM, VMEM, VMEM, HBM, HBM, SMEM],
            [*narrow, wide_b, wide_f, send8, packed16],
            [HBM] * 6 + [VMEM, VMEM],
            [wf, wf, wf, wf, wb16, wb16, weight, wf, sems(38)],
            conv_flops,
            18_000_000,
            name="second_back",
            share=1,
            after=tie,
        )
        got = exchange(st)
        tie = ()
        if fast:
            second_two = merge(grid, (first_three, first_four), (u0,))
            tie = ties(second_two)
            second_two = scatter_second(grid, second_two)
        dy2_got = siblings(dy2)
        dy1, tot0 = run(
            k_back_first,
            (u0, y1, got, norm_params, keep0, count),
            [HBM, HBM, VMEM, VMEM, VMEM, SMEM],
            [wide_b, packed8],
            [HBM, VMEM],
            [wf, wf, wb16, sems(21)],
            0,
            5_000_000,
            name="first_back",
            after=(*tie, *dy2_got),
        )
        dy1_got = sibling(dy1)
        late_rows = rows_one // 4 - 9 * CIN // 2 if fast else half_rows + CIN // 2
        half_short = (CIN // 2, COUT)
        outs, out_specs = [shape((late_rows, COUT), bf16), shape(half_short, bf16)], [HBM] * 2
        late_buf = pltpu.VMEM((late_rows, COUT), bf16)
        if fast:
            quarter = [shape((2, 2, part_one, COUT // 2), bf16)] * 4
            outs, out_specs = [*outs, *quarter], [HBM] * 6
            late_buf = pltpu.VMEM((16, part_one, COUT), bf16)
        grads_late, short, *grads_last = run(
            make_pair_second(),
            (a1_mine, a1_got, *dy2, *dy2_got, x_mine, x_theirs, dys, place),
            [HBM] * 13 + [SMEM],
            outs,
            out_specs,
            [
                *pair_scratch,
                late_buf,
                pltpu.VMEM((2 * CIN, CAP), bf16),
                pltpu.VMEM((2 * CIN, CAP), bf16),
                wb16,
                pltpu.VMEM(half_short, bf16),
                sems(48),
            ],
            conv_flops,
            9_000_000,
            name="second_weights",
            after=(dy1_got,),
        )
        tie = (grads_late,)
        if fast:
            first_last = scatter_first(grid, grads_last)
            third_two = line(grid, second_two, (grads_late,))
            tie = ties(third_two)
        short_got = sibling(short)
        half_features = pltpu.VMEM((8 * CIN, CAP), bf16)
        if fast:
            outs, out_specs = quarter, [HBM] * 4
        else:
            outs, out_specs = shape((rows_one // 2, COUT), bf16), HBM
        blocks = (8, part_one, COUT) if fast else (1, rows_one // 2, COUT)
        grads_one = run(
            k_pair_first,
            (x_mine, x_got, dy1, dy1_got, grads_late, short_got, place),
            [HBM] * 6 + [SMEM],
            outs,
            out_specs,
            [
                half_features,
                half_features,
                wb16,
                wb16,
                pltpu.VMEM(blocks, bf16),
                pltpu.VMEM(half_short, bf16),
                sems(48),
            ],
            first_flops,
            8_000_000,
            name="first_weights",
            after=tie,
        )
        def back_to_features():
            dx = run(
                k_input_grad,
                (dy1, dys, w_one),
                [HBM] * 3,
                shape((CAP, 16 * CIN), f32),
                HBM,
                [
                    wb16,
                    wb16,
                    pltpu.VMEM((10 * CIN, COUT), bf16),
                    pltpu.VMEM((CAP, 16 * CIN), f32),
                    sems(28),
                ],
                first_flops,
                9_000_000,
                name="input_grad",
            )
            return dx, dx.reshape(CAP, 4, 4, CIN)

        states_one = (block_one_master, block_one_momentum, block_one_average)
        states_two = (block_two_master, block_two_momentum, block_two_average)
        rate = rate_conv * math.sqrt(images_all)
        if fast:
            first_one = scatter_first(grid, grads_one)
            dx, input_grad = back_to_features()
            second_one = scatter_second(grid, merge(grid, (first_one, first_last), (dx,)))
            fourth_two = sides(grid, third_two, second_one[:1])
            third_one = line(grid, second_one, (fourth_two[0],))
            two_m, two_w, two_a, two_c = update(grid, fourth_two, states_two, rate)
            fourth_one = sides(grid, third_one, (two_m, input_grad))
            one_m, one_w, one_a, one_c = update(grid, fourth_one, states_one, rate)
        else:
            two_sum = reduce_halves(
                devices, side[0, 0], jnp.concatenate([grads_three, grads_four], axis=0)
            )
            one_sum = reduce_halves(devices, side[0, 0], grads_one)
            one_m, one_w, one_a = nesterov(one_sum, *states_one, rate)
            two_m, two_w, two_a = nesterov(two_sum, *states_two, rate)
            one_c, two_c = one_w.astype(bf16), two_w.astype(bf16)
            _, input_grad = back_to_features()
        def unpacked(packed):
            return packed.reshape(-1, COUT)

        t0, t3, t4, t12 = unpacked(tot0), unpacked(tot3), unpacked(tot4), unpacked(tot12)
        norm_grad = jnp.stack(
            [
                jnp.stack([t0[0], t12[0], t12[1], t3[0], t4[0]]),
                jnp.stack([t0[1], t12[2], t12[2], t3[1], t4[1]]),
            ]
        )
        total = keep0[2, 0] * 0.25
        head_sum = head_sum.reshape(-1, LANES)[: 5 * TASKS].reshape(5, TASKS, LANES)
        task_losses = head_sum[4, :, 1] / total
        head_grad = jnp.concatenate(
            [head_sum[:4].transpose(0, 2, 1).reshape(COUT, TASKS), head_sum[4, :, 0][None]], axis=0
        ) / total
        scale_rate = math.sqrt(images_all)
        norm_m, norm_w, norm_a = nesterov(
            norm_grad, norm_params, norm_momentum, norm_average, rate_norm * scale_rate
        )
        head_m, head_w, head_a = nesterov(
            head_grad, head_params, head_momentum, head_average, rate_head * scale_rate
        )
        return (
            pooled,
            input_grad,
            task_losses,
            weights[0, :TASKS],
            one_m,
            one_w,
            one_a,
            one_c,
            two_m,
            two_w,
            two_a,
            two_c,
            norm_m,
            norm_w,
            norm_a,
            head_m,
            head_w,
            head_a,
        )

    return shards


def solution(mesh):
    devices = mesh.shape["batch"] * mesh.shape["pass"]
    fast = mesh.shape["batch"] == 8 and mesh.shape["pass"] == 4
    rows = P(AXES, None)
    in_specs = (
        P(AXES, None, None, None),
        rows,
        P("batch", "pass"),
        rows,
        rows,
        rows,
        rows,
        rows,
        rows,
        P(),
        P(),
        P(),
        P(),
        P(),
        P(),
    )
    out_specs = (
        rows,
        P(AXES, None, None, None),
        P(),
        P(),
        rows,
        rows,
        rows,
        rows,
        rows,
        rows,
        rows,
        rows,
        P(),
        P(),
        P(),
        P(),
        P(),
        P(),
    )
    return jax.shard_map(
        make_shards(devices, fast), mesh=mesh, in_specs=in_specs, out_specs=out_specs, check_vma=False
    )
```
